32 devices in a mesh: dp: 8 (over y, x, core), mem: 4 (over z).
Axes of the slice: x: 2, y: 2, z: 4, core: 2. Of those that a mesh axis runs over, the one named last changes fastest.
Arguments:
- inputs: bfloat16 [32, 1024, 512], P(('dp', 'mem')), may hold values from -6 to 6
- memory: bfloat16 [32, 1024, 512], P('dp', 'mem'), may hold values from -6 to 6
- cotangent: bfloat16 [32, 1024, 512], P(('dp', 'mem')), may hold values from -6 to 6
- tgt_len: int32 [32, 16], P(('dp', 'mem')), may hold values from 0 to 1024, as said below
- src_len: int32 [32, 16], P('dp'), may hold values from 0 to 1024, as said below
- self_qkv: bfloat16 [512, 1536], replicated, may hold values from -0.25 to 0.25
- self_out: bfloat16 [512, 512], replicated, may hold values from -2 to 2
- cross_query: bfloat16 [512, 512], replicated, may hold values from -0.25 to 0.25
- cross_kv: bfloat16 [512, 1024], replicated, may hold values from -0.25 to 0.25
- cross_out: bfloat16 [512, 512], replicated, may hold values from -2 to 2
- ffn_in: bfloat16 [512, 2048], replicated, may hold values from -0.25 to 0.25
- ffn_out: bfloat16 [2048, 512], replicated, may hold values from -0.125 to 0.125
- ln_gain: float32 [3, 512], replicated, may hold values from 0.25 to 1.75
- ln_bias: float32 [3, 512], replicated, may hold values from -0.5 to 0.5
- omega_scale: float32 [3, 512], replicated, may hold values from 1 to 2.5
Outputs:
- output: bfloat16 [32, 1024, 512], P(('dp', 'mem'))
- input_grad: float32 [32, 1024, 512], P(('dp', 'mem'))
- memory_grad: float32 [32, 1024, 512], P('dp', 'mem')
- self_qkv_grad: float32 [512, 1536], replicated
- self_out_grad: float32 [512, 512], replicated
- cross_query_grad: float32 [512, 512], replicated
- cross_kv_grad: float32 [512, 1024], replicated
- cross_out_grad: float32 [512, 512], replicated
- ffn_in_grad: float32 [512, 2048], replicated
- ffn_out_grad: float32 [2048, 512], replicated
- ln_gain_grad: float32 [3, 512], replicated
- ln_bias_grad: float32 [3, 512], replicated
- omega_grad: float32 [3, 512], replicated
The draws below stay inside these ranges and needn't reach their ends.
Inputs may be any that keep to these rules, and one draw needn't show every extreme that they name: A document row has its target length, at least 512, in column 0 and zeros elsewhere. A sentence row has 16 sentences of target length 1 to 64. Among the 4 rows of each dp index, one drawn from the seed is a document of target length 1024. The next row (cyclically) is a sentence row whose first sentence has target length 64. A row is of the same kind in tgt_len and src_len. `src_len`: A document row has its source length, at least 512, in column 0 and zeros elsewhere. A sentence row has 16 sources of length 1 to 64. The full-length document of each dp index has source length 1024. The sentence row after it has a first source of length 64.
All inputs are finite; a program needn't handle non-finite values.
Results may differ from the reference program's by a relative error of at most 0.02.
Values may be sent and summed in bfloat16 or wider, within the bound.
A program may use at most 192 MiB of HBM per device.

```python
import math
from functools import partial
import jax
import jax.numpy as jnp
from jax import lax

D = 512
FF = 2048
HEADS = 8
HEAD_DIM = 64
TGT_LEN = 1024
SRC_LEN = 1024
SENT = 64
PACK = 16
SRC_SENT = 64
GROUP_SEQS = 4
NSEQ = 32


def sequence_kinds(key):
    kinds_key, chosen_key = jax.random.split(jax.random.fold_in(key, 17))
    documents = jax.random.randint(kinds_key, (NSEQ,), 0, 2)
    chosen = jax.random.randint(chosen_key, (NSEQ // GROUP_SEQS,), 0, GROUP_SEQS)
    places = jnp.arange(NSEQ)
    within = places % GROUP_SEQS
    picked = chosen[places // GROUP_SEQS]
    longest = within == picked
    partner = within == (picked + 1) % GROUP_SEQS
    documents = jnp.where(partner, 0, documents)
    return (jnp.where(longest, 1, documents), longest, partner)


def length_rows(kinds, key, full_len, short_len):
    documents, longest, partner = kinds
    long_key, short_key = jax.random.split(key)
    doc_len = jax.random.randint(long_key, (NSEQ,), full_len // 2, full_len + 1)
    doc_len = jnp.where(longest, full_len, doc_len)
    sentence = jax.random.randint(short_key, (NSEQ, PACK), 1, short_len + 1)
    column = jnp.arange(PACK)[None, :]
    sentence = jnp.where((column == 0) & partner[:, None], short_len, sentence)
    doc_rows = jnp.where(column == 0, doc_len[:, None], 0)
    return jnp.where(documents[:, None] == 1, doc_rows, sentence).astype(jnp.int32)


def draw_tgt_len(key, part):
    kinds = sequence_kinds(key)
    key = jax.random.fold_in(key, 3)
    return length_rows(kinds, key, TGT_LEN, SENT)


def draw_src_len(key, part):
    kinds = sequence_kinds(key)
    key = jax.random.fold_in(key, 5)
    return length_rows(kinds, key, SRC_LEN, SRC_SENT)


def shard_levels(key, extent, cuts, least, high):
    level = 1.0
    for axis_at, parts in cuts:
        draws = jax.random.uniform(jax.random.fold_in(jax.random.fold_in(key, 6), axis_at), (parts,), jnp.float32, least / len(cuts), high / len(cuts))
        level = level * jnp.repeat(jnp.exp(draws), extent[axis_at] // parts).reshape((-1,) + (1,) * (len(extent) - 1 - axis_at))
    return level


def noise(own_key, dims, scale, limit, cuts=(), kind=jnp.bfloat16):
    values = scale * jax.random.normal(own_key, dims, jnp.float32)
    if cuts:
        values = values * shard_levels(own_key, dims, cuts, -0.22, 0.18)
    return jnp.clip(values, -limit, limit).astype(kind)


def setup_inputs(seed: int = 0) -> dict:
    splits = jax.random.split(jax.random.key(seed), 16)
    inputs = noise(splits[0], (NSEQ, TGT_LEN, D), 1.0, 6.0, ((0, 32),))
    memory = noise(splits[1], (NSEQ, SRC_LEN, D), 1.0, 6.0, ((0, 8), (1, 4)))
    cotangent = noise(splits[2], (NSEQ, TGT_LEN, D), 1.0, 6.0, ((0, 32),))
    tgt_len = draw_tgt_len(jax.random.fold_in(splits[15], 71), 0)
    src_len = draw_src_len(jax.random.fold_in(splits[15], 71), 0)
    self_qkv = noise(splits[5], (D, 3 * D), D ** -0.5, 0.25)
    self_out = noise(splits[6], (D, D), (D // 64) ** -0.5, 2.0)
    cross_query = noise(splits[7], (D, D), D ** -0.5, 0.25)
    cross_kv = noise(splits[8], (D, 2 * D), D ** -0.5, 0.25)
    cross_out = noise(splits[9], (D, D), (D // 64) ** -0.5, 2.0)
    ffn_in = noise(splits[10], (D, FF), D ** -0.5, 0.25)
    ffn_out = noise(splits[11], (FF, D), FF ** -0.5, 0.125)
    ln_gain = jnp.clip(1.0 + 0.15 * jax.random.normal(splits[12], (3, D), jnp.float32), 0.25, 1.75)
    ln_bias = jnp.clip(jax.random.uniform(splits[13], (3, D), jnp.float32, -0.5, 0.5), -0.5, 0.5)
    omega_scale = jnp.clip(jnp.exp(jax.random.uniform(splits[14], (3, D), jnp.float32, math.log(1.0), math.log(2.5))), 1.0, 2.5)
    return {"inputs": inputs, "memory": memory, "cotangent": cotangent, "tgt_len": tgt_len, "src_len": src_len, "self_qkv": self_qkv, "self_out": self_out, "cross_query": cross_query, "cross_kv": cross_kv, "cross_out": cross_out, "ffn_in": ffn_in, "ffn_out": ffn_out, "ln_gain": ln_gain, "ln_bias": ln_bias, "omega_scale": omega_scale}


@jax.custom_vjp
def low(v):
    return lax.optimization_barrier(v.astype(jnp.bfloat16)).astype(jnp.float32)

@jax.custom_vjp
def low_back(v):
    return v

def low_keep(v):
    return (low(v), None)

def low_pass(kept, grad):
    return (grad,)

def back_keep(v):
    return (v, None)

def back_low(kept, grad):
    return (low(grad),)
low.defvjp(low_keep, low_pass)
low_back.defvjp(back_keep, back_low)
norm_eps = 1e-05
masked_fill = -1e+30

def highest(left_side, right_side):
    return jnp.dot(left_side, right_side, precision=lax.Precision.HIGHEST)

def layer_norm(values, gain_row, shift_row):
    centred = values - lax.optimization_barrier(jnp.mean(values, axis=-1, keepdims=True))
    variance = lax.optimization_barrier(jnp.mean(centred * centred, axis=-1, keepdims=True))
    return centred * lax.rsqrt(variance + norm_eps) * gain_row + shift_row

def layout(positions, is_document, full_width, short_width, lengths):
    width = jnp.where(is_document, full_width, short_width).astype(jnp.int32)
    segment = (positions // width).astype(jnp.int32)
    offset = positions - segment * width
    slots = jnp.arange(lengths.shape[0], dtype=jnp.int32)
    bound = lax.optimization_barrier(jnp.sum(jnp.where(segment[:, None] == slots[None, :], lengths[None, :], 0), axis=1))
    return (segment, offset < bound)

def attention(queries, key_rows, value_rows, allowed):
    q_heads = queries.reshape(queries.shape[0], HEADS, HEAD_DIM)
    k_heads = key_rows.reshape(key_rows.shape[0], HEADS, HEAD_DIM)
    v_heads = value_rows.reshape(value_rows.shape[0], HEADS, HEAD_DIM)
    scores = jnp.einsum('qhd,khd->hqk', q_heads, k_heads, precision=lax.Precision.HIGHEST)
    scores = low_back(scores * HEAD_DIM ** (-0.5))
    masked = jnp.where(allowed[None], scores, masked_fill)
    largest = lax.optimization_barrier(jnp.max(masked, axis=-1, keepdims=True))
    exponent = jnp.exp(masked - largest)
    weights = low(exponent / lax.optimization_barrier(jnp.sum(exponent, axis=-1, keepdims=True)))
    mixed_rows = jnp.einsum('hqk,khd->qhd', weights, v_heads, precision=lax.Precision.HIGHEST)
    return low(low_back(mixed_rows.reshape(queries.shape[0], HEADS * HEAD_DIM)))

def one_sequence(weights, pieces):
    w_qkv, w_self_out, w_query, w_memory, w_cross_out, w_in, w_out, gain_rows, shifts, scales = weights
    source, encoded, target_len, source_len = pieces
    places = jnp.arange(TGT_LEN, dtype=jnp.int32)
    src_pos = jnp.arange(SRC_LEN, dtype=jnp.int32)
    is_document = source_len[0] > SRC_SENT
    t_seg, t_valid = layout(places, is_document, TGT_LEN, SENT, target_len)
    s_seg, s_valid = layout(src_pos, is_document, SRC_LEN, SRC_SENT, source_len)
    causal = (places[None, :] <= places[:, None]) & (t_seg[None, :] == t_seg[:, None]) & t_valid[None, :]
    reach_mask = (s_seg[None, :] == t_seg[:, None]) & s_valid[None, :]
    packed = low(low_back(highest(low(source), w_qkv)))
    head_out = attention(packed[:, :D], packed[:, D:2 * D], packed[:, 2 * D:], causal)
    branch = low_back(highest(head_out, w_self_out))
    first_out = layer_norm(scales[0] * source + branch, gain_rows[0], shifts[0])
    queries = low(low_back(highest(low(first_out), w_query)))
    memory_kv = low(low_back(highest(low(encoded), w_memory)))
    head_out = attention(queries, memory_kv[:, :D], memory_kv[:, D:], reach_mask)
    branch = low_back(highest(head_out, w_cross_out))
    second = layer_norm(scales[1] * first_out + branch, gain_rows[1], shifts[1])
    hidden = low_back(highest(low(second), w_in))
    branch = low_back(highest(low(jax.nn.gelu(hidden)), w_out))
    third_out = layer_norm(scales[2] * second + branch, gain_rows[2], shifts[2])
    return jnp.where(t_valid[:, None], third_out, 0.0)

def reference(inputs, memory, cotangent, tgt_len, src_len, self_qkv, self_out, cross_query, cross_kv, cross_out, ffn_in, ffn_out, ln_gain, ln_bias, omega_scale):
    weights = tuple((matrix.astype(jnp.float32) for matrix in (self_qkv, self_out, cross_query, cross_kv, cross_out, ffn_in, ffn_out, ln_gain, ln_bias, omega_scale)))

    def forward(weight_set, sources, encoded):
        step_fn = jax.checkpoint(partial(one_sequence, weight_set))
        return lax.map(step_fn, (sources, encoded, tgt_len, src_len))
    outputs, pullback = jax.vjp(forward, weights, inputs.astype(jnp.float32), memory.astype(jnp.float32))
    weight_grads, input_grad, memory_grad = pullback(cotangent.astype(jnp.float32))
    return (outputs.astype(jnp.bfloat16), input_grad, memory_grad, weight_grads[0], weight_grads[1], weight_grads[2], weight_grads[3], weight_grads[4], weight_grads[5], weight_grads[6], weight_grads[7], weight_grads[8], weight_grads[9])
```

```python
import functools

import jax
import jax.numpy as jnp
from jax import lax
from jax.experimental import pallas as pl
from jax.experimental.pallas import tpu as pltpu
from jax.sharding import PartitionSpec as P

f32 = jnp.float32
bf = jnp.bfloat16
MESH = pl.DeviceIdType.MESH
NN = (((1,), (0,)), ((), ()))
NT = (((1,), (1,)), ((), ()))
TN = (((0,), (0,)), ((), ()))

L = 1024
D = 512
FF = 2048
HEADS = 8
PAIRS = HEADS // 2
SHORT = 64
SCALE = 0.125
NEG = -1e30
EPS = 1e-05
GELU_C = 0.7978845608028654
GELU_A = 0.044715


def dot(a, b, dims=NN):
    return lax.dot_general(a, b, dims, preferred_element_type=f32)


def span(i, n):
    return pl.ds(pl.multiple_of(i * n, n), n)


def loop(n, body):
    def step(i, carry):
        body(i)
        return carry

    lax.fori_loop(0, n, step, 0)


def half_lanes():
    return lax.broadcasted_iota(jnp.int32, (1, 128), 1) < 64


def norm(values):
    centred = values - jnp.mean(values, axis=-1, keepdims=True)
    scaler = lax.rsqrt(jnp.mean(centred * centred, axis=-1, keepdims=True) + EPS)
    return centred * scaler, scaler


def norm_back(upstream, normed, scaler, gain_row):
    scaled = upstream * gain_row
    centred = scaled - jnp.mean(scaled, axis=-1, keepdims=True)
    centred = centred - normed * jnp.mean(scaled * normed, axis=-1, keepdims=True)
    return centred * scaler


def total(values):
    return jnp.sum(values, axis=0, keepdims=True)


def three_parts(values, base):
    lane = lax.broadcasted_iota(jnp.int32, (1, 128), 1)
    high = values.astype(bf).astype(f32)
    rest = values - high
    middle = rest.astype(bf).astype(f32)
    low = rest - middle
    picked = jnp.where(lane == 16, high, jnp.where(lane == 17, middle, jnp.where(lane == 18, low, base)))
    return picked.astype(bf)


def key_features(lengths, is_doc, rows, first):
    pos = first + lax.broadcasted_iota(jnp.int32, (rows, 128), 0)
    lane = lax.broadcasted_iota(jnp.int32, (rows, 128), 1)
    seg = (pos >> 6) * (1 - is_doc)
    inside = (seg == lane) & (pos - seg * SHORT < lengths)
    feats = jnp.where(lane < 16, jnp.where(inside, 0.0, NEG), jnp.where(lane < 19, 1.0, 0.0))
    hot = jnp.where(seg == lane, 1.0, 0.0)
    return feats.astype(bf), hot.astype(bf), jnp.where(inside, 1.0, 0.0)


def softmax_pair(qp, sections, heads, lse_out, base):
    half = half_lanes()
    mixed = []
    for e in range(2):
        sel = half if e == 0 else jnp.logical_not(half)
        qa = jnp.concatenate([jnp.where(sel, qp, jnp.zeros_like(qp)), base], axis=1)
        scores = []
        largest = None
        for keys, _, mask in sections:
            s = dot(qa, keys, NT)
            if mask is not None:
                s = jnp.where(mask, s, NEG)
            scores.append(s)
            m = jnp.max(s, axis=1, keepdims=True)
            largest = m if largest is None else jnp.maximum(largest, m)
        acc = None
        for s, (_, values, _) in zip(scores, sections):
            o = dot(jnp.exp(s - largest).astype(bf), values)
            acc = o if acc is None else acc + o
        summed = acc[:, 128:]
        lse_out(e, three_parts(-(largest + jnp.log(summed)), base.astype(f32)))
        mixed.append(acc[:, :128] / summed)
    heads(jnp.where(half, mixed[0], mixed[1]).astype(bf))


def back_tile(ka, va, k_rows, qp, qfeat, gp, gfeat, mask):
    half = half_lanes()
    dk, dv, dq = [], [], []
    for e in range(2):
        sel = half if e == 0 else jnp.logical_not(half)
        qa = jnp.concatenate([jnp.where(sel, qp, jnp.zeros_like(qp)), qfeat[e]], axis=1)
        ga = jnp.concatenate([jnp.where(sel, gp, jnp.zeros_like(gp)), gfeat[e]], axis=1)
        probs = jnp.exp(dot(ka, qa, NT))
        if mask is not None:
            width = mask.shape[1]
            first = jnp.where(mask, probs[:, :width], 0.0)
            probs = first if probs.shape[1] == width else jnp.concatenate([first, probs[:, width:]], axis=1)
        ds = (probs * dot(va, ga, NT)).astype(bf)
        dv.append(dot(probs.astype(bf), gp))
        dk.append(dot(ds, qp))
        dq.append(dot(ds, k_rows, TN))
    return (
        jnp.where(half, dk[0], dk[1]),
        jnp.where(half, dv[0], dv[1]),
        jnp.where(half, dq[0], dq[1]),
    )


def delta_features(product, store):
    half = half_lanes()
    for j in range(PAIRS):
        part = product[:, 128 * j : 128 * (j + 1)]
        for e in range(2):
            sel = half if e == 0 else jnp.logical_not(half)
            delta = jnp.sum(jnp.where(sel, part, 0.0), axis=1, keepdims=True)
            store(2 * j + e, three_parts(jnp.broadcast_to(-delta, part.shape), jnp.zeros_like(part)))


SELF_BQ = 256
SELF_BK = 256
CROSS_BQ = 512
CROSS_BK = 256
TB = 256


def forward_kernel(
    x, meml, cot, meta, wqkv, wso, wcq, wckv, wco, win, wout, gain, bias, omega,
    out, packed, sh, qfs, kfs, n1, r1, q8, mem, kv, qfc, kfc, dfc, pre2, do, gffn, vecs,
    hot, keep, ch, act, hg, br3, slow, br2, dg, send_sem, recv_sem, own_sem,
):
    me = lax.axis_index("mem")
    dp = lax.axis_index("dp")
    n = 4
    piece = L // n
    barrier = pltpu.get_barrier_semaphore()
    for t in range(1, n):
        pl.semaphore_signal(barrier, inc=1, device_id=(dp, lax.rem(me + t, n)), device_id_type=MESH)
    pl.semaphore_wait(barrier, n - 1)

    def exchange(t):
        peer = lax.rem(me + t, n)
        return pltpu.make_async_remote_copy(
            src_ref=meml.at[peer],
            dst_ref=mem.at[span(me, piece), :],
            send_sem=send_sem.at[t],
            recv_sem=recv_sem.at[t],
            device_id=(dp, peer),
            device_id_type=MESH,
        )

    own = pltpu.make_async_copy(meml.at[me], mem.at[span(me, piece), :], own_sem)
    for t in range(1, n):
        exchange(t).start()
    own.start()

    is_doc = (meta[1:2, 0:1] > SHORT).astype(jnp.int32)

    def features(i):
        rows = span(i, TB)
        feats, one_hot, inside = key_features(meta[0:1, :], is_doc, TB, i * TB)
        kfs[rows, :] = feats
        hot[rows, :] = one_hot
        keep[rows, :] = jnp.sum(inside, axis=1, keepdims=True)
        feats, _, _ = key_features(meta[1:2, :], is_doc, TB, i * TB)
        kfc[rows, :] = feats

    loop(L // TB, features)

    def project(i):
        rows = span(i, TB)
        packed[rows, :D] = dot(x[rows, :], wqkv[:, :D]).astype(bf) * bf(SCALE)
        packed[rows, D:] = dot(x[rows, :], wqkv[:, D:]).astype(bf)

    loop(L // TB, project)

    ones = jnp.ones((SELF_BQ, 128), bf)
    causal = lax.broadcasted_iota(jnp.int32, (SELF_BQ, SELF_BQ), 0) >= lax.broadcasted_iota(
        jnp.int32, (SELF_BQ, SELF_BQ), 1
    )
    for b in range(L // SELF_BQ):
        low, high = b * SELF_BQ, (b + 1) * SELF_BQ

        def self_pair(j, low=low, high=high):
            def section(first, last, mask):
                return (
                    jnp.concatenate([packed[first:last, pl.ds(pl.multiple_of(D + j * 128, 128), 128)], kfs[first:last, :]], axis=1),
                    jnp.concatenate([packed[first:last, pl.ds(pl.multiple_of(2 * D + j * 128, 128), 128)], jnp.ones((last - first, 128), bf)], axis=1),
                    mask,
                )

            sections = [section(low, high, causal)]
            if low:
                sections.append(section(0, low, None))

            def heads(value):
                sh[low:high, span(j, 128)] = value

            def lse_out(e, value):
                qfs[2 * j + e, low:high, :] = value

            softmax_pair(packed[low:high, span(j, 128)], sections, heads, lse_out, hot[low:high, :])

        loop(PAIRS, self_pair)

    def first_norm(i):
        rows = span(i, TB)
        normed, scaler = norm(omega[0:1, :] * x[rows, :].astype(f32) + dot(sh[rows, :], wso[...]))
        n1[rows, :] = normed
        r1[rows, :] = scaler
        first = (normed * gain[0:1, :] + bias[0:1, :]).astype(bf)
        q8[rows, :] = dot(first, wcq[...]).astype(bf) * bf(SCALE)

    loop(L // TB, first_norm)

    own.wait()
    for t in range(1, n):
        exchange(t).wait()

    def memory_project(i):
        rows = span(i, TB)
        kv[rows, :] = dot(mem[rows, :], wckv[...]).astype(bf)

    loop(L // TB, memory_project)

    def cross_pair(i):
        j = i // (L // CROSS_BQ)
        rows = span(lax.rem(i, L // CROSS_BQ), CROSS_BQ)
        keys = jnp.concatenate([kv[:, span(j, 128)], kfc[...]], axis=1)
        values = jnp.concatenate(
            [kv[:, pl.ds(pl.multiple_of(D + j * 128, 128), 128)], jnp.ones((L, 128), bf)], axis=1
        )

        def heads(value):
            ch[rows, span(j, 128)] = value

        def lse_out(e, value):
            qfc[2 * j + e, rows, :] = value

        softmax_pair(q8[rows, span(j, 128)], [(keys, values, None)], heads, lse_out, hot[rows, :])

    loop(PAIRS * (L // CROSS_BQ), cross_pair)

    vecs[...] = jnp.zeros_like(vecs)
    wide = 512

    def tokens(i):
        rows = span(i, TB)
        first = n1[rows, :] * gain[0:1, :] + bias[0:1, :]
        n2, r2 = norm(omega[1:2, :] * first + dot(ch[rows, :], wco[...]))
        second = n2 * gain[1:2, :] + bias[1:2, :]
        second_low = second.astype(bf)
        slow[rows, :] = second_low
        branch = jnp.zeros((TB, D), f32)
        for c in range(FF // wide):
            cols = slice(c * wide, (c + 1) * wide)
            h = dot(second_low, win[:, cols])
            square = h * h
            th = jnp.tanh(GELU_C * (h + GELU_A * (h * square)))
            cdf = 0.5 * (1.0 + th)
            low = (h * cdf).astype(bf)
            act[rows, cols] = low
            dg[:, cols] = cdf + 0.5 * h * (1.0 - th * th) * (GELU_C * (1.0 + 3.0 * GELU_A * square))
            branch = branch + dot(low, wout[cols, :])
        n3, r3 = norm(omega[2:3, :] * second + branch)
        third = n3 * gain[2:3, :] + bias[2:3, :]
        kept = keep[rows, :]
        out[rows, :] = (third * kept).astype(bf)
        up = cot[rows, :].astype(f32) * kept
        pre3 = norm_back(up, n3, r3, gain[2:3, :])
        vecs[2:3, :] += total(up * n3)
        vecs[5:6, :] += total(up)
        vecs[8:9, :] += total(pre3 * second)
        low3 = pre3.astype(bf)
        br3[rows, :] = low3
        grad = omega[2:3, :] * pre3
        for c in range(FF // wide):
            cols = slice(c * wide, (c + 1) * wide)
            hl = (dot(low3, wout[cols, :], NT) * dg[:, cols]).astype(bf)
            hg[rows, cols] = hl
            grad = grad + dot(hl, win[:, cols], NT)
        back2 = norm_back(grad, n2, r2, gain[1:2, :])
        vecs[1:2, :] += total(grad * n2)
        vecs[4:5, :] += total(grad)
        vecs[7:8, :] += total(back2 * first)
        pre2[rows, :] = back2
        low2 = back2.astype(bf)
        br2[rows, :] = low2
        dlow = dot(low2, wco[...], NT).astype(bf)
        do[rows, :] = dlow

        def store(h, value):
            dfc[h, rows, :] = value

        delta_features(dlow.astype(f32) * ch[rows, :].astype(f32), store)

    loop(L // TB, tokens)

    def out_weight(i):
        gffn[span(i, 256), :] = dot(act[:, span(i, 256)], br3[...], TN).astype(bf)

    loop(FF // 256, out_weight)
    for c in range(FF // wide):

        def in_weight(i, c=c):
            gffn[pl.ds(pl.multiple_of(FF + c * 512 + i * 256, 256), 256), :] = dot(
                slow[:, span(i, 256)], hg[:, c * wide : (c + 1) * wide], TN
            ).astype(bf)

        loop(2, in_weight)

    def cross_out_weight(i):
        gffn[pl.ds(pl.multiple_of(2 * FF + i * 256, 256), 256), :] = dot(
            ch[:, span(i, 256)], br2[...], TN
        ).astype(bf)

    loop(2, cross_out_weight)


class Segment:
    def __init__(self, index, source, base, n, parts, acc, bufs, fin, final, final_base, sems, place):
        self.index, self.source, self.base, self.n, self.parts = index, source, base, n, parts
        self.acc, (self.r0, self.r1, self.r2, self.r3), self.fin = acc, bufs, fin
        self.final, self.final_base = final, final_base
        self.send, self.recv, self.local = sems
        self.place = place

    def rows(self, first, count):
        return pl.ds(pl.multiple_of(first, 16), count)

    def remote(self, src, dst, k, device):
        return pltpu.make_async_remote_copy(
            src_ref=src,
            dst_ref=dst,
            send_sem=self.send.at[self.index, k],
            recv_sem=self.recv.at[self.index, k],
            device_id=device,
            device_id_type=MESH,
        )

    def core_copy(self):
        n, (dp, me, bits) = self.n, self.place
        other = 1 - bits[0]
        return self.remote(
            self.source.at[self.rows(self.base + other * (n // 2), n // 2), :],
            self.r0,
            0,
            (dp + 1 - 2 * bits[0], me),
        )

    def own_copy(self):
        n, (_, _, bits) = self.n, self.place
        return pltpu.make_async_copy(
            self.source.at[self.rows(self.base + bits[0] * (n // 2), n // 2), :],
            self.acc,
            self.local.at[self.index],
        )

    def partner(self, axis):
        dp, me, bits = self.place
        return (dp + 2 * axis * (1 - 2 * bits[axis]), me)

    def axes(self, p):
        return (1, 2) if self.parts[p][2] == 0 else (2, 1)

    def lanes(self, p):
        return slice(self.parts[p][0], self.parts[p][1])

    def offset(self, p, depth):
        if depth == 0:
            return 0
        n, (_, me, bits) = self.n, self.place
        one, two = self.axes(p)
        result = bits[one] * (n // 4)
        if depth > 1:
            result = result + bits[two] * (n // 8)
        if depth > 2:
            result = result + me * (n // 32)
        return result

    def halving(self, p, depth):
        n, (_, _, bits) = self.n, self.place
        axis = self.axes(p)[depth - 1]
        size = n // (4 if depth == 1 else 8)
        other = self.offset(p, depth - 1) + (1 - bits[axis]) * size
        buf = self.r1 if depth == 1 else self.r2
        return self.remote(
            self.acc.at[self.rows(other, size), self.lanes(p)],
            buf.at[:, self.lanes(p)],
            2 * depth - 1 + p,
            self.partner(axis),
        )

    def quarter(self, p, t):
        n, (dp, me, _) = self.n, self.place
        peer = lax.rem(me + t, 4)
        return self.remote(
            self.acc.at[self.rows(self.offset(p, 2) + peer * (n // 32), n // 32), self.lanes(p)],
            self.r3.at[t - 1, :, self.lanes(p)],
            5 + 3 * p + t - 1,
            (dp, peer),
        )

    def final_rows(self, p, depth):
        n, (_, _, bits) = self.n, self.place
        size = n // (2, 4, 8, 32)[depth]
        return self.final.at[
            self.rows(self.final_base + bits[0] * (n // 2) + self.offset(p, depth), size),
            slice(None) if p is None else self.lanes(p),
        ]

    def keep_copy(self, p):
        return pltpu.make_async_copy(
            self.fin.at[:, self.lanes(p)], self.final_rows(p, 3), self.local.at[self.index + 16 * (p + 1)]
        )

    def spread(self, p, t):
        dp, me, _ = self.place
        return self.remote(
            self.fin.at[:, self.lanes(p)],
            self.final_rows(p, 3),
            11 + 3 * p + t - 1,
            (dp, lax.rem(me + t, 4)),
        )

    def doubling(self, p, depth):
        ref = self.final_rows(p, depth)
        return self.remote(ref, ref, 15 + 2 * (3 - depth) + p, self.partner(self.axes(p)[depth - 1]))

    def core_back(self):
        dp, me, bits = self.place
        ref = self.final_rows(None, 0)
        return self.remote(ref, ref, 21, (dp + 1 - 2 * bits[0], me))

    def add(self, first, buf, count, lanes):
        step = 128 if count % 128 == 0 else count

        def body(i):
            rows = self.rows(first + i * step, step)
            self.acc[rows, lanes] = self.acc[rows, lanes] + buf[pl.ds(pl.multiple_of(i * step, 16), step), lanes]

        loop(count // step, body)

    def stages(self):
        n = self.n
        both = range(len(self.parts))

        def s0():
            self.core_copy().start()
            self.own_copy().start()

        def s1():
            self.own_copy().wait()
            self.core_copy().wait()
            self.add(0, self.r0, n // 2, slice(None))
            for p in both:
                self.halving(p, 1).start()

        def s2():
            for p in both:
                self.halving(p, 1).wait()
                self.add(self.offset(p, 1), self.r1, n // 4, self.lanes(p))
                self.halving(p, 2).start()

        def s3():
            for p in both:
                self.halving(p, 2).wait()
                self.add(self.offset(p, 2), self.r2, n // 8, self.lanes(p))
                for t in range(1, 4):
                    self.quarter(p, t).start()

        def s4():
            for p in both:
                for t in range(1, 4):
                    self.quarter(p, t).wait()
                lanes = self.lanes(p)
                mine = self.acc[self.rows(self.offset(p, 3), n // 32), lanes].astype(f32)
                for t in range(3):
                    mine = mine + self.r3[t, :, lanes].astype(f32)
                self.fin[:, lanes] = mine.astype(bf)
                self.keep_copy(p).start()
                for t in range(1, 4):
                    self.spread(p, t).start()

        def s5():
            for p in both:
                self.keep_copy(p).wait()
                for t in range(1, 4):
                    self.spread(p, t).wait()
                self.doubling(p, 2).start()

        def s6():
            for p in both:
                self.doubling(p, 2).wait()
                self.doubling(p, 1).start()

        def s7():
            for p in both:
                self.doubling(p, 1).wait()
            self.core_back().start()

        def s8():
            self.core_back().wait()

        return [s0, s1, s2, s3, s4, s5, s6, s7, s8]


def seg_scratch(n, w):
    return [
        pltpu.VMEM((n // 2, w), bf),
        pltpu.VMEM((n // 2, w), bf),
        pltpu.VMEM((n // 4, w), bf),
        pltpu.VMEM((n // 8, w), bf),
        pltpu.VMEM((3, n // 32, w), bf),
        pltpu.VMEM((n // 32, w), bf),
    ]


SEGMENTS = [(FF, D), (FF + D, D), (4 * D, D)] + [(D, 384)] * PAIRS


def backward_kernel(
    x, packed, sh, qfs, kfs, n1, r1, q8, mem, kv, qfc, kfc, dfc, pre2, do, gffn, vecs_in,
    wqkv, wso, wcq, wckv, gain, bias, omega,
    igrad, mgrad, f1, f2, f3, vout,
    fl, qg, kvg, mgs, pre1, br1, dos, dfs, pg, g2, g3, vec, vbuf, vz,
    *rest,
):
    seg_bufs, (send, recv, local, vsend, vrecv, msend, mrecv) = rest[:-7], rest[-7:]
    me = lax.axis_index("mem")
    dp = lax.axis_index("dp")
    bits = (lax.rem(dp, 2), lax.rem(dp // 2, 2), lax.rem(dp // 4, 2))
    place = (dp, me, bits)
    near = [(dp + (1 << a) * (1 - 2 * bits[a]), me) for a in range(3)]
    peers = near + [(dp, lax.rem(me + t, 4)) for t in range(1, 4)]
    barrier = pltpu.get_barrier_semaphore()
    for peer in peers:
        pl.semaphore_signal(barrier, inc=1, device_id=peer, device_id_type=MESH)
    pl.semaphore_wait(barrier, len(peers))

    whole_parts = ((0, 256, 0), (256, 512, 1))
    pair_parts = ((0, 128, 0), (128, 384, 1))
    sources = [(gffn, 0), (gffn, FF), (g2, 0)] + [(g3.at[j], 0) for j in range(PAIRS)]
    finals = [(f1, 0), (f1, FF), (f2, 0)] + [(f3.at[j], 0) for j in range(PAIRS)]
    segs = []
    for i, (n, w) in enumerate(SEGMENTS):
        acc, b0, b1, b2, b3, fin = seg_bufs[6 * i : 6 * i + 6]
        parts = whole_parts if w == D else pair_parts
        segs.append(
            Segment(i, *sources[i], n, parts, acc, (b0, b1, b2, b3), fin, *finals[i], (send, recv, local), place).stages()
        )

    ticks = {}

    def at(phase, step, fn):
        ticks.setdefault((phase, step), []).append(fn)

    def run(phase, i):
        for (name, step), fns in ticks.items():
            if name == phase:

                @pl.when(i == step)
                def _(fns=fns):
                    for fn in fns:
                        fn()

    for k in range(9):
        at("cross", min(15, 2 * k), segs[0][k]) if k < 8 else None
        at("cross", 2 * k + 1, segs[1][k]) if k < 8 else None

    def first_low(i):
        rows = span(i, TB)
        fl[rows, :] = (n1[rows, :] * gain[0:1, :] + bias[0:1, :]).astype(bf)

    loop(L // TB, first_low)

    blocks = L // CROSS_BK

    def cross_pair(i):
        run("cross", i)
        j = i // blocks
        b = lax.rem(i, blocks)
        rows = span(b, CROSS_BK)
        lanes = span(j, 128)
        vlanes = pl.ds(pl.multiple_of(D + j * 128, 128), 128)
        k_rows = kv[rows, lanes]
        ka = jnp.concatenate([k_rows, kfc[rows, :]], axis=1)
        va = jnp.concatenate([kv[rows, vlanes], kfc[rows, :]], axis=1)
        dk, dv, dq = back_tile(
            ka, va, k_rows, q8[:, lanes], [qfc[2 * j], qfc[2 * j + 1]], do[:, lanes], [dfc[2 * j], dfc[2 * j + 1]], None
        )
        kvg[rows, lanes] = dk.astype(bf)
        kvg[rows, vlanes] = dv.astype(bf)

        @pl.when(b == 0)
        def _():
            pre1[:, lanes] = dq

        @pl.when(b > 0)
        def _():
            pre1[:, lanes] += dq

    loop(PAIRS * blocks, cross_pair)
    segs[0][8]()
    segs[1][8]()

    def query_low(i):
        rows = span(i, TB)
        qg[rows, :] = (pre1[rows, :] * SCALE).astype(bf)
        mgs[rows, :] = dot(kvg[rows, :], wckv[...], NT).astype(bf)

    loop(L // TB, query_low)

    def memory_back(t):
        peer = lax.rem(me + t, 4)
        return pltpu.make_async_remote_copy(
            src_ref=mgs.at[span(peer, L // 4), :],
            dst_ref=mgrad.at[me],
            send_sem=msend.at[t],
            recv_sem=mrecv.at[t],
            device_id=(dp, peer),
            device_id_type=MESH,
        )

    memory_own = pltpu.make_async_copy(mgs.at[span(me, L // 4), :], mgrad.at[me], msend.at[0])
    memory_own.start()
    for t in range(1, 4):
        memory_back(t).start()

    def weights_two(i):
        cols = span(i, 256)
        g2[cols, :] = dot(fl[:, cols], qg[...], TN).astype(bf)
        g2[pl.ds(pl.multiple_of(D + i * 256, 256), 256), :] = dot(mem[:, cols], kvg[:, :D], TN).astype(bf)
        g2[pl.ds(pl.multiple_of(2 * D + i * 256, 256), 256), :] = dot(mem[:, cols], kvg[:, D:], TN).astype(bf)

    loop(2, weights_two)
    vec[...] = jnp.zeros_like(vec)
    vec[0:9, :] = vecs_in[0:9, :]

    def first_back(i):
        rows = span(i, TB)
        normed = n1[rows, :]
        grad = omega[1:2, :] * pre2[rows, :] + dot(qg[rows, :], wcq[...], NT)
        back1 = norm_back(grad, normed, r1[rows, :], gain[0:1, :])
        vec[0:1, :] += total(grad * normed)
        vec[3:4, :] += total(grad)
        vec[6:7, :] += total(back1 * x[rows, :].astype(f32))
        pre1[rows, :] = back1
        low1 = back1.astype(bf)
        br1[rows, :] = low1
        dlow = dot(low1, wso[...], NT).astype(bf)
        dos[rows, :] = dlow

        def store(h, value):
            dfs[h, rows, :] = value

        delta_features(dlow.astype(f32) * sh[rows, :].astype(f32), store)

    loop(L // TB, first_back)

    def weights_out(i):
        cols = span(i, 256)
        g2[pl.ds(pl.multiple_of(3 * D + i * 256, 256), 256), :] = dot(sh[:, cols], br1[...], TN).astype(bf)

    loop(2, weights_out)

    def vec_near(a):
        return pltpu.make_async_remote_copy(
            src_ref=vec.at[pl.ds(16 * a, 16), :],
            dst_ref=vbuf.at[a],
            send_sem=vsend.at[a],
            recv_sem=vrecv.at[a],
            device_id=near[a],
            device_id_type=MESH,
        )

    def vec_far(t):
        return pltpu.make_async_remote_copy(
            src_ref=vec.at[pl.ds(48, 16), :],
            dst_ref=vz.at[me],
            send_sem=vsend.at[2 + t],
            recv_sem=vrecv.at[2 + t],
            device_id=(dp, lax.rem(me + t, 4)),
            device_id_type=MESH,
        )

    def v_start():
        vec_near(0).start()

    def v_next(a):
        vec_near(a).wait()
        vec[16 * (a + 1) : 16 * (a + 2), :] = vec[16 * a : 16 * (a + 1), :] + vbuf[a]
        if a < 2:
            vec_near(a + 1).start()
        else:
            for t in range(1, 4):
                vec_far(t).start()

    def v_last():
        for t in range(1, 4):
            vec_far(t).wait()
        vz[me] = vec[48:64, :]
        vout[...] = (vz[0] + vz[1]) + (vz[2] + vz[3])

    v_start()
    segs[2][0]()
    at("self", 0, segs[2][1])
    at("self", 0, lambda: v_next(0))
    at("self", 1, segs[2][2])
    at("self", 1, lambda: v_next(1))
    at("self", 2, segs[2][3])
    at("self", 2, lambda: v_next(2))
    at("self", 3, segs[2][4])
    at("self", 3, v_last)
    at("self", 1, segs[3][0])
    at("self", 2, segs[3][1])
    at("self", 2, segs[4][0])
    at("self", 3, segs[3][2])
    at("self", 3, segs[4][1])
    at("self", 3, segs[5][0])

    below = lax.broadcasted_iota(jnp.int32, (SELF_BK, SELF_BK), 1) >= lax.broadcasted_iota(
        jnp.int32, (SELF_BK, SELF_BK), 0
    )

    def self_pair(j):
        run("self", j)
        qlanes = span(j, 128)
        klanes = pl.ds(pl.multiple_of(D + j * 128, 128), 128)
        vlanes = pl.ds(pl.multiple_of(2 * D + j * 128, 128), 128)
        dqs = []
        for b in range(L // SELF_BK):
            low, high = b * SELF_BK, (b + 1) * SELF_BK
            k_rows = packed[low:high, klanes]
            ka = jnp.concatenate([k_rows, kfs[low:high, :]], axis=1)
            va = jnp.concatenate([packed[low:high, vlanes], kfs[low:high, :]], axis=1)
            dk, dv, dq = back_tile(
                ka,
                va,
                k_rows,
                packed[low:, qlanes],
                [qfs[2 * j, low:, :], qfs[2 * j + 1, low:, :]],
                dos[low:, qlanes],
                [dfs[2 * j, low:, :], dfs[2 * j + 1, low:, :]],
                below,
            )
            pg[low:high, klanes] = dk.astype(bf)
            pg[low:high, vlanes] = dv.astype(bf)
            for i in range(b, L // SELF_BK):
                piece = dq[(i - b) * SELF_BK : (i - b + 1) * SELF_BK, :]
                if b == 0:
                    dqs.append(piece)
                else:
                    dqs[i] = dqs[i] + piece
        for i, piece in enumerate(dqs):
            pg[i * SELF_BK : (i + 1) * SELF_BK, qlanes] = (piece * SCALE).astype(bf)
        for c in range(3):
            lanes = pl.ds(pl.multiple_of(c * D + j * 128, 128), 128)
            g3[j, :, c * 128 : (c + 1) * 128] = dot(x[...], pg[:, lanes], TN).astype(bf)

    loop(PAIRS, self_pair)
    segs[6][0]()

    def input_back(i):
        rows = span(i, TB)
        igrad[rows, :] = omega[0:1, :] * pre1[rows, :] + dot(pg[rows, :], wqkv[...], NT)

    loop(L // TB, input_back)
    memory_own.wait()
    for t in range(1, 4):
        memory_back(t).wait()
    for k in range(1, 9):
        if k + 4 < 9:
            segs[2][k + 4]()
        if k + 2 < 9:
            segs[3][k + 2]()
        if k + 1 < 9:
            segs[4][k + 1]()
        segs[5][k]()
        segs[6][k]()


VM = pl.BlockSpec(memory_space=pltpu.VMEM)
ANY = pl.BlockSpec(memory_space=pl.ANY)


def per_device(
    inputs, memory, cotangent, tgt_len, src_len,
    self_qkv, self_out, cross_query, cross_kv, cross_out, ffn_in, ffn_out, ln_gain, ln_bias, omega_scale, dp,
):
    x = inputs.reshape(L, D)
    me = lax.axis_index("mem")
    own_src = lax.dynamic_slice_in_dim(src_len, me, 1, 0)
    meta = jnp.pad(jnp.concatenate([tgt_len, own_src], axis=0), ((0, 6), (0, 112)))

    shape = jax.ShapeDtypeStruct
    fwd_out = [
        shape((L, D), bf),
        shape((L, 3 * D), bf),
        shape((L, D), bf),
        shape((HEADS, L, 128), bf),
        shape((L, 128), bf),
        shape((L, D), f32),
        shape((L, 1), f32),
        shape((L, D), bf),
        shape((L, D), bf),
        shape((L, 2 * D), bf),
        shape((HEADS, L, 128), bf),
        shape((L, 128), bf),
        shape((HEADS, L, 128), bf),
        shape((L, D), f32),
        shape((L, D), bf),
        shape((2 * FF + D, D), bf),
        shape((16, D), f32),
    ]
    fwd = pl.pallas_call(
        forward_kernel,
        out_shape=fwd_out,
        in_specs=[VM] * 14,
        out_specs=[VM] * len(fwd_out),
        scratch_shapes=[
            pltpu.VMEM((L, 128), bf),
            pltpu.VMEM((L, 1), f32),
            pltpu.VMEM((L, D), bf),
            pltpu.VMEM((L, FF), bf),
            pltpu.VMEM((L, FF), bf),
            pltpu.VMEM((L, D), bf),
            pltpu.VMEM((L, D), bf),
            pltpu.VMEM((L, D), bf),
            pltpu.VMEM((TB, FF), f32),
            pltpu.SemaphoreType.DMA((4,)),
            pltpu.SemaphoreType.DMA((4,)),
            pltpu.SemaphoreType.DMA,
        ],
        compiler_params=pltpu.CompilerParams(collective_id=0, has_side_effects=True, vmem_limit_bytes=62 << 20),
        name="forward",
    )(
        x, memory, cotangent.reshape(L, D), meta, self_qkv, self_out, cross_query, cross_kv, cross_out,
        ffn_in, ffn_out, ln_gain, ln_bias, omega_scale,
    )
    (output, packed, sh, qfs, kfs, n1, r1, q8, mem, kv, qfc, kfc, dfc, pre2, do, gffn, vecs) = fwd

    bwd_out = [
        shape((L, D), f32),
        shape((4, L // 4, D), bf),
        shape((2 * FF + D, D), bf),
        shape((4 * D, D), bf),
        shape((PAIRS, D, 384), bf),
        shape((16, D), f32),
    ]
    scratch = [
        pltpu.VMEM((L, D), bf),
        pltpu.VMEM((L, D), bf),
        pltpu.VMEM((L, 2 * D), bf),
        pltpu.VMEM((L, D), bf),
        pltpu.VMEM((L, D), f32),
        pltpu.VMEM((L, D), bf),
        pltpu.VMEM((L, D), bf),
        pltpu.VMEM((HEADS, L, 128), bf),
        pltpu.VMEM((L, 3 * D), bf),
        pltpu.VMEM((4 * D, D), bf),
        pltpu.VMEM((PAIRS, D, 384), bf),
        pltpu.VMEM((64, D), f32),
        pltpu.VMEM((3, 16, D), f32),
        pltpu.VMEM((4, 16, D), f32),
    ]
    for n, w in SEGMENTS:
        scratch += seg_scratch(n, w)
    count = len(SEGMENTS)
    scratch += [
        pltpu.SemaphoreType.DMA((count, 22)),
        pltpu.SemaphoreType.DMA((count, 22)),
        pltpu.SemaphoreType.DMA((48,)),
        pltpu.SemaphoreType.DMA((6,)),
        pltpu.SemaphoreType.DMA((6,)),
        pltpu.SemaphoreType.DMA((4,)),
        pltpu.SemaphoreType.DMA((4,)),
    ]
    igrad, mgrad, f1, f2, f3, small = pl.pallas_call(
        backward_kernel,
        out_shape=bwd_out,
        in_specs=[VM] * 15 + [ANY] + [VM] * 8,
        out_specs=[VM] + [ANY] * 4 + [VM],
        scratch_shapes=scratch,
        compiler_params=pltpu.CompilerParams(collective_id=1, has_side_effects=True, vmem_limit_bytes=63 << 20),
        name="backward",
    )(
        x, packed, sh, qfs, kfs, n1, r1, q8, mem, kv, qfc, kfc, dfc, pre2, do, gffn, vecs,
        self_qkv, self_out, cross_query, cross_kv, ln_gain, ln_bias, omega_scale,
    )

    blocks = dp // 8
    if blocks > 1:
        groups = [[i + 8 * b for b in range(blocks)] for i in range(8)]
        f1, f2, f3, small = lax.psum((f1, f2, f3, small), "dp", axis_index_groups=groups)

    def columns(stack, count):
        return stack.reshape(count, D, D).transpose(1, 0, 2).reshape(D, count * D).astype(f32)

    qkv_grad = f3.reshape(PAIRS, D, 3, 128).transpose(1, 2, 0, 3).reshape(D, 3 * D).astype(f32)
    return (
        output.reshape(1, L, D),
        igrad.reshape(1, L, D),
        mgrad.astype(f32),
        qkv_grad,
        f2[3 * D :].astype(f32),
        f2[:D].astype(f32),
        columns(f2[D : 3 * D], 2),
        f1[2 * FF :].astype(f32),
        columns(f1[FF : 2 * FF], FF // D),
        f1[:FF].astype(f32),
        small[0:3],
        small[3:6],
        small[6:9],
    )


def solution(mesh):
    rows = P(("dp", "mem"), None, None)
    return jax.shard_map(
        functools.partial(per_device, dp=mesh.shape["dp"]),
        mesh=mesh,
        in_specs=(rows, P("dp", "mem", None), rows, P(("dp", "mem"), None), P("dp", None)) + (P(),) * 10,
        out_specs=(rows, rows, P("dp", "mem", None)) + (P(),) * 10,
        check_vma=False,
    )
```

```python
import functools

import jax
import jax.numpy as jnp
from jax import lax
from jax.experimental import pallas as pl
from jax.experimental.pallas import tpu as pltpu
from jax.sharding import PartitionSpec as P

f32 = jnp.float32
bf = jnp.bfloat16
MESH = pl.DeviceIdType.MESH
NN = (((1,), (0,)), ((), ()))
NT = (((1,), (1,)), ((), ()))
TN = (((0,), (0,)), ((), ()))

L = 1024
D = 512
FF = 2048
HEADS = 8
PAIRS = HEADS // 2
SHORT = 64
SCALE = 0.125
NEG = -1e30
EPS = 1e-05
GELU_C = 0.7978845608028654
GELU_A = 0.044715


def dot(a, b, dims=NN):
    return lax.dot_general(a, b, dims, preferred_element_type=f32)


def span(i, n):
    return pl.ds(pl.multiple_of(i * n, n), n)


def loop(n, body):
    def step(i, carry):
        body(i)
        return carry

    lax.fori_loop(0, n, step, 0)


def half_lanes():
    return lax.broadcasted_iota(jnp.int32, (1, 128), 1) < 64


def norm(values):
    centred = values - jnp.mean(values, axis=-1, keepdims=True)
    scaler = lax.rsqrt(jnp.mean(centred * centred, axis=-1, keepdims=True) + EPS)
    return centred * scaler, scaler


def norm_back(upstream, normed, scaler, gain_row):
    scaled = upstream * gain_row
    centred = scaled - jnp.mean(scaled, axis=-1, keepdims=True)
    centred = centred - normed * jnp.mean(scaled * normed, axis=-1, keepdims=True)
    return centred * scaler


def total(values):
    return jnp.sum(values, axis=0, keepdims=True)


def lane_of():
    return lax.broadcasted_iota(jnp.int32, (1, 128), 1)


def put_parts(values, head, old):
    at = lane_of() - (16 + 3 * head)
    high = values.astype(bf).astype(f32)
    rest = values - high
    middle = rest.astype(bf).astype(f32)
    low = rest - middle
    return jnp.where(at == 0, high, jnp.where(at == 1, middle, jnp.where(at == 2, low, old)))


def head_keys(feats, head):
    at = lane_of() - (16 + 3 * head)
    return jnp.where((at >= 0) & (at < 3), jnp.ones_like(feats), feats)


def key_features(lengths, is_doc, rows, first):
    pos = first + lax.broadcasted_iota(jnp.int32, (rows, 128), 0)
    lane = lax.broadcasted_iota(jnp.int32, (rows, 128), 1)
    seg = (pos >> 6) * (1 - is_doc)
    inside = (seg == lane) & (pos - seg * SHORT < lengths)
    feats = jnp.where(lane < 16, jnp.where(inside, 0.0, NEG), 0.0)
    hot = jnp.where(seg == lane, 1.0, 0.0)
    return feats.astype(bf), hot.astype(bf), jnp.where(inside, 1.0, 0.0)


def softmax_pair(j, qp, hot, sections, lse_ref, rows):
    half = half_lanes()
    mixed = []
    feats = lse_ref[rows, :].astype(f32)
    for e in range(2):
        sel = half if e == 0 else jnp.logical_not(half)
        qa = jnp.concatenate([jnp.where(sel, qp, jnp.zeros_like(qp)), hot], axis=1)
        scores = []
        largest = None
        for keys, _, mask in sections:
            s = dot(qa, keys, NT)
            if mask is not None:
                s = jnp.where(mask, s, NEG)
            scores.append(s)
            m = jnp.max(s, axis=1, keepdims=True)
            largest = m if largest is None else jnp.maximum(largest, m)
        acc = None
        for s, (_, values, _) in zip(scores, sections):
            o = dot(jnp.exp(s - largest).astype(bf), values)
            acc = o if acc is None else acc + o
        summed = acc[:, 128:]
        feats = put_parts(-(largest + jnp.log(summed)), 2 * j + e, feats)
        mixed.append(acc[:, :128] / summed)
    lse_ref[rows, :] = feats.astype(bf)
    return jnp.where(half, mixed[0], mixed[1]).astype(bf)


def back_tile(j, k_rows, v_rows, kfeat, qp, qfeat, gp, gfeat, mask):
    half = half_lanes()
    dk, dv, dq = [], [], []
    for e in range(2):
        sel = half if e == 0 else jnp.logical_not(half)
        kf = head_keys(kfeat, 2 * j + e)
        qa = jnp.concatenate([jnp.where(sel, qp, jnp.zeros_like(qp)), qfeat], axis=1)
        ga = jnp.concatenate([jnp.where(sel, gp, jnp.zeros_like(gp)), gfeat], axis=1)
        probs = jnp.exp(dot(jnp.concatenate([k_rows, kf], axis=1), qa, NT))
        if mask is not None:
            width = mask.shape[1]
            first = jnp.where(mask, probs[:, :width], 0.0)
            probs = first if probs.shape[1] == width else jnp.concatenate([first, probs[:, width:]], axis=1)
        ds = (probs * dot(jnp.concatenate([v_rows, kf], axis=1), ga, NT)).astype(bf)
        dv.append(dot(probs.astype(bf), gp))
        dk.append(dot(ds, qp))
        dq.append(dot(ds, k_rows, TN))
    return (
        jnp.where(half, dk[0], dk[1]),
        jnp.where(half, dv[0], dv[1]),
        jnp.where(half, dq[0], dq[1]),
    )


def delta_features(product):
    half = half_lanes()
    feats = jnp.zeros((product.shape[0], 128), f32)
    for j in range(PAIRS):
        part = product[:, 128 * j : 128 * (j + 1)]
        for e in range(2):
            sel = half if e == 0 else jnp.logical_not(half)
            delta = jnp.sum(jnp.where(sel, part, 0.0), axis=1, keepdims=True)
            feats = put_parts(-delta, 2 * j + e, feats)
    return feats.astype(bf)


SELF_BQ = 256
SELF_BK = 256
CROSS_BQ = 512
CROSS_BK = 256
TB = 256
WIDE = 512


class Segment:
    def __init__(self, index, source, parts, bufs, final, sems, place):
        self.index, self.source, self.parts = index, source, parts
        self.n = source.shape[0]
        (self.r0, self.r1, self.r2, self.r3, self.fin) = bufs
        self.final = final
        self.send, self.recv, self.local = sems
        self.place = place

    def remote(self, src, dst, k, device):
        return pltpu.make_async_remote_copy(
            src_ref=src,
            dst_ref=dst,
            send_sem=self.send.at[self.index, k],
            recv_sem=self.recv.at[self.index, k],
            device_id=device,
            device_id_type=MESH,
        )

    def mine(self, first, count):
        return pl.ds(pl.multiple_of(self.place[2][0] * (self.n // 2) + first, 16), count)

    def core_copy(self):
        n, (dp, me, bits) = self.n, self.place
        other = pl.ds(pl.multiple_of((1 - bits[0]) * (n // 2), 16), n // 2)
        return self.remote(self.source.at[other, :], self.r0, 0, (dp + 1 - 2 * bits[0], me))

    def partner(self, axis):
        dp, me, bits = self.place
        return (dp + 2 * axis * (1 - 2 * bits[axis]), me)

    def axes(self, p):
        return (1, 2) if self.parts[p][2] == 0 else (2, 1)

    def lanes(self, p):
        return slice(self.parts[p][0], self.parts[p][1])

    def offset(self, p, depth):
        if depth == 0:
            return 0
        n, (_, me, bits) = self.n, self.place
        one, two = self.axes(p)
        result = bits[one] * (n // 4)
        if depth > 1:
            result = result + bits[two] * (n // 8)
        if depth > 2:
            result = result + me * (n // 32)
        return result

    def halving(self, p, depth):
        n, (_, _, bits) = self.n, self.place
        axis = self.axes(p)[depth - 1]
        size = n // (4 if depth == 1 else 8)
        other = self.offset(p, depth - 1) + (1 - bits[axis]) * size
        buf = self.r1 if depth == 1 else self.r2
        return self.remote(
            self.source.at[self.mine(other, size), self.lanes(p)],
            buf.at[:, self.lanes(p)],
            2 * depth - 1 + p,
            self.partner(axis),
        )

    def quarter(self, p, t):
        n, (dp, me, _) = self.n, self.place
        peer = lax.rem(me + t, 4)
        return self.remote(
            self.source.at[self.mine(self.offset(p, 2) + peer * (n // 32), n // 32), self.lanes(p)],
            self.r3.at[t - 1, :, self.lanes(p)],
            5 + 3 * p + t - 1,
            (dp, peer),
        )

    def final_rows(self, p, depth):
        size = self.n // (2, 4, 8, 32)[depth]
        lanes = slice(None) if p is None else self.lanes(p)
        return self.final.at[self.mine(self.offset(p, depth), size), lanes]

    def keep_copy(self, p):
        return pltpu.make_async_copy(
            self.fin.at[:, self.lanes(p)], self.final_rows(p, 3), self.local.at[2 * self.index + p]
        )

    def spread(self, p, t):
        dp, me, _ = self.place
        return self.remote(
            self.fin.at[:, self.lanes(p)],
            self.final_rows(p, 3),
            11 + 3 * p + t - 1,
            (dp, lax.rem(me + t, 4)),
        )

    def doubling(self, p, depth):
        ref = self.final_rows(p, depth)
        return self.remote(ref, ref, 15 + 2 * (3 - depth) + p, self.partner(self.axes(p)[depth - 1]))

    def core_back(self):
        dp, me, bits = self.place
        ref = self.final_rows(None, 0)
        return self.remote(ref, ref, 21, (dp + 1 - 2 * bits[0], me))

    def add(self, first, buf, count, lanes):
        step = 128 if count % 128 == 0 else count

        def body(i):
            rows = self.mine(first + i * step, step)
            self.source[rows, lanes] = self.source[rows, lanes] + buf[pl.ds(pl.multiple_of(i * step, 16), step), lanes]

        if count == step:
            body(0)
        else:
            loop(count // step, body)

    def stages(self):
        n = self.n
        both = range(len(self.parts))

        def s0():
            self.core_copy().start()

        def s1():
            self.core_copy().wait()
            self.add(0, self.r0, n // 2, slice(None))
            for p in both:
                self.halving(p, 1).start()

        def s2():
            for p in both:
                self.halving(p, 1).wait()
                self.add(self.offset(p, 1), self.r1, n // 4, self.lanes(p))
                self.halving(p, 2).start()

        def s3():
            for p in both:
                self.halving(p, 2).wait()
                self.add(self.offset(p, 2), self.r2, n // 8, self.lanes(p))
                for t in range(1, 4):
                    self.quarter(p, t).start()

        def s4():
            for p in both:
                for t in range(1, 4):
                    self.quarter(p, t).wait()
                lanes = self.lanes(p)
                mine = self.source[self.mine(self.offset(p, 3), n // 32), lanes].astype(f32)
                for t in range(3):
                    mine = mine + self.r3[t, :, lanes].astype(f32)
                self.fin[:, lanes] = mine.astype(bf)
                self.keep_copy(p).start()
                for t in range(1, 4):
                    self.spread(p, t).start()

        def s5():
            for p in both:
                self.keep_copy(p).wait()
                for t in range(1, 4):
                    self.spread(p, t).wait()
                self.doubling(p, 2).start()

        def s6():
            for p in both:
                self.doubling(p, 2).wait()
                self.doubling(p, 1).start()

        def s7():
            for p in both:
                self.doubling(p, 1).wait()
            self.core_back().start()

        def s8():
            self.core_back().wait()

        return [s0, s1, s2, s3, s4, s5, s6, s7, s8]


SEGMENTS = [(FF, D), (D, FF), (4 * D, D), (D, D)] + [(D, 384)] * PAIRS


def seg_scratch(n, w):
    return [
        pltpu.VMEM((n // 2, w), bf),
        pltpu.VMEM((n // 4, w), bf),
        pltpu.VMEM((n // 8, w), bf),
        pltpu.VMEM((3, n // 32, w), bf),
        pltpu.VMEM((n // 32, w), bf),
    ]


SCHEDULE = {
    0: [("in_weight", 0), ("in_weight", 7), ("cross", 4), ("cross", 9), ("cross", 14), ("first", 1), ("self", 1), ("self", 8), ("self", 10)],
    1: [("cross", 0), ("cross", 3), ("cross", 7), ("cross", 10), ("query", 1), ("self", 0), ("self", 5), ("self", 13), ("input", 0)],
    2: [("first", 0), ("so", 0), ("self", 4), ("self", 10), ("self", 15), ("end", 2), ("end", 8), ("end", 15), ("end", 21)],
    3: [("self", 0), ("self", 1), ("self", 9), ("self", 13), ("input", 0), ("end", 3), ("end", 9), ("end", 16), ("end", 22)],
    4: [("self", 4), ("self", 5), ("self", 14), ("input", 1), ("end", 5), ("end", 11), ("end", 17), ("end", 23), ("end", 26)],
    5: [("self", 8), ("self", 11), ("self", 14), ("input", 1), ("end", 6), ("end", 12), ("end", 18), ("end", 24), ("end", 28)],
    6: [("self", 12), ("self", 15), ("input", 2), ("end", 1), ("end", 7), ("end", 13), ("end", 20), ("end", 27), ("end", 29)],
    7: [("input", 2), ("end", 0), ("end", 4), ("end", 10), ("end", 14), ("end", 19), ("end", 25), ("end", 30), ("end", 31)],
}


def layer_kernel(
    tgt_len, src_len, x_in, meml, cot_in, wqkv_in, wso_in, wcq_in, wckv_in, wco_in, win_in, wout_in, gain, bias, omega,
    out, igrad, mgrad, f_out, f_in, f_two, f_so, f_qkv, vout,
    x, cot, wqkv, wso, wcq, wckv, wco, win, wout,
    packed, sh, n1, r1, q8, mem, kv, ch, qfs, kfs, qfc, kfc, dfc, hot, keep, pre2, do,
    act, hg, br3, slow, br2, dg, g2, gso, g3, vec, vbuf, vz,
    *rest,
):
    (load_sem, out_sem, send, recv, local, vsend, vrecv, xsend, xrecv, msend, mrecv) = rest[-11:]
    seg_bufs = rest[:-11]
    me = lax.axis_index("mem")
    dp = lax.axis_index("dp")
    n = 4
    piece = L // n
    bits = (lax.rem(dp, 2), lax.rem(dp // 2, 2), lax.rem(dp // 4, 2))
    place = (dp, me, bits)
    near = [(dp + (1 << a) * (1 - 2 * bits[a]), me) for a in range(3)]
    peers = near + [(dp, lax.rem(me + t, n)) for t in range(1, n)]

    loads = {}
    for i, (name, src, dst) in enumerate(
        [
            ("x", x_in, x), ("wqkv", wqkv_in, wqkv), ("wso", wso_in, wso), ("wcq", wcq_in, wcq), ("wckv", wckv_in, wckv),
            ("wco", wco_in, wco), ("win", win_in, win), ("wout", wout_in, wout), ("cot", cot_in, cot),
        ]
    ):
        loads[name] = pltpu.make_async_copy(src, dst, load_sem.at[i])
        loads[name].start()

    barrier = pltpu.get_barrier_semaphore()
    for peer in peers:
        pl.semaphore_signal(barrier, inc=1, device_id=peer, device_id_type=MESH)
    pl.semaphore_wait(barrier, len(peers))

    def exchange(t):
        peer = lax.rem(me + t, n)
        return pltpu.make_async_remote_copy(
            src_ref=meml.at[peer],
            dst_ref=mem.at[span(me, piece), :],
            send_sem=xsend.at[t],
            recv_sem=xrecv.at[t],
            device_id=(dp, peer),
            device_id_type=MESH,
        )

    own = pltpu.make_async_copy(meml.at[me], mem.at[span(me, piece), :], xsend.at[0])
    for t in range(1, n):
        exchange(t).start()
    own.start()

    whole_parts = ((0, 256, 0), (256, 512, 1))
    wide_parts = ((0, 1024, 0), (1024, 2048, 1))
    pair_parts = ((0, 128, 0), (128, 384, 1))
    sources = [wout, win, g2, gso] + [g3.at[j] for j in range(PAIRS)]
    finals = [f_out, f_in, f_two, f_so] + [f_qkv.at[j] for j in range(PAIRS)]
    ticks = {}
    for i, (rows, width) in enumerate(SEGMENTS):
        parts = {D: whole_parts, FF: wide_parts, 384: pair_parts}[width]
        stages = Segment(i, sources[i], parts, seg_bufs[5 * i : 5 * i + 5], finals[i], (send, recv, local), place).stages()
        for (phase, step), fn in zip(SCHEDULE[i], stages):
            ticks.setdefault(phase, []).append((step, i, fn))

    def at(phase, step, fn):
        ticks.setdefault(phase, []).append((step, -1, fn))

    def run(phase, i, unit=1, part=0):
        todo = {}
        for step, order, fn in ticks.get(phase, []):
            if step % unit == part:
                todo.setdefault(step // unit, []).append((order, fn))
        for step, fns in sorted(todo.items()):

            @pl.when(i == step)
            def _(fns=fns):
                for _, fn in sorted(fns, key=lambda item: item[0]):
                    fn()

    lane = lane_of()
    lengths = [jnp.zeros((1, 128), jnp.int32)] * 2
    for s in range(16):
        lengths[0] = jnp.where(lane == s, tgt_len[0, s], lengths[0])
        lengths[1] = jnp.where(lane == s, src_len[me, s], lengths[1])
    is_doc = jnp.where(src_len[me, 0] > SHORT, 1, 0)

    def features(i):
        rows = span(i, TB)
        feats, one_hot, inside = key_features(lengths[0], is_doc, TB, i * TB)
        kfs[rows, :] = feats
        hot[rows, :] = one_hot
        qfs[rows, :] = one_hot
        qfc[rows, :] = one_hot
        keep[rows, :] = jnp.sum(inside, axis=1, keepdims=True)
        feats, _, _ = key_features(lengths[1], is_doc, TB, i * TB)
        kfc[rows, :] = feats

    loop(L // TB, features)
    loads["x"].wait()
    loads["wqkv"].wait()

    def project(i):
        rows = span(i, TB)
        packed[rows, :D] = dot(x[rows, :], wqkv[:, :D]).astype(bf) * bf(SCALE)
        packed[rows, D:] = dot(x[rows, :], wqkv[:, D:]).astype(bf)

    loop(L // TB, project)

    causal = lax.broadcasted_iota(jnp.int32, (SELF_BQ, SELF_BQ), 0) >= lax.broadcasted_iota(
        jnp.int32, (SELF_BQ, SELF_BQ), 1
    )

    def lanes_at(first, j):
        return pl.ds(pl.multiple_of(first + j * 128, 128), 128)

    for b in range(L // SELF_BQ):
        low, high = b * SELF_BQ, (b + 1) * SELF_BQ

        def self_pair(j, low=low, high=high):
            def section(first, last, mask):
                keys = jnp.concatenate([packed[first:last, lanes_at(D, j)], kfs[first:last, :]], axis=1)
                values = packed[first:last, lanes_at(2 * D, j)]
                return keys, jnp.concatenate([values, jnp.ones((last - first, 128), bf)], axis=1), mask

            sections = [section(low, high, causal)]
            if low:
                sections.append(section(0, low, None))
            sh[low:high, span(j, 128)] = softmax_pair(
                j, packed[low:high, span(j, 128)], hot[low:high, :], sections, qfs, slice(low, high)
            )

        loop(PAIRS, self_pair)

    loads["wso"].wait()
    loads["wcq"].wait()

    def first_norm(i):
        rows = span(i, TB)
        normed, scaler = norm(omega[0:1, :] * x[rows, :].astype(f32) + dot(sh[rows, :], wso[...]))
        n1[rows, :] = normed
        r1[rows, :] = scaler
        first = (normed * gain[0:1, :] + bias[0:1, :]).astype(bf)
        q8[rows, :] = dot(first, wcq[...]).astype(bf) * bf(SCALE)

    loop(L // TB, first_norm)

    own.wait()
    for t in range(1, n):
        exchange(t).wait()
    loads["wckv"].wait()

    def memory_project(i):
        rows = span(i, TB)
        kv[rows, :] = dot(mem[rows, :], wckv[...]).astype(bf)

    loop(L // TB, memory_project)

    def cross_pair(i):
        j = i // (L // CROSS_BQ)
        rows = span(lax.rem(i, L // CROSS_BQ), CROSS_BQ)
        keys = jnp.concatenate([kv[:, span(j, 128)], kfc[...]], axis=1)
        values = jnp.concatenate([kv[:, lanes_at(D, j)], jnp.ones((L, 128), bf)], axis=1)
        ch[rows, span(j, 128)] = softmax_pair(j, q8[rows, span(j, 128)], hot[rows, :], [(keys, values, None)], qfc, rows)

    loop(PAIRS * (L // CROSS_BQ), cross_pair)

    vec[...] = jnp.zeros_like(vec)
    for name in ("wco", "win", "wout", "cot"):
        loads[name].wait()

    def tokens(i):
        rows = span(i, TB)
        first = n1[rows, :] * gain[0:1, :] + bias[0:1, :]
        n2, r2 = norm(omega[1:2, :] * first + dot(ch[rows, :], wco[...]))
        second = n2 * gain[1:2, :] + bias[1:2, :]
        second_low = second.astype(bf)
        slow[rows, :] = second_low
        branch = jnp.zeros((TB, D), f32)
        for c in range(FF // WIDE):
            cols = slice(c * WIDE, (c + 1) * WIDE)
            h = dot(second_low, win[:, cols])
            square = h * h
            th = jnp.tanh(GELU_C * (h + GELU_A * (h * square)))
            cdf = 0.5 * (1.0 + th)
            low = (h * cdf).astype(bf)
            act[rows, cols] = low
            dg[c * TB : (c + 1) * TB, :] = cdf + 0.5 * h * (1.0 - th * th) * (GELU_C * (1.0 + 3.0 * GELU_A * square))
            branch = branch + dot(low, wout[cols, :])
        n3, r3 = norm(omega[2:3, :] * second + branch)
        third = n3 * gain[2:3, :] + bias[2:3, :]
        kept = keep[rows, :]
        up = cot[rows, :].astype(f32) * kept
        cot[rows, :] = (third * kept).astype(bf)
        pre3 = norm_back(up, n3, r3, gain[2:3, :])
        vec[2:3, :] += total(up * n3)
        vec[5:6, :] += total(up)
        vec[8:9, :] += total(pre3 * second)
        low3 = pre3.astype(bf)
        br3[rows, :] = low3
        grad = omega[2:3, :] * pre3
        for c in range(FF // WIDE):
            cols = slice(c * WIDE, (c + 1) * WIDE)
            hl = (dot(low3, wout[cols, :], NT) * dg[c * TB : (c + 1) * TB, :]).astype(bf)
            hg[rows, cols] = hl
            grad = grad + dot(hl, win[:, cols], NT)
        back2 = norm_back(grad, n2, r2, gain[1:2, :])
        vec[1:2, :] += total(grad * n2)
        vec[4:5, :] += total(grad)
        vec[7:8, :] += total(back2 * first)
        pre2[rows, :] = back2
        low2 = back2.astype(bf)
        br2[rows, :] = low2
        dlow = dot(low2, wco[...], NT).astype(bf)
        do[rows, :] = dlow
        dfc[rows, :] = delta_features(dlow.astype(f32) * ch[rows, :].astype(f32))

    loop(L // TB, tokens)
    out_copy = pltpu.make_async_copy(cot, out, out_sem.at[0])
    out_copy.start()

    def out_weight(i):
        wout[span(i, 256), :] = dot(act[:, span(i, 256)], br3[...], TN).astype(bf)

    loop(FF // 256, out_weight)

    def in_weight(i):
        run("in_weight", i)
        rows = span(i // 4, 256)
        cols = span(lax.rem(i, 4), WIDE)
        win[rows, cols] = dot(slow[:, rows], hg[:, cols], TN).astype(bf)

    loop(8, in_weight)

    def cross_out_weight(i):
        run("co", i)
        g2[span(i, 256), :] = dot(ch[:, span(i, 256)], br2[...], TN).astype(bf)

    loop(2, cross_out_weight)

    kvg, qg, fl = hg.at[:, : 2 * D], hg.at[:, 2 * D : 3 * D], hg.at[:, 3 * D :]
    pg, mgs = act.at[:, : 3 * D], act.at[:, 3 * D :]
    pre1, br1 = dg, br3
    blocks = L // CROSS_BK

    def cross_back(i):
        run("cross", i)
        j = i // blocks
        b = lax.rem(i, blocks)
        rows = span(b, CROSS_BK)
        lanes = span(j, 128)
        dk, dv, dq = back_tile(
            j, kv[rows, lanes], kv[rows, lanes_at(D, j)], kfc[rows, :], q8[:, lanes], qfc[...], do[:, lanes], dfc[...], None
        )
        kvg[rows, lanes] = dk.astype(bf)
        kvg[rows, lanes_at(D, j)] = dv.astype(bf)

        @pl.when(b == 0)
        def _():
            pre1[:, lanes] = dq

        @pl.when(b > 0)
        def _():
            pre1[:, lanes] += dq

    loop(PAIRS * blocks, cross_back)

    def query_low(i):
        run("query", i)
        rows = span(i, TB)
        fl[rows, :] = (n1[rows, :] * gain[0:1, :] + bias[0:1, :]).astype(bf)
        qg[rows, :] = (pre1[rows, :] * SCALE).astype(bf)
        mgs[rows, :] = dot(kvg[rows, :], wckv[...], NT).astype(bf)

    loop(L // TB, query_low)

    def memory_back(t):
        peer = lax.rem(me + t, n)
        return pltpu.make_async_remote_copy(
            src_ref=mgs.at[span(peer, piece), :],
            dst_ref=mgrad.at[me],
            send_sem=msend.at[t],
            recv_sem=mrecv.at[t],
            device_id=(dp, peer),
            device_id_type=MESH,
        )

    memory_own = pltpu.make_async_copy(mgs.at[span(me, piece), :], mgrad.at[me], msend.at[0])
    memory_own.start()
    for t in range(1, n):
        memory_back(t).start()

    def weights_two(i):
        run("two", i)
        cols = span(i, 256)
        g2[pl.ds(pl.multiple_of(D + i * 256, 256), 256), :] = dot(fl[:, cols], qg[...], TN).astype(bf)
        g2[pl.ds(pl.multiple_of(2 * D + i * 256, 256), 256), :] = dot(mem[:, cols], kvg[:, :D], TN).astype(bf)
        g2[pl.ds(pl.multiple_of(3 * D + i * 256, 256), 256), :] = dot(mem[:, cols], kvg[:, D:], TN).astype(bf)

    loop(2, weights_two)

    def first_back(i):
        run("first", i)
        rows = span(i, TB)
        normed = n1[rows, :]
        grad = omega[1:2, :] * pre2[rows, :] + dot(qg[rows, :], wcq[...], NT)
        back1 = norm_back(grad, normed, r1[rows, :], gain[0:1, :])
        vec[0:1, :] += total(grad * normed)
        vec[3:4, :] += total(grad)
        vec[6:7, :] += total(back1 * x[rows, :].astype(f32))
        pre1[rows, :] = back1
        low1 = back1.astype(bf)
        br1[rows, :] = low1
        dlow = dot(low1, wso[...], NT).astype(bf)
        do[rows, :] = dlow
        dfc[rows, :] = delta_features(dlow.astype(f32) * sh[rows, :].astype(f32))

    loop(L // TB, first_back)

    def self_out_weight(i):
        run("so", i)
        gso[span(i, 256), :] = dot(sh[:, span(i, 256)], br1[...], TN).astype(bf)

    loop(2, self_out_weight)

    def vec_near(a):
        return pltpu.make_async_remote_copy(
            src_ref=vec.at[pl.ds(16 * a, 16), :],
            dst_ref=vbuf.at[a],
            send_sem=vsend.at[a],
            recv_sem=vrecv.at[a],
            device_id=near[a],
            device_id_type=MESH,
        )

    def vec_far(t):
        return pltpu.make_async_remote_copy(
            src_ref=vec.at[pl.ds(48, 16), :],
            dst_ref=vz.at[me],
            send_sem=vsend.at[2 + t],
            recv_sem=vrecv.at[2 + t],
            device_id=(dp, lax.rem(me + t, n)),
            device_id_type=MESH,
        )

    def vec_next(a):
        vec_near(a).wait()
        vec[16 * (a + 1) : 16 * (a + 2), :] = vec[16 * a : 16 * (a + 1), :] + vbuf[a]
        if a < 2:
            vec_near(a + 1).start()
        else:
            for t in range(1, n):
                vec_far(t).start()

    def vec_last():
        for t in range(1, n):
            vec_far(t).wait()
        vz[me] = vec[48:64, :]
        vout[...] = (vz[0] + vz[1]) + (vz[2] + vz[3])

    vec_near(0).start()
    at("self", 1, lambda: vec_next(0))
    at("self", 3, lambda: vec_next(1))
    at("self", 5, lambda: vec_next(2))
    at("self", 8, vec_last)

    below = lax.broadcasted_iota(jnp.int32, (SELF_BK, SELF_BK), 1) >= lax.broadcasted_iota(
        jnp.int32, (SELF_BK, SELF_BK), 0
    )
    parts = L // SELF_BK

    def self_back(j):
        dqs = []
        for b in range(parts):
            run("self", j, parts, b)
            low, high = b * SELF_BK, (b + 1) * SELF_BK
            dk, dv, dq = back_tile(
                j,
                packed[low:high, lanes_at(D, j)],
                packed[low:high, lanes_at(2 * D, j)],
                kfs[low:high, :],
                packed[low:, span(j, 128)],
                qfs[low:, :],
                do[low:, span(j, 128)],
                dfc[low:, :],
                below,
            )
            pg[low:high, lanes_at(D, j)] = dk.astype(bf)
            pg[low:high, lanes_at(2 * D, j)] = dv.astype(bf)
            for i in range(b, parts):
                share = dq[(i - b) * SELF_BK : (i - b + 1) * SELF_BK, :]
                if b == 0:
                    dqs.append(share)
                else:
                    dqs[i] = dqs[i] + share
        for i, share in enumerate(dqs):
            pg[i * SELF_BK : (i + 1) * SELF_BK, span(j, 128)] = (share * SCALE).astype(bf)
        for c in range(3):
            g3[j, :, c * 128 : (c + 1) * 128] = dot(x[...], pg[:, lanes_at(c * D, j)], TN).astype(bf)

    loop(PAIRS, self_back)

    def igrad_copy(i):
        return pltpu.make_async_copy(pre1.at[span(i, TB), :], igrad.at[span(i, TB), :], out_sem.at[1 + i])

    def input_back(i):
        run("input", i)
        rows = span(i, TB)
        pre1[rows, :] = omega[0:1, :] * pre1[rows, :] + dot(pg[rows, :], wqkv[...], NT)
        igrad_copy(i).start()

    loop(L // TB, input_back)
    out_copy.wait()
    memory_own.wait()
    for t in range(1, n):
        memory_back(t).wait()
    for _, _, fn in sorted(ticks["end"], key=lambda item: item[:2]):
        fn()
    for i in range(L // TB):
        igrad_copy(i).wait()


CASTS = (
    [(0, (slice(i * D, (i + 1) * D), slice(0, D)), 0, (slice(i * D, (i + 1) * D), slice(0, D))) for i in range(4)]
    + [(1, (slice(0, D), slice(i * D, (i + 1) * D)), 1, (slice(0, D), slice(i * D, (i + 1) * D))) for i in range(4)]
    + [
        (2, (slice(0, D), slice(0, D)), 2, (slice(0, D), slice(0, D))),
        (2, (slice(D, 2 * D), slice(0, D)), 3, (slice(0, D), slice(0, D))),
        (2, (slice(2 * D, 3 * D), slice(0, D)), 4, (slice(0, D), slice(0, D))),
        (2, (slice(3 * D, 4 * D), slice(0, D)), 4, (slice(0, D), slice(D, 2 * D))),
        (3, (slice(0, D), slice(0, D)), 5, (slice(0, D), slice(0, D))),
    ]
)


def cast_kernel(
    out_in, igrad_in, mgrad_in, f_out, f_in, f_two, f_so, f_qkv,
    out, igrad, mgrad, g_out, g_in, g_co, g_cq, g_ckv, g_so, g_qkv,
    narrow, wide, qkv_narrow, qkv_wide, out_held, igrad_held, sems, out_sems,
):
    passed = [(out_in, out_held, out), (igrad_in, igrad_held, igrad)]
    whole_in = [pltpu.make_async_copy(src, held, sems.at[i]) for i, (src, held, _) in enumerate(passed)]
    froms = (f_out, f_in, f_two, f_so)
    tos = (g_out, g_in, g_co, g_cq, g_ckv, g_so)
    pieces = []
    for source, window, target, place in CASTS:
        pieces.append((froms[source].at[window], tos[target].at[place]))
    for i in range(2):
        pieces.append((mgrad_in.at[pl.ds(i * D, D), :], mgrad.at[pl.ds(i * D, D), :]))
    ins = [pltpu.make_async_copy(src, narrow.at[i], sems.at[2 + i]) for i, (src, _) in enumerate(pieces)]
    outs = [pltpu.make_async_copy(wide.at[i], dst, out_sems.at[i]) for i, (_, dst) in enumerate(pieces)]
    qkv_in = pltpu.make_async_copy(f_qkv, qkv_narrow, sems.at[2 + len(pieces)])
    qkv_out = pltpu.make_async_copy(qkv_wide, g_qkv, out_sems.at[len(pieces)])
    for copy in ins:
        copy.start()
    qkv_in.start()
    whole_out = [
        pltpu.make_async_copy(held, dst, out_sems.at[len(pieces) + 1 + i]) for i, (_, held, dst) in enumerate(passed)
    ]
    for copy in whole_in:
        copy.start()
    for i, copy in enumerate(ins):
        copy.wait()

        def body(r, i=i):
            wide[i, span(r, 64), :] = narrow[i, span(r, 64), :].astype(f32)

        loop(D // 64, body)
        outs[i].start()
    qkv_in.wait()

    def body(r):
        for j in range(PAIRS):
            for c in range(3):
                qkv_wide[span(r, 64), c * D + j * 128 : c * D + (j + 1) * 128] = qkv_narrow[
                    j, span(r, 64), c * 128 : (c + 1) * 128
                ].astype(f32)

    loop(D // 64, body)
    qkv_out.start()
    for copy_in, copy_out in zip(whole_in, whole_out):
        copy_in.wait()
        copy_out.start()
    for copy in whole_out + outs:
        copy.wait()
    qkv_out.wait()


VM = pl.BlockSpec(memory_space=pltpu.VMEM)
SM = pl.BlockSpec(memory_space=pltpu.SMEM)
ANY = pl.BlockSpec(memory_space=pl.ANY)


def per_device(
    inputs, memory, cotangent, tgt_len, src_len,
    self_qkv, self_out, cross_query, cross_kv, cross_out, ffn_in, ffn_out, ln_gain, ln_bias, omega_scale, dp,
):
    shape = jax.ShapeDtypeStruct
    scratch = [
        pltpu.VMEM((L, D), bf),
        pltpu.VMEM((L, D), bf),
        pltpu.VMEM((D, 3 * D), bf),
        pltpu.VMEM((D, D), bf),
        pltpu.VMEM((D, D), bf),
        pltpu.VMEM((D, 2 * D), bf),
        pltpu.VMEM((D, D), bf),
        pltpu.VMEM((D, FF), bf),
        pltpu.VMEM((FF, D), bf),
        pltpu.VMEM((L, 3 * D), bf),
        pltpu.VMEM((L, D), bf),
        pltpu.VMEM((L, D), f32),
        pltpu.VMEM((L, 1), f32),
        pltpu.VMEM((L, D), bf),
        pltpu.VMEM((L, D), bf),
        pltpu.VMEM((L, 2 * D), bf),
        pltpu.VMEM((L, D), bf),
        pltpu.VMEM((L, 128), bf),
        pltpu.VMEM((L, 128), bf),
        pltpu.VMEM((L, 128), bf),
        pltpu.VMEM((L, 128), bf),
        pltpu.VMEM((L, 128), bf),
        pltpu.VMEM((L, 128), bf),
        pltpu.VMEM((L, 1), f32),
        pltpu.VMEM((L, D), f32),
        pltpu.VMEM((L, D), bf),
        pltpu.VMEM((L, FF), bf),
        pltpu.VMEM((L, FF), bf),
        pltpu.VMEM((L, D), bf),
        pltpu.VMEM((L, D), bf),
        pltpu.VMEM((L, D), bf),
        pltpu.VMEM((L, D), f32),
        pltpu.VMEM((4 * D, D), bf),
        pltpu.VMEM((D, D), bf),
        pltpu.VMEM((PAIRS, D, 384), bf),
        pltpu.VMEM((64, D), f32),
        pltpu.VMEM((3, 16, D), f32),
        pltpu.VMEM((4, 16, D), f32),
    ]
    for n, w in SEGMENTS:
        scratch += seg_scratch(n, w)
    count = len(SEGMENTS)
    sem = pltpu.SemaphoreType.DMA
    scratch += [
        sem((9,)), sem((5,)), sem((count, 22)), sem((count, 22)), sem((2 * count,)), sem((6,)), sem((6,)),
        sem((4,)), sem((4,)), sem((4,)), sem((4,)),
    ]
    results = pl.pallas_call(
        layer_kernel,
        out_shape=[
            shape((L, D), bf),
            shape((L, D), f32),
            shape((4, L // 4, D), bf),
            shape((FF, D), bf),
            shape((D, FF), bf),
            shape((4 * D, D), bf),
            shape((D, D), bf),
            shape((PAIRS, D, 384), bf),
            shape((16, D), f32),
        ],
        in_specs=[SM] * 2 + [ANY] * 10 + [VM] * 3,
        out_specs=[ANY] * 8 + [VM],
        scratch_shapes=scratch,
        compiler_params=pltpu.CompilerParams(collective_id=0, has_side_effects=True, vmem_limit_bytes=63 << 20),
        name="layer",
    )(
        tgt_len, src_len, inputs.reshape(L, D), memory, cotangent.reshape(L, D), self_qkv, self_out, cross_query, cross_kv,
        cross_out, ffn_in, ffn_out, ln_gain, ln_bias, omega_scale,
    )
    output, igrad, mgrad, grads, small = results[0], results[1], results[2], results[3:8], results[8]

    blocks = dp // 8
    if blocks > 1:
        groups = [[i + 8 * b for b in range(blocks)] for i in range(8)]
        *grads, small = lax.psum((*grads, small), "dp", axis_index_groups=groups)

    pieces = len(CASTS) + 2
    output, igrad, mgrad, g_out, g_in, g_co, g_cq, g_ckv, g_so, g_qkv = pl.pallas_call(
        cast_kernel,
        out_shape=[
            shape((L, D), bf),
            shape((L, D), f32),
            shape((L, D), f32),
            shape((FF, D), f32),
            shape((D, FF), f32),
            shape((D, D), f32),
            shape((D, D), f32),
            shape((D, 2 * D), f32),
            shape((D, D), f32),
            shape((D, 3 * D), f32),
        ],
        in_specs=[ANY] * 8,
        out_specs=[ANY] * 10,
        scratch_shapes=[
            pltpu.VMEM((pieces, D, D), bf),
            pltpu.VMEM((pieces, D, D), f32),
            pltpu.VMEM((PAIRS, D, 384), bf),
            pltpu.VMEM((D, 3 * D), f32),
            pltpu.VMEM((L, D), bf),
            pltpu.VMEM((L, D), f32),
            sem((pieces + 3,)),
            sem((pieces + 3,)),
        ],
        compiler_params=pltpu.CompilerParams(vmem_limit_bytes=62 << 20),
        name="casts",
    )(output, igrad, mgrad.reshape(L, D), *grads)
    return (
        output.reshape(1, L, D),
        igrad.reshape(1, L, D),
        mgrad.reshape(4, L // 4, D),
        g_qkv,
        g_so,
        g_cq,
        g_ckv,
        g_co,
        g_in,
        g_out,
        small[0:3],
        small[3:6],
        small[6:9],
    )


def solution(mesh):
    rows = P(("dp", "mem"), None, None)
    return jax.shard_map(
        functools.partial(per_device, dp=mesh.shape["dp"]),
        mesh=mesh,
        in_specs=(rows, P("dp", "mem", None), rows, P(("dp", "mem"), None), P("dp", None)) + (P(),) * 10,
        out_specs=(rows, rows, P("dp", "mem", None)) + (P(),) * 10,
        check_vma=False,
    )
```

```python
import functools

import jax
import jax.numpy as jnp
from jax import lax
from jax.experimental import pallas as pl
from jax.experimental.pallas import tpu as pltpu
from jax.sharding import PartitionSpec as P

f32 = jnp.float32
bf = jnp.bfloat16
MESH = pl.DeviceIdType.MESH
NN = (((1,), (0,)), ((), ()))
NT = (((1,), (1,)), ((), ()))
TN = (((0,), (0,)), ((), ()))

L = 1024
D = 512
FF = 2048
HEADS = 8
PAIRS = HEADS // 2
SHORT = 64
SCALE = 0.125
NEG = -1e30
EPS = 1e-05
GELU_C = 0.7978845608028654
GELU_A = 0.044715


def dot(a, b, dims=NN):
    return lax.dot_general(a, b, dims, preferred_element_type=f32)


def span(i, n):
    return pl.ds(pl.multiple_of(i * n, n), n)


def loop(n, body):
    def step(i, carry):
        body(i)
        return carry

    lax.fori_loop(0, n, step, 0)


def weave(parts):
    parts = list(parts)
    live = set(range(len(parts)))
    turn = 0
    while live:
        for k in sorted(live):
            if turn >= k and next(parts[k], "done") == "done":
                live.discard(k)
        turn += 1


def half_lanes():
    return lax.broadcasted_iota(jnp.int32, (1, 128), 1) < 64


def norm(values):
    centred = values - jnp.mean(values, axis=-1, keepdims=True)
    scaler = lax.rsqrt(jnp.mean(centred * centred, axis=-1, keepdims=True) + EPS)
    return centred * scaler, scaler


def norm_back(upstream, normed, scaler, gain_row):
    scaled = upstream * gain_row
    centred = scaled - jnp.mean(scaled, axis=-1, keepdims=True)
    centred = centred - normed * jnp.mean(scaled * normed, axis=-1, keepdims=True)
    return centred * scaler


def total(values):
    return jnp.sum(values, axis=0, keepdims=True)


def lane_of():
    return lax.broadcasted_iota(jnp.int32, (1, 128), 1)


def put_parts(values, head, old):
    at = lane_of() - (16 + 3 * head)
    high = values.astype(bf).astype(f32)
    rest = values - high
    middle = rest.astype(bf).astype(f32)
    low = rest - middle
    return jnp.where(at == 0, high, jnp.where(at == 1, middle, jnp.where(at == 2, low, old)))


def head_keys(feats, head):
    at = lane_of() - (16 + 3 * head)
    return jnp.where((at >= 0) & (at < 3), jnp.ones_like(feats), feats)


def key_features(lengths, is_doc, rows, first):
    pos = first + lax.broadcasted_iota(jnp.int32, (rows, 128), 0)
    lane = lax.broadcasted_iota(jnp.int32, (rows, 128), 1)
    seg = (pos >> 6) * (1 - is_doc)
    inside = (seg == lane) & (pos - seg * SHORT < lengths)
    feats = jnp.where(lane < 16, jnp.where(inside, 0.0, NEG), 0.0)
    hot = jnp.where(seg == lane, 1.0, 0.0)
    return feats.astype(bf), hot.astype(bf), jnp.where(inside, 1.0, 0.0)


def softmax_pair(j, qp, sections, lse_ref, rows):
    half = half_lanes()
    mixed = []
    base = lse_ref[rows, :]
    feats = base.astype(f32)
    scores = []
    for e in range(2):
        sel = half if e == 0 else jnp.logical_not(half)
        qa = jnp.concatenate([jnp.where(sel, qp, jnp.zeros_like(qp)), base], axis=1)
        scores.append([dot(qa, keys, NT) for keys, _, _ in sections])
    for e in range(2):
        masked = [s if mask is None else jnp.where(mask, s, NEG) for s, (_, _, mask) in zip(scores[e], sections)]
        largest = functools.reduce(jnp.maximum, [jnp.max(s, axis=1, keepdims=True) for s in masked])
        acc = None
        for s, (_, values, _) in zip(masked, sections):
            o = dot(jnp.exp(s - largest).astype(bf), values)
            acc = o if acc is None else acc + o
        summed = acc[:, 128:]
        feats = put_parts(-(largest + jnp.log(summed)), 2 * j + e, feats)
        mixed.append(acc[:, :128] / summed)
    lse_ref[rows, :] = feats.astype(bf)
    return jnp.where(half, mixed[0], mixed[1]).astype(bf)


def back_tile(j, k_rows, v_rows, kfeat, qp, qfeat, gp, gfeat, mask):
    half = half_lanes()
    dk, dv, dq = [], [], []
    scores, slopes = [], []
    for e in range(2):
        sel = half if e == 0 else jnp.logical_not(half)
        kf = head_keys(kfeat, 2 * j + e)
        qa = jnp.concatenate([jnp.where(sel, qp, jnp.zeros_like(qp)), qfeat], axis=1)
        ga = jnp.concatenate([jnp.where(sel, gp, jnp.zeros_like(gp)), gfeat], axis=1)
        scores.append(dot(jnp.concatenate([k_rows, kf], axis=1), qa, NT))
        slopes.append(dot(jnp.concatenate([v_rows, kf], axis=1), ga, NT))
    for e in range(2):
        probs = jnp.exp(scores[e])
        if mask is not None:
            width = mask.shape[1]
            first = jnp.where(mask, probs[:, :width], 0.0)
            probs = first if probs.shape[1] == width else jnp.concatenate([first, probs[:, width:]], axis=1)
        ds = (probs * slopes[e]).astype(bf)
        dv.append(dot(probs.astype(bf), gp))
        dk.append(dot(ds, qp))
        dq.append(dot(ds, k_rows, TN))
    return (
        jnp.where(half, dk[0], dk[1]),
        jnp.where(half, dv[0], dv[1]),
        jnp.where(half, dq[0], dq[1]),
    )


def delta_features(product):
    half = half_lanes()
    feats = jnp.zeros((product.shape[0], 128), f32)
    for j in range(PAIRS):
        part = product[:, 128 * j : 128 * (j + 1)]
        for e in range(2):
            sel = half if e == 0 else jnp.logical_not(half)
            delta = jnp.sum(jnp.where(sel, part, 0.0), axis=1, keepdims=True)
            feats = put_parts(-delta, 2 * j + e, feats)
    return feats.astype(bf)


SELF_BQ = 512
SELF_BK = 256
CROSS_BQ = 512
CROSS_BK = 512
TB = 512
WIDE = 1024


class Segment:
    def __init__(self, index, source, parts, bufs, final, sems, place):
        self.index, self.source, self.parts = index, source, parts
        self.n = source.shape[0]
        (self.r0, self.r1, self.r2, self.r3, self.fin) = bufs
        self.final = final
        self.send, self.recv, self.local = sems
        self.place = place

    def remote(self, src, dst, k, device):
        return pltpu.make_async_remote_copy(
            src_ref=src,
            dst_ref=dst,
            send_sem=self.send.at[self.index, k],
            recv_sem=self.recv.at[self.index, k],
            device_id=device,
            device_id_type=MESH,
        )

    def mine(self, first, count):
        return pl.ds(pl.multiple_of(self.place[2][0] * (self.n // 2) + first, 16), count)

    def core_copy(self):
        n, (dp, me, bits) = self.n, self.place
        other = pl.ds(pl.multiple_of((1 - bits[0]) * (n // 2), 16), n // 2)
        return self.remote(self.source.at[other, :], self.r0, 0, (dp + 1 - 2 * bits[0], me))

    def partner(self, axis):
        dp, me, bits = self.place
        return (dp + 2 * axis * (1 - 2 * bits[axis]), me)

    def axes(self, p):
        return (1, 2) if self.parts[p][2] == 0 else (2, 1)

    def lanes(self, p):
        return slice(self.parts[p][0], self.parts[p][1])

    def offset(self, p, depth):
        if depth == 0:
            return 0
        n, (_, me, bits) = self.n, self.place
        one, two = self.axes(p)
        result = bits[one] * (n // 4)
        if depth > 1:
            result = result + bits[two] * (n // 8)
        if depth > 2:
            result = result + me * (n // 32)
        return result

    def halving(self, p, depth):
        n, (_, _, bits) = self.n, self.place
        axis = self.axes(p)[depth - 1]
        size = n // (4 if depth == 1 else 8)
        other = self.offset(p, depth - 1) + (1 - bits[axis]) * size
        buf = self.r1 if depth == 1 else self.r2
        return self.remote(
            self.source.at[self.mine(other, size), self.lanes(p)],
            buf.at[:, self.lanes(p)],
            2 * depth - 1 + p,
            self.partner(axis),
        )

    def quarter(self, p, t):
        n, (dp, me, _) = self.n, self.place
        peer = lax.rem(me + t, 4)
        return self.remote(
            self.source.at[self.mine(self.offset(p, 2) + peer * (n // 32), n // 32), self.lanes(p)],
            self.r3.at[t - 1, :, self.lanes(p)],
            5 + 3 * p + t - 1,
            (dp, peer),
        )

    def final_rows(self, p, depth):
        size = self.n // (2, 4, 8, 32)[depth]
        lanes = slice(None) if p is None else self.lanes(p)
        return self.final.at[self.mine(self.offset(p, depth), size), lanes]

    def keep_copy(self, p):
        return pltpu.make_async_copy(
            self.fin.at[:, self.lanes(p)], self.final_rows(p, 3), self.local.at[2 * self.index + p]
        )

    def spread(self, p, t):
        dp, me, _ = self.place
        return self.remote(
            self.fin.at[:, self.lanes(p)],
            self.final_rows(p, 3),
            11 + 3 * p + t - 1,
            (dp, lax.rem(me + t, 4)),
        )

    def doubling(self, p, depth):
        ref = self.final_rows(p, depth)
        return self.remote(ref, ref, 15 + 2 * (3 - depth) + p, self.partner(self.axes(p)[depth - 1]))

    def core_back(self):
        dp, me, bits = self.place
        ref = self.final_rows(None, 0)
        return self.remote(ref, ref, 21, (dp + 1 - 2 * bits[0], me))

    def add(self, first, buf, count, lanes):
        step = 128 if count % 128 == 0 else count

        def body(i):
            rows = self.mine(first + i * step, step)
            self.source[rows, lanes] = self.source[rows, lanes] + buf[pl.ds(pl.multiple_of(i * step, 16), step), lanes]

        if count == step:
            body(0)
        else:
            loop(count // step, body)

    def stages(self):
        n = self.n
        both = range(len(self.parts))

        def s0():
            self.core_copy().start()

        def s1():
            self.core_copy().wait()
            self.add(0, self.r0, n // 2, slice(None))
            for p in both:
                self.halving(p, 1).start()

        def s2():
            for p in both:
                self.halving(p, 1).wait()
                self.add(self.offset(p, 1), self.r1, n // 4, self.lanes(p))
                self.halving(p, 2).start()

        def s3():
            for p in both:
                self.halving(p, 2).wait()
                self.add(self.offset(p, 2), self.r2, n // 8, self.lanes(p))
                for t in range(1, 4):
                    self.quarter(p, t).start()

        def s4():
            for p in both:
                for t in range(1, 4):
                    self.quarter(p, t).wait()
                lanes = self.lanes(p)
                mine = self.source[self.mine(self.offset(p, 3), n // 32), lanes].astype(f32)
                for t in range(3):
                    mine = mine + self.r3[t, :, lanes].astype(f32)
                self.fin[:, lanes] = mine.astype(bf)
                self.keep_copy(p).start()
                for t in range(1, 4):
                    self.spread(p, t).start()

        def s5():
            for p in both:
                self.keep_copy(p).wait()
                for t in range(1, 4):
                    self.spread(p, t).wait()
                self.doubling(p, 2).start()

        def s6():
            for p in both:
                self.doubling(p, 2).wait()
                self.doubling(p, 1).start()

        def s7():
            for p in both:
                self.doubling(p, 1).wait()
            self.core_back().start()

        def s8():
            self.core_back().wait()

        return [s0, s1, s2, s3, s4, s5, s6, s7, s8]


SEGMENTS = [(FF // 2, D)] * 2 + [(D, FF // 2)] * 2 + [(D, D), (3 * D, D), (D, D)] + [(D, 384)] * PAIRS


def seg_scratch(n, w):
    return [
        pltpu.VMEM((n // 2, w), bf),
        pltpu.VMEM((n // 4, w), bf),
        pltpu.VMEM((n // 8, w), bf),
        pltpu.VMEM((3, n // 32, w), bf),
        pltpu.VMEM((n // 32, w), bf),
    ]


SCHEDULE = {
    0: [("sums", 0), ("sums", 1), ("cross", 1), ("cross", 2), ("cross", 4), ("cross", 7), ("sums", 3), ("first", 1), ("self", 4)],
    1: [("sums", 0), ("sums", 2), ("cross", 3), ("cross", 4), ("cross", 7), ("sums", 4), ("first", 1), ("self", 1), ("self", 5)],
    2: [("sums", 1), ("cross", 1), ("cross", 4), ("cross", 5), ("cross", 7), ("self", 1), ("self", 8), ("input", 1), ("end", 3)],
    3: [("cross", 1), ("cross", 2), ("cross", 5), ("cross", 6), ("sums", 3), ("self", 0), ("self", 3), ("self", 11), ("self", 14)],
    4: [("sums", 2), ("first", 0), ("gso", 0), ("self", 4), ("input", 0), ("end", 5), ("end", 8), ("end", 13), ("end", 15)],
    5: [("sums", 5), ("self", 0), ("self", 6), ("self", 13), ("input", 1), ("end", 9), ("end", 17), ("end", 25), ("end", 31)],
    6: [("sums", 6), ("self", 5), ("self", 14), ("end", 2), ("end", 14), ("end", 22), ("end", 29), ("end", 36), ("end", 38)],
    7: [("self", 4), ("self", 5), ("self", 13), ("self", 15), ("end", 4), ("end", 16), ("end", 21), ("end", 27), ("end", 32)],
    8: [("self", 8), ("self", 9), ("self", 15), ("input", 1), ("end", 12), ("end", 20), ("end", 26), ("end", 33), ("end", 35)],
    9: [("self", 13), ("end", 1), ("end", 7), ("end", 11), ("end", 19), ("end", 24), ("end", 30), ("end", 37), ("end", 40)],
    10: [("end", 0), ("end", 6), ("end", 10), ("end", 18), ("end", 23), ("end", 28), ("end", 34), ("end", 39), ("end", 41)],
}


def layer_kernel(
    tgt_len, src_len, x_in, meml, cot_in, wqkv_in, wso_in, wcq_in, wckv_in, wco_in, win_in, wout_in, gain, bias, omega,
    out, igrad, mgrad, f_out, f_in, f_two, f_so, f_qkv, vout,
    x, cot, wqkv, wso, wcq, wckv, wco, win, wout,
    packed, sh, n1, marks, q8, mem, kv, ch, qfs, kfs, qfc, kfc, dfc, pre2, do,
    act, hg, br3, late, pre1, g3, vec, vbuf, vz,
    *rest,
):
    (load_sem, out_sem, send, recv, local, vsend, vrecv, xsend, xrecv, msend, mrecv) = rest[-11:]
    seg_bufs = rest[:-11]
    slow, br2 = late.at[:L], late.at[L:]
    two, gso = late.at[: 3 * D], late.at[3 * D :]
    me = lax.axis_index("mem")
    dp = lax.axis_index("dp")
    n = 4
    piece = L // n
    bits = (lax.rem(dp, 2), lax.rem(dp // 2, 2), lax.rem(dp // 4, 2))
    place = (dp, me, bits)
    near = [(dp + (1 << a) * (1 - 2 * bits[a]), me) for a in range(3)]
    peers = near + [(dp, lax.rem(me + t, n)) for t in range(1, n)]

    loads = {}
    for i, (name, src, dst) in enumerate(
        [
            ("x", x_in, x), ("wqkv", wqkv_in, wqkv), ("wso", wso_in, wso), ("wcq", wcq_in, wcq), ("wckv", wckv_in, wckv),
            ("wco", wco_in, wco), ("win", win_in, win), ("wout", wout_in, wout), ("cot", cot_in, cot),
        ]
    ):
        loads[name] = pltpu.make_async_copy(src, dst, load_sem.at[i])
        loads[name].start()

    barrier = pltpu.get_barrier_semaphore()
    for peer in peers:
        pl.semaphore_signal(barrier, inc=1, device_id=peer, device_id_type=MESH)
    pl.semaphore_wait(barrier, len(peers))

    def exchange(t):
        peer = lax.rem(me + t, n)
        return pltpu.make_async_remote_copy(
            src_ref=meml.at[peer],
            dst_ref=mem.at[span(me, piece), :],
            send_sem=xsend.at[t],
            recv_sem=xrecv.at[t],
            device_id=(dp, peer),
            device_id_type=MESH,
        )

    own = pltpu.make_async_copy(meml.at[me], mem.at[span(me, piece), :], xsend.at[0])
    for t in range(1, n):
        exchange(t).start()
    own.start()

    whole_parts = ((0, 256, 0), (256, 512, 1))
    wide_parts = ((0, 512, 0), (512, 1024, 1))
    pair_parts = ((0, 128, 0), (128, 384, 1))

    def pieces(w_out, w_in, co, two, so, qkv):
        half = FF // 2
        return [
            w_out.at[:half], w_out.at[half:], w_in.at[:, :half], w_in.at[:, half:], co, two, so,
        ] + [qkv.at[j] for j in range(PAIRS)]

    sources = pieces(wout, win, wco, two, gso, g3)
    finals = pieces(f_out, f_in, f_two.at[:D], f_two.at[D:], f_so, f_qkv)
    ticks = {}
    for i, (rows, width) in enumerate(SEGMENTS):
        parts = {D: whole_parts, FF // 2: wide_parts, 384: pair_parts}[width]
        stages = Segment(i, sources[i], parts, seg_bufs[5 * i : 5 * i + 5], finals[i], (send, recv, local), place).stages()
        for (phase, step), fn in zip(SCHEDULE[i], stages):
            ticks.setdefault(phase, []).append((step, i, fn))

    def at(phase, step, fn):
        ticks.setdefault(phase, []).append((step, -1, fn))

    def run(phase, i, unit=1, part=0):
        todo = {}
        for step, order, fn in ticks.get(phase, []):
            if step % unit == part:
                todo.setdefault(step // unit, []).append((order, fn))
        for step, fns in sorted(todo.items()):

            def stage(fns=fns):
                for _, fn in sorted(fns, key=lambda item: item[0]):
                    fn()

            if not isinstance(i, int):
                pl.when(i == step)(stage)
            elif i == step:
                stage()

    lane = lane_of()
    lengths = [jnp.zeros((1, 128), jnp.int32)] * 2
    for s in range(16):
        lengths[0] = jnp.where(lane == s, tgt_len[0, s], lengths[0])
        lengths[1] = jnp.where(lane == s, src_len[me, s], lengths[1])
    is_doc = jnp.where(src_len[me, 0] > SHORT, 1, 0)

    def features(i):
        rows = span(i, TB)
        feats, one_hot, inside = key_features(lengths[0], is_doc, TB, i * TB)
        kfs[rows, :] = feats
        qfs[rows, :] = one_hot
        qfc[rows, :] = one_hot
        marks[rows, :] = jnp.broadcast_to(jnp.sum(inside, axis=1, keepdims=True), (TB, 128))
        feats, _, _ = key_features(lengths[1], is_doc, TB, i * TB)
        kfc[rows, :] = feats

    loop(L // TB, features)
    loads["x"].wait()
    loads["wqkv"].wait()

    packed[:, :D] = dot(x[...], wqkv[:, :D]).astype(bf) * bf(SCALE)
    packed[:, D:] = dot(x[...], wqkv[:, D:]).astype(bf)

    causal = lax.broadcasted_iota(jnp.int32, (SELF_BQ, SELF_BQ), 0) >= lax.broadcasted_iota(
        jnp.int32, (SELF_BQ, SELF_BQ), 1
    )

    def lanes_at(first, j):
        return pl.ds(pl.multiple_of(first + j * 128, 128), 128)

    for b in range(L // SELF_BQ):
        low, high = b * SELF_BQ, (b + 1) * SELF_BQ

        def self_pair(j, low=low, high=high):
            def section(first, last, mask):
                keys = jnp.concatenate([packed[first:last, lanes_at(D, j)], kfs[first:last, :]], axis=1)
                values = packed[first:last, lanes_at(2 * D, j)]
                return keys, jnp.concatenate([values, jnp.ones((last - first, 128), bf)], axis=1), mask

            sections = [section(low, high, causal)]
            if low:
                sections.append(section(0, low, None))
            sh[low:high, span(j, 128)] = softmax_pair(
                j, packed[low:high, span(j, 128)], sections, qfs, slice(low, high)
            )

        loop(PAIRS, self_pair)

    loads["wso"].wait()
    loads["wcq"].wait()

    def first_norm(i):
        rows = slice(i * TB, (i + 1) * TB)
        branch = dot(sh[rows, :], wso[...])
        yield
        normed, scaler = norm(omega[0:1, :] * x[rows, :].astype(f32) + branch)
        n1[rows, :] = normed
        marks[rows, :] = jnp.where(half_lanes(), marks[rows, :], scaler)
        first = (normed * gain[0:1, :] + bias[0:1, :]).astype(bf)
        yield
        q8[rows, :] = dot(first, wcq[...]).astype(bf) * bf(SCALE)

    weave(first_norm(i) for i in range(L // TB))

    own.wait()
    for t in range(1, n):
        exchange(t).wait()
    loads["wckv"].wait()

    kv[...] = dot(mem[...], wckv[...]).astype(bf)

    def cross_pair(i):
        j = i // (L // CROSS_BQ)
        rows = span(lax.rem(i, L // CROSS_BQ), CROSS_BQ)
        keys = jnp.concatenate([kv[:, span(j, 128)], kfc[...]], axis=1)
        values = jnp.concatenate([kv[:, lanes_at(D, j)], jnp.ones((L, 128), bf)], axis=1)
        ch[rows, span(j, 128)] = softmax_pair(j, q8[rows, span(j, 128)], [(keys, values, None)], qfc, rows)

    loop(PAIRS * (L // CROSS_BQ), cross_pair)

    vec[...] = jnp.zeros_like(vec)
    for name in ("wco", "win", "wout", "cot"):
        loads[name].wait()

    def tokens(i):
        rows = slice(i * TB, (i + 1) * TB)
        branch = dot(ch[rows, :], wco[...])
        yield
        n2, r2 = norm(omega[1:2, :] * (n1[rows, :] * gain[0:1, :] + bias[0:1, :]) + branch)
        pre2[rows, :] = n2
        second_low = (n2 * gain[1:2, :] + bias[1:2, :]).astype(bf)
        slow[rows, :] = second_low
        yield
        for c in range(FF // WIDE):
            cols = slice(c * WIDE, (c + 1) * WIDE)
            h = dot(second_low, win[:, cols])
            yield
            square = h * h
            cdf = 0.5 + 0.5 * jnp.tanh(h * (GELU_C + (GELU_C * GELU_A) * square))
            value = h * cdf
            act[rows, cols] = value.astype(bf)
            slope = cdf + value * (1.0 - cdf) * (2.0 * GELU_C + (6.0 * GELU_C * GELU_A) * square)
            hg[rows, cols] = slope.astype(bf)
            yield
        branch = dot(act[rows, :], wout[...])
        yield
        second = pre2[rows, :] * gain[1:2, :] + bias[1:2, :]
        n3, r3 = norm(omega[2:3, :] * second + branch)
        third = n3 * gain[2:3, :] + bias[2:3, :]
        kept = marks[rows, :][:, 0:1]
        up = cot[rows, :].astype(f32) * kept
        cot[rows, :] = (third * kept).astype(bf)
        pre3 = norm_back(up, n3, r3, gain[2:3, :])
        vec[2:3, :] += total(up * n3)
        vec[5:6, :] += total(up)
        vec[8:9, :] += total(pre3 * second)
        low3 = pre3.astype(bf)
        br3[rows, :] = low3
        grad = omega[2:3, :] * pre3
        yield
        for c in range(FF // WIDE):
            cols = slice(c * WIDE, (c + 1) * WIDE)
            back = dot(low3, wout[cols, :], NT)
            yield
            hg[rows, cols] = (back * hg[rows, cols].astype(f32)).astype(bf)
            yield
        branch = dot(hg[rows, :], win[...], NT)
        yield
        grad = grad + branch
        n2 = pre2[rows, :]
        back2 = norm_back(grad, n2, r2, gain[1:2, :])
        vec[1:2, :] += total(grad * n2)
        vec[4:5, :] += total(grad)
        vec[7:8, :] += total(back2 * (n1[rows, :] * gain[0:1, :] + bias[0:1, :]))
        pre2[rows, :] = back2
        low2 = back2.astype(bf)
        br2[rows, :] = low2
        yield
        dlow = dot(low2, wco[...], NT).astype(bf)
        do[rows, :] = dlow
        yield
        dfc[rows, :] = delta_features(dlow.astype(f32) * ch[rows, :].astype(f32))

    weave(tokens(i) for i in range(L // TB))
    out_copy = pltpu.make_async_copy(cot, out, out_sem.at[0])
    out_copy.start()

    wout[...] = dot(act[...], br3[...], TN).astype(bf)
    run("sums", 0)
    win[...] = dot(slow[...], hg[...], TN).astype(bf)
    run("sums", 1)
    wco[...] = dot(ch[...], br2[...], TN).astype(bf)
    run("sums", 2)

    kvg, qg, fl = hg.at[:, : 2 * D], hg.at[:, 2 * D : 3 * D], hg.at[:, 3 * D :]
    pg, mgs = act.at[:, : 3 * D], act.at[:, 3 * D :]
    br1 = br3
    blocks = L // CROSS_BK

    def cross_back(i):
        run("cross", i)
        j = i // blocks
        b = lax.rem(i, blocks)
        rows = span(b, CROSS_BK)
        lanes = span(j, 128)
        dk, dv, dq = back_tile(
            j, kv[rows, lanes], kv[rows, lanes_at(D, j)], kfc[rows, :], q8[:, lanes], qfc[...], do[:, lanes], dfc[...], None
        )
        kvg[rows, lanes] = dk.astype(bf)
        kvg[rows, lanes_at(D, j)] = dv.astype(bf)

        @pl.when(b == 0)
        def _():
            pre1[:, lanes] = dq

        @pl.when(b > 0)
        def _():
            pre1[:, lanes] += dq

    loop(PAIRS * blocks, cross_back)

    run("sums", 3)
    fl[...] = (n1[...] * gain[0:1, :] + bias[0:1, :]).astype(bf)
    qg[...] = (pre1[...] * SCALE).astype(bf)
    mgs[...] = dot(kvg[...], wckv[...], NT).astype(bf)

    def memory_back(t):
        peer = lax.rem(me + t, n)
        return pltpu.make_async_remote_copy(
            src_ref=mgs.at[span(peer, piece), :],
            dst_ref=mgrad.at[me],
            send_sem=msend.at[t],
            recv_sem=mrecv.at[t],
            device_id=(dp, peer),
            device_id_type=MESH,
        )

    memory_own = pltpu.make_async_copy(mgs.at[span(me, piece), :], mgrad.at[me], msend.at[0])
    memory_own.start()
    for t in range(1, n):
        memory_back(t).start()

    run("sums", 4)
    two[:D, :] = dot(fl[...], qg[...], TN).astype(bf)
    two[D : 2 * D, :] = dot(mem[...], kvg[:, :D], TN).astype(bf)
    two[2 * D :, :] = dot(mem[...], kvg[:, D:], TN).astype(bf)
    run("sums", 5)

    def first_back(i):
        run("first", i)
        rows = slice(i * TB, (i + 1) * TB)
        branch = dot(qg[rows, :], wcq[...], NT)
        yield
        normed = n1[rows, :]
        grad = omega[1:2, :] * pre2[rows, :] + branch
        back1 = norm_back(grad, normed, marks[rows, :][:, 64:65], gain[0:1, :])
        vec[0:1, :] += total(grad * normed)
        vec[3:4, :] += total(grad)
        vec[6:7, :] += total(back1 * x[rows, :].astype(f32))
        pre1[rows, :] = back1
        low1 = back1.astype(bf)
        br1[rows, :] = low1
        yield
        dlow = dot(low1, wso[...], NT).astype(bf)
        do[rows, :] = dlow
        yield
        dfc[rows, :] = delta_features(dlow.astype(f32) * sh[rows, :].astype(f32))

    weave(first_back(i) for i in range(L // TB))

    run("gso", 0)
    gso[...] = dot(sh[...], br1[...], TN).astype(bf)
    run("sums", 6)

    def vec_near(a):
        return pltpu.make_async_remote_copy(
            src_ref=vec.at[pl.ds(16 * a, 16), :],
            dst_ref=vbuf.at[a],
            send_sem=vsend.at[a],
            recv_sem=vrecv.at[a],
            device_id=near[a],
            device_id_type=MESH,
        )

    def vec_far(t):
        return pltpu.make_async_remote_copy(
            src_ref=vec.at[pl.ds(48, 16), :],
            dst_ref=vz.at[me],
            send_sem=vsend.at[2 + t],
            recv_sem=vrecv.at[2 + t],
            device_id=(dp, lax.rem(me + t, n)),
            device_id_type=MESH,
        )

    def vec_next(a):
        vec_near(a).wait()
        vec[16 * (a + 1) : 16 * (a + 2), :] = vec[16 * a : 16 * (a + 1), :] + vbuf[a]
        if a < 2:
            vec_near(a + 1).start()
        else:
            for t in range(1, n):
                vec_far(t).start()

    def vec_last():
        for t in range(1, n):
            vec_far(t).wait()
        vz[me] = vec[48:64, :]
        vout[...] = (vz[0] + vz[1]) + (vz[2] + vz[3])

    vec_near(0).start()
    at("self", 3, lambda: vec_next(0))
    at("self", 7, lambda: vec_next(1))
    at("self", 12, lambda: vec_next(2))
    at("end", 4, vec_last)

    below = lax.broadcasted_iota(jnp.int32, (SELF_BK, SELF_BK), 1) >= lax.broadcasted_iota(
        jnp.int32, (SELF_BK, SELF_BK), 0
    )
    parts = L // SELF_BK

    def self_back(j):
        dqs = []
        for b in range(parts):
            run("self", j, parts, b)
            low, high = b * SELF_BK, (b + 1) * SELF_BK
            dk, dv, dq = back_tile(
                j,
                packed[low:high, lanes_at(D, j)],
                packed[low:high, lanes_at(2 * D, j)],
                kfs[low:high, :],
                packed[low:, span(j, 128)],
                qfs[low:, :],
                do[low:, span(j, 128)],
                dfc[low:, :],
                below,
            )
            pg[low:high, lanes_at(D, j)] = dk.astype(bf)
            pg[low:high, lanes_at(2 * D, j)] = dv.astype(bf)
            for i in range(b, parts):
                share = dq[(i - b) * SELF_BK : (i - b + 1) * SELF_BK, :]
                if b == 0:
                    dqs.append(share)
                else:
                    dqs[i] = dqs[i] + share
        for i, share in enumerate(dqs):
            pg[i * SELF_BK : (i + 1) * SELF_BK, span(j, 128)] = (share * SCALE).astype(bf)
        both = jnp.concatenate([pg[:, lanes_at(c * D, j)] for c in range(3)], axis=1)
        g3[j] = dot(x[...], both, TN).astype(bf)

    loop(PAIRS, self_back)

    def igrad_copy(i):
        return pltpu.make_async_copy(pre1.at[span(i, TB), :], igrad.at[span(i, TB), :], out_sem.at[1 + i])

    def input_back(i):
        run("input", i)
        rows = span(i, TB)
        pre1[rows, :] = omega[0:1, :] * pre1[rows, :] + dot(pg[rows, :], wqkv[...], NT)
        igrad_copy(i).start()

    loop(L // TB, input_back)
    for _, _, fn in sorted(ticks["end"], key=lambda item: item[:2]):
        fn()
    out_copy.wait()
    memory_own.wait()
    for t in range(1, n):
        memory_back(t).wait()
    for i in range(L // TB):
        igrad_copy(i).wait()


CASTS = (
    [(0, (slice(i * D, (i + 1) * D), slice(0, D)), 0, (slice(i * D, (i + 1) * D), slice(0, D))) for i in range(4)]
    + [(1, (slice(0, D), slice(i * D, (i + 1) * D)), 1, (slice(0, D), slice(i * D, (i + 1) * D))) for i in range(4)]
    + [
        (2, (slice(0, D), slice(0, D)), 2, (slice(0, D), slice(0, D))),
        (2, (slice(D, 2 * D), slice(0, D)), 3, (slice(0, D), slice(0, D))),
        (2, (slice(2 * D, 3 * D), slice(0, D)), 4, (slice(0, D), slice(0, D))),
        (2, (slice(3 * D, 4 * D), slice(0, D)), 4, (slice(0, D), slice(D, 2 * D))),
        (3, (slice(0, D), slice(0, D)), 5, (slice(0, D), slice(0, D))),
    ]
)


def cast_kernel(
    out_in, igrad_in, mgrad_in, f_out, f_in, f_two, f_so, f_qkv,
    out, igrad, mgrad, g_out, g_in, g_co, g_cq, g_ckv, g_so, g_qkv,
    narrow, wide, qkv_narrow, qkv_wide, out_held, igrad_held, sems, out_sems,
):
    passed = [(out_in, out_held, out), (igrad_in, igrad_held, igrad)]
    whole_in = [pltpu.make_async_copy(src, held, sems.at[i]) for i, (src, held, _) in enumerate(passed)]
    froms = (f_out, f_in, f_two, f_so)
    tos = (g_out, g_in, g_co, g_cq, g_ckv, g_so)
    pieces = []
    for source, window, target, place in CASTS:
        pieces.append((froms[source].at[window], tos[target].at[place]))
    for i in range(2):
        pieces.append((mgrad_in.at[pl.ds(i * D, D), :], mgrad.at[pl.ds(i * D, D), :]))
    ins = [pltpu.make_async_copy(src, narrow.at[i], sems.at[2 + i]) for i, (src, _) in enumerate(pieces)]
    outs = [pltpu.make_async_copy(wide.at[i], dst, out_sems.at[i]) for i, (_, dst) in enumerate(pieces)]
    qkv_in = pltpu.make_async_copy(f_qkv, qkv_narrow, sems.at[2 + len(pieces)])
    qkv_out = pltpu.make_async_copy(qkv_wide, g_qkv, out_sems.at[len(pieces)])
    for copy in ins:
        copy.start()
    qkv_in.start()
    whole_out = [
        pltpu.make_async_copy(held, dst, out_sems.at[len(pieces) + 1 + i]) for i, (_, held, dst) in enumerate(passed)
    ]
    for copy in whole_in:
        copy.start()
    for i, copy in enumerate(ins):
        copy.wait()

        def body(r, i=i):
            wide[i, span(r, 64), :] = narrow[i, span(r, 64), :].astype(f32)

        loop(D // 64, body)
        outs[i].start()
    qkv_in.wait()

    def body(r):
        for j in range(PAIRS):
            for c in range(3):
                qkv_wide[span(r, 64), c * D + j * 128 : c * D + (j + 1) * 128] = qkv_narrow[
                    j, span(r, 64), c * 128 : (c + 1) * 128
                ].astype(f32)

    loop(D // 64, body)
    qkv_out.start()
    for copy_in, copy_out in zip(whole_in, whole_out):
        copy_in.wait()
        copy_out.start()
    for copy in whole_out + outs:
        copy.wait()
    qkv_out.wait()


VM = pl.BlockSpec(memory_space=pltpu.VMEM)
SM = pl.BlockSpec(memory_space=pltpu.SMEM)
ANY = pl.BlockSpec(memory_space=pl.ANY)


def per_device(
    inputs, memory, cotangent, tgt_len, src_len,
    self_qkv, self_out, cross_query, cross_kv, cross_out, ffn_in, ffn_out, ln_gain, ln_bias, omega_scale, dp,
):
    shape = jax.ShapeDtypeStruct
    scratch = [
        pltpu.VMEM((L, D), bf),
        pltpu.VMEM((L, D), bf),
        pltpu.VMEM((D, 3 * D), bf),
        pltpu.VMEM((D, D), bf),
        pltpu.VMEM((D, D), bf),
        pltpu.VMEM((D, 2 * D), bf),
        pltpu.VMEM((D, D), bf),
        pltpu.VMEM((D, FF), bf),
        pltpu.VMEM((FF, D), bf),
        pltpu.VMEM((L, 3 * D), bf),
        pltpu.VMEM((L, D), bf),
        pltpu.VMEM((L, D), f32),
        pltpu.VMEM((L, 128), f32),
        pltpu.VMEM((L, D), bf),
        pltpu.VMEM((L, D), bf),
        pltpu.VMEM((L, 2 * D), bf),
        pltpu.VMEM((L, D), bf),
        pltpu.VMEM((L, 128), bf),
        pltpu.VMEM((L, 128), bf),
        pltpu.VMEM((L, 128), bf),
        pltpu.VMEM((L, 128), bf),
        pltpu.VMEM((L, 128), bf),
        pltpu.VMEM((L, D), f32),
        pltpu.VMEM((L, D), bf),
        pltpu.VMEM((L, FF), bf),
        pltpu.VMEM((L, FF), bf),
        pltpu.VMEM((L, D), bf),
        pltpu.VMEM((2 * L, D), bf),
        pltpu.VMEM((L, D), f32),
        pltpu.VMEM((PAIRS, D, 384), bf),
        pltpu.VMEM((64, D), f32),
        pltpu.VMEM((3, 16, D), f32),
        pltpu.VMEM((4, 16, D), f32),
    ]
    for n, w in SEGMENTS:
        scratch += seg_scratch(n, w)
    count = len(SEGMENTS)
    sem = pltpu.SemaphoreType.DMA
    scratch += [
        sem((9,)), sem((5,)), sem((count, 22)), sem((count, 22)), sem((2 * count,)), sem((6,)), sem((6,)),
        sem((4,)), sem((4,)), sem((4,)), sem((4,)),
    ]
    results = pl.pallas_call(
        layer_kernel,
        out_shape=[
            shape((L, D), bf),
            shape((L, D), f32),
            shape((4, L // 4, D), bf),
            shape((FF, D), bf),
            shape((D, FF), bf),
            shape((4 * D, D), bf),
            shape((D, D), bf),
            shape((PAIRS, D, 384), bf),
            shape((16, D), f32),
        ],
        in_specs=[SM] * 2 + [ANY] * 10 + [VM] * 3,
        out_specs=[ANY] * 8 + [VM],
        scratch_shapes=scratch,
        compiler_params=pltpu.CompilerParams(collective_id=0, has_side_effects=True, vmem_limit_bytes=(64 << 20) - (128 << 10)),
        name="layer",
    )(
        tgt_len, src_len, inputs.reshape(L, D), memory, cotangent.reshape(L, D), self_qkv, self_out, cross_query, cross_kv,
        cross_out, ffn_in, ffn_out, ln_gain, ln_bias, omega_scale,
    )
    output, igrad, mgrad, grads, small = results[0], results[1], results[2], results[3:8], results[8]

    blocks = dp // 8
    if blocks > 1:
        groups = [[i + 8 * b for b in range(blocks)] for i in range(8)]
        *grads, small = lax.psum((*grads, small), "dp", axis_index_groups=groups)

    pieces = len(CASTS) + 2
    output, igrad, mgrad, g_out, g_in, g_co, g_cq, g_ckv, g_so, g_qkv = pl.pallas_call(
        cast_kernel,
        out_shape=[
            shape((L, D), bf),
            shape((L, D), f32),
            shape((L, D), f32),
            shape((FF, D), f32),
            shape((D, FF), f32),
            shape((D, D), f32),
            shape((D, D), f32),
            shape((D, 2 * D), f32),
            shape((D, D), f32),
            shape((D, 3 * D), f32),
        ],
        in_specs=[ANY] * 8,
        out_specs=[ANY] * 10,
        scratch_shapes=[
            pltpu.VMEM((pieces, D, D), bf),
            pltpu.VMEM((pieces, D, D), f32),
            pltpu.VMEM((PAIRS, D, 384), bf),
            pltpu.VMEM((D, 3 * D), f32),
            pltpu.VMEM((L, D), bf),
            pltpu.VMEM((L, D), f32),
            sem((pieces + 3,)),
            sem((pieces + 3,)),
        ],
        compiler_params=pltpu.CompilerParams(vmem_limit_bytes=62 << 20),
        name="casts",
    )(output, igrad, mgrad.reshape(L, D), *grads)
    return (
        output.reshape(1, L, D),
        igrad.reshape(1, L, D),
        mgrad.reshape(4, L // 4, D),
        g_qkv,
        g_so,
        g_cq,
        g_ckv,
        g_co,
        g_in,
        g_out,
        small[0:3],
        small[3:6],
        small[6:9],
    )


def solution(mesh):
    rows = P(("dp", "mem"), None, None)
    return jax.shard_map(
        functools.partial(per_device, dp=mesh.shape["dp"]),
        mesh=mesh,
        in_specs=(rows, P("dp", "mem", None), rows, P(("dp", "mem"), None), P("dp", None)) + (P(),) * 10,
        out_specs=(rows, rows, P("dp", "mem", None)) + (P(),) * 10,
        check_vma=False,
    )
```

```python
import functools

import jax
import jax.numpy as jnp
from jax import lax
from jax.experimental import pallas as pl
from jax.experimental.pallas import tpu as pltpu
from jax.sharding import PartitionSpec as P

f32 = jnp.float32
bf = jnp.bfloat16
MESH = pl.DeviceIdType.MESH
NN = (((1,), (0,)), ((), ()))
NT = (((1,), (1,)), ((), ()))
TN = (((0,), (0,)), ((), ()))

L = 1024
D = 512
FF = 2048
HEADS = 8
PAIRS = HEADS // 2
SHORT = 64
SCALE = 0.125
NEG = -1e30
EPS = 1e-05
GELU_C = 0.7978845608028654
GELU_A = 0.044715


def dot(a, b, dims=NN):
    return lax.dot_general(a, b, dims, preferred_element_type=f32)


def span(i, n):
    return pl.ds(pl.multiple_of(i * n, n), n)


def loop(n, body):
    def step(i, carry):
        body(i)
        return carry

    lax.fori_loop(0, n, step, 0)


def weave(parts):
    parts = list(parts)
    live = set(range(len(parts)))
    turn = 0
    while live:
        for k in sorted(live):
            if turn >= k and next(parts[k], "done") == "done":
                live.discard(k)
        turn += 1


def half_lanes():
    return lax.broadcasted_iota(jnp.int32, (1, 128), 1) < 64


def norm(values):
    centred = values - jnp.mean(values, axis=-1, keepdims=True)
    scaler = lax.rsqrt(jnp.mean(centred * centred, axis=-1, keepdims=True) + EPS)
    return centred * scaler, scaler


def norm_back(upstream, normed, scaler, gain_row):
    scaled = upstream * gain_row
    centred = scaled - jnp.mean(scaled, axis=-1, keepdims=True)
    centred = centred - normed * jnp.mean(scaled * normed, axis=-1, keepdims=True)
    return centred * scaler


def total(values):
    return jnp.sum(values, axis=0, keepdims=True)


def lane_of():
    return lax.broadcasted_iota(jnp.int32, (1, 128), 1)


def put_parts(values, head, old):
    at = lane_of() - (16 + 3 * head)
    high = values.astype(bf).astype(f32)
    rest = values - high
    middle = rest.astype(bf).astype(f32)
    low = rest - middle
    return jnp.where(at == 0, high, jnp.where(at == 1, middle, jnp.where(at == 2, low, old)))


def head_keys(feats, head):
    at = lane_of() - (16 + 3 * head)
    return jnp.where((at >= 0) & (at < 3), jnp.ones_like(feats), feats)


def key_features(lengths, is_doc, rows, first):
    pos = first + lax.broadcasted_iota(jnp.int32, (rows, 128), 0)
    lane = lax.broadcasted_iota(jnp.int32, (rows, 128), 1)
    seg = (pos >> 6) * (1 - is_doc)
    inside = (seg == lane) & (pos - seg * SHORT < lengths)
    feats = jnp.where(lane < 16, jnp.where(inside, 0.0, NEG), 0.0)
    hot = jnp.where(seg == lane, 1.0, 0.0)
    return feats.astype(bf), hot.astype(bf), jnp.where(inside, 1.0, 0.0)


def softmax_pair(j, qp, sections, lse_ref, rows):
    half = half_lanes()
    mixed = []
    base = lse_ref[rows, :]
    feats = base.astype(f32)
    scores = []
    for e in range(2):
        sel = half if e == 0 else jnp.logical_not(half)
        qa = jnp.concatenate([jnp.where(sel, qp, jnp.zeros_like(qp)), base], axis=1)
        scores.append([dot(qa, keys, NT) for keys, _, _ in sections])
    for e in range(2):
        masked = [s if mask is None else jnp.where(mask, s, NEG) for s, (_, _, mask) in zip(scores[e], sections)]
        largest = functools.reduce(jnp.maximum, [jnp.max(s, axis=1, keepdims=True) for s in masked])
        acc = None
        for s, (_, values, _) in zip(masked, sections):
            o = dot(jnp.exp(s - largest).astype(bf), values)
            acc = o if acc is None else acc + o
        summed = acc[:, 128:]
        feats = put_parts(-(largest + jnp.log(summed)), 2 * j + e, feats)
        mixed.append(acc[:, :128] / summed)
    lse_ref[rows, :] = feats.astype(bf)
    return jnp.where(half, mixed[0], mixed[1]).astype(bf)


def back_tile(j, k_rows, v_rows, kfeat, qp, qfeat, gp, gfeat, mask):
    half = half_lanes()
    dk, dv, dq = [], [], []
    scores, slopes = [], []
    for e in range(2):
        sel = half if e == 0 else jnp.logical_not(half)
        kf = head_keys(kfeat, 2 * j + e)
        qa = jnp.concatenate([jnp.where(sel, qp, jnp.zeros_like(qp)), qfeat], axis=1)
        ga = jnp.concatenate([jnp.where(sel, gp, jnp.zeros_like(gp)), gfeat], axis=1)
        scores.append(dot(jnp.concatenate([k_rows, kf], axis=1), qa, NT))
        slopes.append(dot(jnp.concatenate([v_rows, kf], axis=1), ga, NT))
    for e in range(2):
        probs = jnp.exp(scores[e])
        if mask is not None:
            width = mask.shape[1]
            first = jnp.where(mask, probs[:, :width], 0.0)
            probs = first if probs.shape[1] == width else jnp.concatenate([first, probs[:, width:]], axis=1)
        ds = (probs * slopes[e]).astype(bf)
        dv.append(dot(probs.astype(bf), gp))
        dk.append(dot(ds, qp))
        dq.append(dot(ds, k_rows, TN))
    return (
        jnp.where(half, dk[0], dk[1]),
        jnp.where(half, dv[0], dv[1]),
        jnp.where(half, dq[0], dq[1]),
    )


def delta_features(product):
    half = half_lanes()
    feats = jnp.zeros((product.shape[0], 128), f32)
    for j in range(PAIRS):
        part = product[:, 128 * j : 128 * (j + 1)]
        for e in range(2):
            sel = half if e == 0 else jnp.logical_not(half)
            delta = jnp.sum(jnp.where(sel, part, 0.0), axis=1, keepdims=True)
            feats = put_parts(-delta, 2 * j + e, feats)
    return feats.astype(bf)


SELF_BQ = 512
SELF_BK = 256
CROSS_BQ = 512
CROSS_BK = 512
TB = 512
WIDE = 1024


class Segment:
    def __init__(self, index, source, parts, bufs, final, sems, place):
        self.index, self.source, self.parts = index, source, parts
        self.n = source.shape[0]
        (self.r0, self.r1, self.r2, self.r3, self.fin) = bufs
        self.final = final
        self.send, self.recv, self.local = sems
        self.place = place

    def remote(self, src, dst, k, device):
        return pltpu.make_async_remote_copy(
            src_ref=src,
            dst_ref=dst,
            send_sem=self.send.at[self.index, k],
            recv_sem=self.recv.at[self.index, k],
            device_id=device,
            device_id_type=MESH,
        )

    def mine(self, first, count):
        return pl.ds(pl.multiple_of(self.place[2][0] * (self.n // 2) + first, 16), count)

    def core_copy(self):
        n, (dp, me, bits) = self.n, self.place
        other = pl.ds(pl.multiple_of((1 - bits[0]) * (n // 2), 16), n // 2)
        return self.remote(self.source.at[other, :], self.r0, 0, (dp + 1 - 2 * bits[0], me))

    def partner(self, axis):
        dp, me, bits = self.place
        return (dp + 2 * axis * (1 - 2 * bits[axis]), me)

    def axes(self, p):
        return (1, 2) if self.parts[p][2] == 0 else (2, 1)

    def lanes(self, p):
        return slice(self.parts[p][0], self.parts[p][1])

    def offset(self, p, depth):
        if depth == 0:
            return 0
        n, (_, me, bits) = self.n, self.place
        one, two = self.axes(p)
        result = bits[one] * (n // 4)
        if depth > 1:
            result = result + bits[two] * (n // 8)
        if depth > 2:
            result = result + me * (n // 32)
        return result

    def halving(self, p, depth):
        n, (_, _, bits) = self.n, self.place
        axis = self.axes(p)[depth - 1]
        size = n // (4 if depth == 1 else 8)
        other = self.offset(p, depth - 1) + (1 - bits[axis]) * size
        buf = self.r1 if depth == 1 else self.r2
        return self.remote(
            self.source.at[self.mine(other, size), self.lanes(p)],
            buf.at[:, self.lanes(p)],
            2 * depth - 1 + p,
            self.partner(axis),
        )

    def quarter(self, p, t):
        n, (dp, me, _) = self.n, self.place
        peer = lax.rem(me + t, 4)
        return self.remote(
            self.source.at[self.mine(self.offset(p, 2) + peer * (n // 32), n // 32), self.lanes(p)],
            self.r3.at[t - 1, :, self.lanes(p)],
            5 + 3 * p + t - 1,
            (dp, peer),
        )

    def final_rows(self, p, depth):
        size = self.n // (2, 4, 8, 32)[depth]
        lanes = slice(None) if p is None else self.lanes(p)
        return self.final.at[self.mine(self.offset(p, depth), size), lanes]

    def keep_copy(self, p):
        return pltpu.make_async_copy(
            self.fin.at[:, self.lanes(p)], self.final_rows(p, 3), self.local.at[2 * self.index + p]
        )

    def spread(self, p, t):
        dp, me, _ = self.place
        return self.remote(
            self.fin.at[:, self.lanes(p)],
            self.final_rows(p, 3),
            11 + 3 * p + t - 1,
            (dp, lax.rem(me + t, 4)),
        )

    def doubling(self, p, depth):
        ref = self.final_rows(p, depth)
        return self.remote(ref, ref, 15 + 2 * (3 - depth) + p, self.partner(self.axes(p)[depth - 1]))

    def core_back(self):
        dp, me, bits = self.place
        ref = self.final_rows(None, 0)
        return self.remote(ref, ref, 21, (dp + 1 - 2 * bits[0], me))

    def add(self, first, buf, count, lanes):
        step = 128 if count % 128 == 0 else count

        def body(i):
            rows = self.mine(first + i * step, step)
            self.source[rows, lanes] = self.source[rows, lanes] + buf[pl.ds(pl.multiple_of(i * step, 16), step), lanes]

        if count == step:
            body(0)
        else:
            loop(count // step, body)

    def stages(self):
        n = self.n
        both = range(len(self.parts))

        def s0():
            self.core_copy().start()

        def s1():
            self.core_copy().wait()
            self.add(0, self.r0, n // 2, slice(None))
            for p in both:
                self.halving(p, 1).start()

        def s2():
            for p in both:
                self.halving(p, 1).wait()
                self.add(self.offset(p, 1), self.r1, n // 4, self.lanes(p))
                self.halving(p, 2).start()

        def s3():
            for p in both:
                self.halving(p, 2).wait()
                self.add(self.offset(p, 2), self.r2, n // 8, self.lanes(p))
                for t in range(1, 4):
                    self.quarter(p, t).start()

        def s4():
            for p in both:
                for t in range(1, 4):
                    self.quarter(p, t).wait()
                lanes = self.lanes(p)
                mine = self.source[self.mine(self.offset(p, 3), n // 32), lanes].astype(f32)
                for t in range(3):
                    mine = mine + self.r3[t, :, lanes].astype(f32)
                self.fin[:, lanes] = mine.astype(bf)
                self.keep_copy(p).start()
                for t in range(1, 4):
                    self.spread(p, t).start()

        def s5():
            for p in both:
                self.keep_copy(p).wait()
                for t in range(1, 4):
                    self.spread(p, t).wait()
                self.doubling(p, 2).start()

        def s6():
            for p in both:
                self.doubling(p, 2).wait()
                self.doubling(p, 1).start()

        def s7():
            for p in both:
                self.doubling(p, 1).wait()
            self.core_back().start()

        def s8():
            self.core_back().wait()

        return [s0, s1, s2, s3, s4, s5, s6, s7, s8]


SEGMENTS = [(FF // 2, D)] * 2 + [(D, FF // 2)] * 2 + [(D, D), (3 * D, D), (D, D)] + [(D, 384)] * PAIRS


def seg_scratch(n, w):
    return [
        pltpu.VMEM((n // 2, w), bf),
        pltpu.VMEM((n // 4, w), bf),
        pltpu.VMEM((n // 8, w), bf),
        pltpu.VMEM((3, n // 32, w), bf),
        pltpu.VMEM((n // 32, w), bf),
    ]


SCHEDULE = {
    0: [("sums", 0), ("sums", 1), ("cross", 1), ("cross", 2), ("cross", 4), ("cross", 7), ("sums", 3), ("first", 1), ("self", 4)],
    1: [("sums", 0), ("sums", 2), ("cross", 3), ("cross", 4), ("cross", 7), ("sums", 4), ("first", 1), ("self", 1), ("self", 5)],
    2: [("sums", 1), ("cross", 1), ("cross", 4), ("cross", 5), ("cross", 7), ("self", 1), ("self", 8), ("input", 1), ("end", 3)],
    3: [("cross", 1), ("cross", 2), ("cross", 5), ("cross", 6), ("sums", 3), ("self", 0), ("self", 3), ("self", 11), ("self", 14)],
    4: [("sums", 2), ("first", 0), ("gso", 0), ("self", 4), ("input", 0), ("end", 5), ("end", 8), ("end", 13), ("end", 15)],
    5: [("sums", 5), ("self", 0), ("self", 6), ("self", 13), ("input", 1), ("end", 9), ("end", 17), ("end", 25), ("end", 31)],
    6: [("sums", 6), ("self", 5), ("self", 14), ("end", 2), ("end", 14), ("end", 22), ("end", 29), ("end", 36), ("end", 38)],
    7: [("self", 4), ("self", 5), ("self", 13), ("self", 15), ("end", 4), ("end", 16), ("end", 21), ("end", 27), ("end", 32)],
    8: [("self", 8), ("self", 9), ("self", 15), ("input", 1), ("end", 12), ("end", 20), ("end", 26), ("end", 33), ("end", 35)],
    9: [("self", 13), ("end", 1), ("end", 7), ("end", 11), ("end", 19), ("end", 24), ("end", 30), ("end", 37), ("end", 40)],
    10: [("end", 0), ("end", 6), ("end", 10), ("end", 18), ("end", 23), ("end", 28), ("end", 34), ("end", 39), ("end", 41)],
}


def layer_kernel(
    tgt_len, src_len, x_in, meml, cot_in, wqkv_in, wso_in, wcq_in, wckv_in, wco_in, win_in, wout_in, gain, bias, omega,
    out, igrad, mgrad, f_out, f_in, f_two, f_so, f_qkv, vout,
    x, cot, wqkv, wso, wcq, wckv, wco, win, wout,
    packed, sh, n1, marks, q8, mem, kv, ch, qfs, kfs, qfc, kfc, dfc, pre2, do,
    act, hg, br3, late, pre1, g3, vec, vbuf, vz,
    *rest,
):
    (load_sem, out_sem, send, recv, local, vsend, vrecv, xsend, xrecv, msend, mrecv) = rest[-11:]
    seg_bufs = rest[:-11]
    slow, br2 = late.at[:L], late.at[L:]
    two, gso = late.at[: 3 * D], late.at[3 * D :]
    me = lax.axis_index("mem")
    dp = lax.axis_index("dp")
    n = 4
    piece = L // n
    bits = (lax.rem(dp, 2), lax.rem(dp // 2, 2), lax.rem(dp // 4, 2))
    place = (dp, me, bits)
    near = [(dp + (1 << a) * (1 - 2 * bits[a]), me) for a in range(3)]
    peers = near + [(dp, lax.rem(me + t, n)) for t in range(1, n)]

    loads = {}
    for i, (name, src, dst) in enumerate(
        [
            ("x", x_in, x), ("wqkv", wqkv_in, wqkv), ("wso", wso_in, wso), ("wcq", wcq_in, wcq), ("wckv", wckv_in, wckv),
            ("wco", wco_in, wco), ("win", win_in, win), ("wout", wout_in, wout), ("cot", cot_in, cot),
        ]
    ):
        loads[name] = pltpu.make_async_copy(src, dst, load_sem.at[i])
        loads[name].start()

    barrier = pltpu.get_barrier_semaphore()
    for peer in peers:
        pl.semaphore_signal(barrier, inc=1, device_id=peer, device_id_type=MESH)
    pl.semaphore_wait(barrier, len(peers))

    def exchange(t):
        peer = lax.rem(me + t, n)
        return pltpu.make_async_remote_copy(
            src_ref=meml.at[peer],
            dst_ref=mem.at[span(me, piece), :],
            send_sem=xsend.at[t],
            recv_sem=xrecv.at[t],
            device_id=(dp, peer),
            device_id_type=MESH,
        )

    own = pltpu.make_async_copy(meml.at[me], mem.at[span(me, piece), :], xsend.at[0])
    for t in range(1, n):
        exchange(t).start()
    own.start()

    whole_parts = ((0, 256, 0), (256, 512, 1))
    wide_parts = ((0, 512, 0), (512, 1024, 1))
    pair_parts = (((0, 128, 0), (128, 384, 1)), ((0, 128, 1), (128, 384, 0)))

    def pieces(w_out, w_in, co, two, so, qkv):
        half = FF // 2
        return [
            w_out.at[:half], w_out.at[half:], w_in.at[:, :half], w_in.at[:, half:], co, two, so,
        ] + [qkv.at[j] for j in range(PAIRS)]

    sources = pieces(wout, win, wco, two, gso, g3)
    finals = pieces(f_out, f_in, f_two.at[:D], f_two.at[D:], f_so, f_qkv)
    ticks = {}
    for i, (rows, width) in enumerate(SEGMENTS):
        parts = {D: whole_parts, FF // 2: wide_parts, 384: pair_parts[i % 2]}[width]
        stages = Segment(i, sources[i], parts, seg_bufs[5 * i : 5 * i + 5], finals[i], (send, recv, local), place).stages()
        for (phase, step), fn in zip(SCHEDULE[i], stages):
            ticks.setdefault(phase, []).append((step, i, fn))

    def at(phase, step, fn):
        ticks.setdefault(phase, []).append((step, -1, fn))

    def run(phase, i, unit=1, part=0):
        todo = {}
        for step, order, fn in ticks.get(phase, []):
            if step % unit == part:
                todo.setdefault(step // unit, []).append((order, fn))
        for step, fns in sorted(todo.items()):

            def stage(fns=fns):
                for _, fn in sorted(fns, key=lambda item: item[0]):
                    fn()

            if not isinstance(i, int):
                pl.when(i == step)(stage)
            elif i == step:
                stage()

    lane = lane_of()
    lengths = [jnp.zeros((1, 128), jnp.int32)] * 2
    for s in range(16):
        lengths[0] = jnp.where(lane == s, tgt_len[0, s], lengths[0])
        lengths[1] = jnp.where(lane == s, src_len[me, s], lengths[1])
    is_doc = jnp.where(src_len[me, 0] > SHORT, 1, 0)

    def features(i):
        rows = span(i, TB)
        feats, one_hot, inside = key_features(lengths[0], is_doc, TB, i * TB)
        kfs[rows, :] = feats
        qfs[rows, :] = one_hot
        qfc[rows, :] = one_hot
        marks[rows, :] = jnp.broadcast_to(jnp.sum(inside, axis=1, keepdims=True), (TB, 128))
        feats, _, _ = key_features(lengths[1], is_doc, TB, i * TB)
        kfc[rows, :] = feats

    loop(L // TB, features)
    loads["x"].wait()
    loads["wqkv"].wait()

    packed[:, :D] = dot(x[...], wqkv[:, :D]).astype(bf) * bf(SCALE)
    packed[:, D:] = dot(x[...], wqkv[:, D:]).astype(bf)

    causal = lax.broadcasted_iota(jnp.int32, (SELF_BQ, SELF_BQ), 0) >= lax.broadcasted_iota(
        jnp.int32, (SELF_BQ, SELF_BQ), 1
    )

    def lanes_at(first, j):
        return pl.ds(pl.multiple_of(first + j * 128, 128), 128)

    for b in range(L // SELF_BQ):
        low, high = b * SELF_BQ, (b + 1) * SELF_BQ

        def self_pair(j, low=low, high=high):
            def section(first, last, mask):
                keys = jnp.concatenate([packed[first:last, lanes_at(D, j)], kfs[first:last, :]], axis=1)
                values = packed[first:last, lanes_at(2 * D, j)]
                return keys, jnp.concatenate([values, jnp.ones((last - first, 128), bf)], axis=1), mask

            sections = [section(low, high, causal)]
            if low:
                sections.append(section(0, low, None))
            sh[low:high, span(j, 128)] = softmax_pair(
                j, packed[low:high, span(j, 128)], sections, qfs, slice(low, high)
            )

        loop(PAIRS, self_pair)

    loads["wso"].wait()
    loads["wcq"].wait()

    def first_norm(i):
        rows = slice(i * TB, (i + 1) * TB)
        branch = dot(sh[rows, :], wso[...])
        yield
        normed, scaler = norm(omega[0:1, :] * x[rows, :].astype(f32) + branch)
        n1[rows, :] = normed
        marks[rows, :] = jnp.where(half_lanes(), marks[rows, :], scaler)
        first = (normed * gain[0:1, :] + bias[0:1, :]).astype(bf)
        yield
        q8[rows, :] = dot(first, wcq[...]).astype(bf) * bf(SCALE)

    weave(first_norm(i) for i in range(L // TB))

    own.wait()
    for t in range(1, n):
        exchange(t).wait()
    loads["wckv"].wait()

    kv[...] = dot(mem[...], wckv[...]).astype(bf)

    def cross_pair(i):
        j = i // (L // CROSS_BQ)
        rows = span(lax.rem(i, L // CROSS_BQ), CROSS_BQ)
        keys = jnp.concatenate([kv[:, span(j, 128)], kfc[...]], axis=1)
        values = jnp.concatenate([kv[:, lanes_at(D, j)], jnp.ones((L, 128), bf)], axis=1)
        ch[rows, span(j, 128)] = softmax_pair(j, q8[rows, span(j, 128)], [(keys, values, None)], qfc, rows)

    loop(PAIRS * (L // CROSS_BQ), cross_pair)

    vec[...] = jnp.zeros_like(vec)
    for name in ("wco", "win", "wout", "cot"):
        loads[name].wait()

    def tokens(i):
        rows = slice(i * TB, (i + 1) * TB)
        branch = dot(ch[rows, :], wco[...])
        yield
        n2, r2 = norm(omega[1:2, :] * (n1[rows, :] * gain[0:1, :] + bias[0:1, :]) + branch)
        pre2[rows, :] = n2
        second_low = (n2 * gain[1:2, :] + bias[1:2, :]).astype(bf)
        slow[rows, :] = second_low
        yield
        for c in range(FF // WIDE):
            cols = slice(c * WIDE, (c + 1) * WIDE)
            h = dot(second_low, win[:, cols])
            yield
            square = h * h
            cdf = 0.5 + 0.5 * jnp.tanh(h * (GELU_C + (GELU_C * GELU_A) * square))
            value = h * cdf
            act[rows, cols] = value.astype(bf)
            slope = cdf + value * (1.0 - cdf) * (2.0 * GELU_C + (6.0 * GELU_C * GELU_A) * square)
            hg[rows, cols] = slope.astype(bf)
            yield
        branch = dot(act[rows, :], wout[...])
        yield
        second = pre2[rows, :] * gain[1:2, :] + bias[1:2, :]
        n3, r3 = norm(omega[2:3, :] * second + branch)
        third = n3 * gain[2:3, :] + bias[2:3, :]
        kept = marks[rows, :][:, 0:1]
        up = cot[rows, :].astype(f32) * kept
        cot[rows, :] = (third * kept).astype(bf)
        pre3 = norm_back(up, n3, r3, gain[2:3, :])
        vec[2:3, :] += total(up * n3)
        vec[5:6, :] += total(up)
        vec[8:9, :] += total(pre3 * second)
        low3 = pre3.astype(bf)
        br3[rows, :] = low3
        grad = omega[2:3, :] * pre3
        yield
        for c in range(FF // WIDE):
            cols = slice(c * WIDE, (c + 1) * WIDE)
            back = dot(low3, wout[cols, :], NT)
            yield
            hg[rows, cols] = (back * hg[rows, cols].astype(f32)).astype(bf)
            yield
        branch = dot(hg[rows, :], win[...], NT)
        yield
        grad = grad + branch
        n2 = pre2[rows, :]
        back2 = norm_back(grad, n2, r2, gain[1:2, :])
        vec[1:2, :] += total(grad * n2)
        vec[4:5, :] += total(grad)
        vec[7:8, :] += total(back2 * (n1[rows, :] * gain[0:1, :] + bias[0:1, :]))
        pre2[rows, :] = back2
        low2 = back2.astype(bf)
        br2[rows, :] = low2
        yield
        dlow = dot(low2, wco[...], NT).astype(bf)
        do[rows, :] = dlow
        yield
        dfc[rows, :] = delta_features(dlow.astype(f32) * ch[rows, :].astype(f32))

    weave(tokens(i) for i in range(L // TB))
    out_copy = pltpu.make_async_copy(cot, out, out_sem.at[0])
    out_copy.start()

    wout[...] = dot(act[...], br3[...], TN).astype(bf)
    run("sums", 0)
    win[...] = dot(slow[...], hg[...], TN).astype(bf)
    run("sums", 1)
    wco[...] = dot(ch[...], br2[...], TN).astype(bf)
    run("sums", 2)

    kvg, qg, fl = hg.at[:, : 2 * D], hg.at[:, 2 * D : 3 * D], hg.at[:, 3 * D :]
    pg, mgs = act.at[:, : 3 * D], act.at[:, 3 * D :]
    br1 = br3
    blocks = L // CROSS_BK

    def cross_back(i):
        run("cross", i)
        j = i // blocks
        b = lax.rem(i, blocks)
        rows = span(b, CROSS_BK)
        lanes = span(j, 128)
        dk, dv, dq = back_tile(
            j, kv[rows, lanes], kv[rows, lanes_at(D, j)], kfc[rows, :], q8[:, lanes], qfc[...], do[:, lanes], dfc[...], None
        )
        kvg[rows, lanes] = dk.astype(bf)
        kvg[rows, lanes_at(D, j)] = dv.astype(bf)

        @pl.when(b == 0)
        def _():
            pre1[:, lanes] = dq

        @pl.when(b > 0)
        def _():
            pre1[:, lanes] += dq

    loop(PAIRS * blocks, cross_back)

    run("sums", 3)
    fl[...] = (n1[...] * gain[0:1, :] + bias[0:1, :]).astype(bf)
    qg[...] = (pre1[...] * SCALE).astype(bf)

    run("sums", 4)
    two[:D, :] = dot(fl[...], qg[...], TN).astype(bf)
    two[D : 2 * D, :] = dot(mem[...], kvg[:, :D], TN).astype(bf)
    two[2 * D :, :] = dot(mem[...], kvg[:, D:], TN).astype(bf)
    run("sums", 5)
    mgs[...] = dot(kvg[...], wckv[...], NT).astype(bf)

    def memory_back(t):
        peer = lax.rem(me + t, n)
        return pltpu.make_async_remote_copy(
            src_ref=mgs.at[span(peer, piece), :],
            dst_ref=mgrad.at[me],
            send_sem=msend.at[t],
            recv_sem=mrecv.at[t],
            device_id=(dp, peer),
            device_id_type=MESH,
        )

    memory_own = pltpu.make_async_copy(mgs.at[span(me, piece), :], mgrad.at[me], msend.at[0])
    memory_own.start()
    for t in range(1, n):
        memory_back(t).start()

    def first_back(i):
        run("first", i)
        rows = slice(i * TB, (i + 1) * TB)
        branch = dot(qg[rows, :], wcq[...], NT)
        yield
        normed = n1[rows, :]
        grad = omega[1:2, :] * pre2[rows, :] + branch
        back1 = norm_back(grad, normed, marks[rows, :][:, 64:65], gain[0:1, :])
        vec[0:1, :] += total(grad * normed)
        vec[3:4, :] += total(grad)
        vec[6:7, :] += total(back1 * x[rows, :].astype(f32))
        pre1[rows, :] = back1
        low1 = back1.astype(bf)
        br1[rows, :] = low1
        yield
        dlow = dot(low1, wso[...], NT).astype(bf)
        do[rows, :] = dlow
        yield
        dfc[rows, :] = delta_features(dlow.astype(f32) * sh[rows, :].astype(f32))

    weave(first_back(i) for i in range(L // TB))

    run("gso", 0)
    gso[...] = dot(sh[...], br1[...], TN).astype(bf)
    run("sums", 6)

    def vec_near(a):
        return pltpu.make_async_remote_copy(
            src_ref=vec.at[pl.ds(16 * a, 16), :],
            dst_ref=vbuf.at[a],
            send_sem=vsend.at[a],
            recv_sem=vrecv.at[a],
            device_id=near[a],
            device_id_type=MESH,
        )

    def vec_far(t):
        return pltpu.make_async_remote_copy(
            src_ref=vec.at[pl.ds(48, 16), :],
            dst_ref=vz.at[me],
            send_sem=vsend.at[2 + t],
            recv_sem=vrecv.at[2 + t],
            device_id=(dp, lax.rem(me + t, n)),
            device_id_type=MESH,
        )

    def vec_next(a):
        vec_near(a).wait()
        vec[16 * (a + 1) : 16 * (a + 2), :] = vec[16 * a : 16 * (a + 1), :] + vbuf[a]
        if a < 2:
            vec_near(a + 1).start()
        else:
            for t in range(1, n):
                vec_far(t).start()

    def vec_last():
        for t in range(1, n):
            vec_far(t).wait()
        vz[me] = vec[48:64, :]
        vout[...] = (vz[0] + vz[1]) + (vz[2] + vz[3])

    vec_near(0).start()
    at("self", 3, lambda: vec_next(0))
    at("self", 7, lambda: vec_next(1))
    at("self", 12, lambda: vec_next(2))
    at("end", 4, vec_last)

    below = lax.broadcasted_iota(jnp.int32, (SELF_BK, SELF_BK), 1) >= lax.broadcasted_iota(
        jnp.int32, (SELF_BK, SELF_BK), 0
    )
    parts = L // SELF_BK

    def self_back(j):
        dqs = []
        for b in range(parts):
            run("self", j, parts, b)
            low, high = b * SELF_BK, (b + 1) * SELF_BK
            dk, dv, dq = back_tile(
                j,
                packed[low:high, lanes_at(D, j)],
                packed[low:high, lanes_at(2 * D, j)],
                kfs[low:high, :],
                packed[low:, span(j, 128)],
                qfs[low:, :],
                do[low:, span(j, 128)],
                dfc[low:, :],
                below,
            )
            pg[low:high, lanes_at(D, j)] = dk.astype(bf)
            pg[low:high, lanes_at(2 * D, j)] = dv.astype(bf)
            for i in range(b, parts):
                share = dq[(i - b) * SELF_BK : (i - b + 1) * SELF_BK, :]
                if b == 0:
                    dqs.append(share)
                else:
                    dqs[i] = dqs[i] + share
        for i, share in enumerate(dqs):
            pg[i * SELF_BK : (i + 1) * SELF_BK, span(j, 128)] = (share * SCALE).astype(bf)
        both = jnp.concatenate([pg[:, lanes_at(c * D, j)] for c in range(3)], axis=1)
        g3[j] = dot(x[...], both, TN).astype(bf)

    loop(PAIRS, self_back)

    def igrad_copy(i):
        return pltpu.make_async_copy(pre1.at[span(i, TB), :], igrad.at[span(i, TB), :], out_sem.at[1 + i])

    def input_back(i):
        run("input", i)
        rows = span(i, TB)
        pre1[rows, :] = omega[0:1, :] * pre1[rows, :] + dot(pg[rows, :], wqkv[...], NT)
        igrad_copy(i).start()

    loop(L // TB, input_back)
    for _, _, fn in sorted(ticks["end"], key=lambda item: item[:2]):
        fn()
    out_copy.wait()
    memory_own.wait()
    for t in range(1, n):
        memory_back(t).wait()
    for i in range(L // TB):
        igrad_copy(i).wait()


CASTS = (
    [(0, (slice(i * D, (i + 1) * D), slice(0, D)), 0, (slice(i * D, (i + 1) * D), slice(0, D))) for i in range(4)]
    + [(1, (slice(0, D), slice(i * D, (i + 1) * D)), 1, (slice(0, D), slice(i * D, (i + 1) * D))) for i in range(4)]
    + [
        (2, (slice(0, D), slice(0, D)), 2, (slice(0, D), slice(0, D))),
        (2, (slice(D, 2 * D), slice(0, D)), 3, (slice(0, D), slice(0, D))),
        (2, (slice(2 * D, 3 * D), slice(0, D)), 4, (slice(0, D), slice(0, D))),
        (2, (slice(3 * D, 4 * D), slice(0, D)), 4, (slice(0, D), slice(D, 2 * D))),
        (3, (slice(0, D), slice(0, D)), 5, (slice(0, D), slice(0, D))),
    ]
)


def cast_kernel(
    out_in, igrad_in, mgrad_in, f_out, f_in, f_two, f_so, f_qkv,
    out, igrad, mgrad, g_out, g_in, g_co, g_cq, g_ckv, g_so, g_qkv,
    narrow, wide, qkv_narrow, qkv_wide, out_held, igrad_held, sems, out_sems,
):
    passed = [(out_in, out_held, out), (igrad_in, igrad_held, igrad)]
    whole_in = [pltpu.make_async_copy(src, held, sems.at[i]) for i, (src, held, _) in enumerate(passed)]
    froms = (f_out, f_in, f_two, f_so)
    tos = (g_out, g_in, g_co, g_cq, g_ckv, g_so)
    pieces = []
    for source, window, target, place in CASTS:
        pieces.append((froms[source].at[window], tos[target].at[place]))
    for i in range(2):
        pieces.append((mgrad_in.at[pl.ds(i * D, D), :], mgrad.at[pl.ds(i * D, D), :]))
    ins = [pltpu.make_async_copy(src, narrow.at[i], sems.at[2 + i]) for i, (src, _) in enumerate(pieces)]
    outs = [pltpu.make_async_copy(wide.at[i], dst, out_sems.at[i]) for i, (_, dst) in enumerate(pieces)]
    qkv_in = pltpu.make_async_copy(f_qkv, qkv_narrow, sems.at[2 + len(pieces)])
    qkv_out = pltpu.make_async_copy(qkv_wide, g_qkv, out_sems.at[len(pieces)])
    for copy in whole_in + ins:
        copy.start()
    qkv_in.start()
    whole_out = [
        pltpu.make_async_copy(held, dst, out_sems.at[len(pieces) + 1 + i]) for i, (_, held, dst) in enumerate(passed)
    ]
    for copy_in, copy_out in zip(whole_in, whole_out):
        copy_in.wait()
        copy_out.start()
    for i, copy in enumerate(ins):
        copy.wait()

        def body(r, i=i):
            wide[i, span(r, 64), :] = narrow[i, span(r, 64), :].astype(f32)

        loop(D // 64, body)
        outs[i].start()
    qkv_in.wait()

    def body(r):
        for j in range(PAIRS):
            for c in range(3):
                qkv_wide[span(r, 64), c * D + j * 128 : c * D + (j + 1) * 128] = qkv_narrow[
                    j, span(r, 64), c * 128 : (c + 1) * 128
                ].astype(f32)

    loop(D // 64, body)
    qkv_out.start()
    for copy in whole_out + outs:
        copy.wait()
    qkv_out.wait()


VM = pl.BlockSpec(memory_space=pltpu.VMEM)
SM = pl.BlockSpec(memory_space=pltpu.SMEM)
ANY = pl.BlockSpec(memory_space=pl.ANY)


def per_device(
    inputs, memory, cotangent, tgt_len, src_len,
    self_qkv, self_out, cross_query, cross_kv, cross_out, ffn_in, ffn_out, ln_gain, ln_bias, omega_scale, dp,
):
    shape = jax.ShapeDtypeStruct
    scratch = [
        pltpu.VMEM((L, D), bf),
        pltpu.VMEM((L, D), bf),
        pltpu.VMEM((D, 3 * D), bf),
        pltpu.VMEM((D, D), bf),
        pltpu.VMEM((D, D), bf),
        pltpu.VMEM((D, 2 * D), bf),
        pltpu.VMEM((D, D), bf),
        pltpu.VMEM((D, FF), bf),
        pltpu.VMEM((FF, D), bf),
        pltpu.VMEM((L, 3 * D), bf),
        pltpu.VMEM((L, D), bf),
        pltpu.VMEM((L, D), f32),
        pltpu.VMEM((L, 128), f32),
        pltpu.VMEM((L, D), bf),
        pltpu.VMEM((L, D), bf),
        pltpu.VMEM((L, 2 * D), bf),
        pltpu.VMEM((L, D), bf),
        pltpu.VMEM((L, 128), bf),
        pltpu.VMEM((L, 128), bf),
        pltpu.VMEM((L, 128), bf),
        pltpu.VMEM((L, 128), bf),
        pltpu.VMEM((L, 128), bf),
        pltpu.VMEM((L, D), f32),
        pltpu.VMEM((L, D), bf),
        pltpu.VMEM((L, FF), bf),
        pltpu.VMEM((L, FF), bf),
        pltpu.VMEM((L, D), bf),
        pltpu.VMEM((2 * L, D), bf),
        pltpu.VMEM((L, D), f32),
        pltpu.VMEM((PAIRS, D, 384), bf),
        pltpu.VMEM((64, D), f32),
        pltpu.VMEM((3, 16, D), f32),
        pltpu.VMEM((4, 16, D), f32),
    ]
    for n, w in SEGMENTS:
        scratch += seg_scratch(n, w)
    count = len(SEGMENTS)
    sem = pltpu.SemaphoreType.DMA
    scratch += [
        sem((9,)), sem((5,)), sem((count, 22)), sem((count, 22)), sem((2 * count,)), sem((6,)), sem((6,)),
        sem((4,)), sem((4,)), sem((4,)), sem((4,)),
    ]
    results = pl.pallas_call(
        layer_kernel,
        out_shape=[
            shape((L, D), bf),
            shape((L, D), f32),
            shape((4, L // 4, D), bf),
            shape((FF, D), bf),
            shape((D, FF), bf),
            shape((4 * D, D), bf),
            shape((D, D), bf),
            shape((PAIRS, D, 384), bf),
            shape((16, D), f32),
        ],
        in_specs=[SM] * 2 + [ANY] * 10 + [VM] * 3,
        out_specs=[ANY] * 8 + [VM],
        scratch_shapes=scratch,
        compiler_params=pltpu.CompilerParams(collective_id=0, has_side_effects=True, vmem_limit_bytes=(64 << 20) - (128 << 10)),
        name="layer",
    )(
        tgt_len, src_len, inputs.reshape(L, D), memory, cotangent.reshape(L, D), self_qkv, self_out, cross_query, cross_kv,
        cross_out, ffn_in, ffn_out, ln_gain, ln_bias, omega_scale,
    )
    output, igrad, mgrad, grads, small = results[0], results[1], results[2], results[3:8], results[8]

    blocks = dp // 8
    if blocks > 1:
        groups = [[i + 8 * b for b in range(blocks)] for i in range(8)]
        *grads, small = lax.psum((*grads, small), "dp", axis_index_groups=groups)

    pieces = len(CASTS) + 2
    output, igrad, mgrad, g_out, g_in, g_co, g_cq, g_ckv, g_so, g_qkv = pl.pallas_call(
        cast_kernel,
        out_shape=[
            shape((L, D), bf),
            shape((L, D), f32),
            shape((L, D), f32),
            shape((FF, D), f32),
            shape((D, FF), f32),
            shape((D, D), f32),
            shape((D, D), f32),
            shape((D, 2 * D), f32),
            shape((D, D), f32),
            shape((D, 3 * D), f32),
        ],
        in_specs=[ANY] * 8,
        out_specs=[ANY] * 10,
        scratch_shapes=[
            pltpu.VMEM((pieces, D, D), bf),
            pltpu.VMEM((pieces, D, D), f32),
            pltpu.VMEM((PAIRS, D, 384), bf),
            pltpu.VMEM((D, 3 * D), f32),
            pltpu.VMEM((L, D), bf),
            pltpu.VMEM((L, D), f32),
            sem((pieces + 3,)),
            sem((pieces + 3,)),
        ],
        compiler_params=pltpu.CompilerParams(vmem_limit_bytes=62 << 20),
        name="casts",
    )(output, igrad, mgrad.reshape(L, D), *grads)
    return (
        output.reshape(1, L, D),
        igrad.reshape(1, L, D),
        mgrad.reshape(4, L // 4, D),
        g_qkv,
        g_so,
        g_cq,
        g_ckv,
        g_co,
        g_in,
        g_out,
        small[0:3],
        small[3:6],
        small[6:9],
    )


def solution(mesh):
    rows = P(("dp", "mem"), None, None)
    return jax.shard_map(
        functools.partial(per_device, dp=mesh.shape["dp"]),
        mesh=mesh,
        in_specs=(rows, P("dp", "mem", None), rows, P(("dp", "mem"), None), P("dp", None)) + (P(),) * 10,
        out_specs=(rows, rows, P("dp", "mem", None)) + (P(),) * 10,
        check_vma=False,
    )
```

```python
import functools

import jax
import jax.numpy as jnp
from jax import lax
from jax.experimental import pallas as pl
from jax.experimental.pallas import tpu as pltpu
from jax.sharding import PartitionSpec as P

f32 = jnp.float32
bf = jnp.bfloat16
MESH = pl.DeviceIdType.MESH
NN = (((1,), (0,)), ((), ()))
NT = (((1,), (1,)), ((), ()))
TN = (((0,), (0,)), ((), ()))

L = 1024
D = 512
FF = 2048
HEADS = 8
PAIRS = HEADS // 2
SHORT = 64
SCALE = 0.125
NEG = -1e30
EPS = 1e-05
GELU_C = 0.7978845608028654
GELU_A = 0.044715


def dot(a, b, dims=NN):
    return lax.dot_general(a, b, dims, preferred_element_type=f32)


def span(i, n):
    return pl.ds(pl.multiple_of(i * n, n), n)


def loop(n, body):
    def step(i, carry):
        body(i)
        return carry

    lax.fori_loop(0, n, step, 0)


def weave(parts):
    parts = list(parts)
    live = set(range(len(parts)))
    turn = 0
    while live:
        for k in sorted(live):
            if turn >= k and next(parts[k], "done") == "done":
                live.discard(k)
        turn += 1


def half_lanes():
    return lax.broadcasted_iota(jnp.int32, (1, 128), 1) < 64


def norm(values):
    centred = values - jnp.mean(values, axis=-1, keepdims=True)
    scaler = lax.rsqrt(jnp.mean(centred * centred, axis=-1, keepdims=True) + EPS)
    return centred * scaler, scaler


def norm_back(upstream, normed, scaler, gain_row):
    scaled = upstream * gain_row
    centred = scaled - jnp.mean(scaled, axis=-1, keepdims=True)
    centred = centred - normed * jnp.mean(scaled * normed, axis=-1, keepdims=True)
    return centred * scaler


def total(values):
    return jnp.sum(values, axis=0, keepdims=True)


def lane_of():
    return lax.broadcasted_iota(jnp.int32, (1, 128), 1)


def put_parts(values, head, old):
    at = lane_of() - (16 + 3 * head)
    high = values.astype(bf).astype(f32)
    rest = values - high
    middle = rest.astype(bf).astype(f32)
    low = rest - middle
    return jnp.where(at == 0, high, jnp.where(at == 1, middle, jnp.where(at == 2, low, old)))


def head_keys(feats, head):
    at = lane_of() - (16 + 3 * head)
    return jnp.where((at >= 0) & (at < 3), jnp.ones_like(feats), feats)


def key_features(lengths, is_doc, rows, first):
    pos = first + lax.broadcasted_iota(jnp.int32, (rows, 128), 0)
    lane = lax.broadcasted_iota(jnp.int32, (rows, 128), 1)
    seg = (pos >> 6) * (1 - is_doc)
    inside = (seg == lane) & (pos - seg * SHORT < lengths)
    feats = jnp.where(lane < 16, jnp.where(inside, 0.0, NEG), 0.0)
    hot = jnp.where(seg == lane, 1.0, 0.0)
    return feats.astype(bf), hot.astype(bf), jnp.where(inside, 1.0, 0.0)


def softmax_pair(j, qp, sections, lse_ref, rows):
    half = half_lanes()
    mixed = []
    base = lse_ref[rows, :]
    feats = base.astype(f32)
    scores = []
    for e in range(2):
        sel = half if e == 0 else jnp.logical_not(half)
        qa = jnp.concatenate([jnp.where(sel, qp, jnp.zeros_like(qp)), base], axis=1)
        scores.append([dot(qa, keys, NT) for keys, _, _ in sections])
    for e in range(2):
        masked = [s if mask is None else jnp.where(mask, s, NEG) for s, (_, _, mask) in zip(scores[e], sections)]
        largest = functools.reduce(jnp.maximum, [jnp.max(s, axis=1, keepdims=True) for s in masked])
        acc = None
        for s, (_, values, _) in zip(masked, sections):
            o = dot(jnp.exp(s - largest).astype(bf), values)
            acc = o if acc is None else acc + o
        summed = acc[:, 128:]
        feats = put_parts(-(largest + jnp.log(summed)), 2 * j + e, feats)
        mixed.append(acc[:, :128] / summed)
    lse_ref[rows, :] = feats.astype(bf)
    return jnp.where(half, mixed[0], mixed[1]).astype(bf)


def back_tile(j, k_rows, v_rows, kfeat, qp, qfeat, gp, gfeat, mask):
    half = half_lanes()
    dk, dv, dq = [], [], []
    scores, slopes = [], []
    for e in range(2):
        sel = half if e == 0 else jnp.logical_not(half)
        kf = head_keys(kfeat, 2 * j + e)
        qa = jnp.concatenate([jnp.where(sel, qp, jnp.zeros_like(qp)), qfeat], axis=1)
        ga = jnp.concatenate([jnp.where(sel, gp, jnp.zeros_like(gp)), gfeat], axis=1)
        scores.append(dot(jnp.concatenate([k_rows, kf], axis=1), qa, NT))
        slopes.append(dot(jnp.concatenate([v_rows, kf], axis=1), ga, NT))
    for e in range(2):
        probs = jnp.exp(scores[e])
        if mask is not None:
            width = mask.shape[1]
            first = jnp.where(mask, probs[:, :width], 0.0)
            probs = first if probs.shape[1] == width else jnp.concatenate([first, probs[:, width:]], axis=1)
        ds = (probs * slopes[e]).astype(bf)
        dv.append(dot(probs.astype(bf), gp))
        dk.append(dot(ds, qp))
        dq.append(dot(ds, k_rows, TN))
    return (
        jnp.where(half, dk[0], dk[1]),
        jnp.where(half, dv[0], dv[1]),
        jnp.where(half, dq[0], dq[1]),
    )


def delta_features(product):
    half = half_lanes()
    feats = jnp.zeros((product.shape[0], 128), f32)
    for j in range(PAIRS):
        part = product[:, 128 * j : 128 * (j + 1)]
        for e in range(2):
            sel = half if e == 0 else jnp.logical_not(half)
            delta = jnp.sum(jnp.where(sel, part, 0.0), axis=1, keepdims=True)
            feats = put_parts(-delta, 2 * j + e, feats)
    return feats.astype(bf)


SELF_BQ = 512
SELF_BK = 256
CROSS_BQ = 512
CROSS_BK = 512
TB = 512
WIDE = 1024


class Segment:
    def __init__(self, index, source, parts, bufs, final, sems, place):
        self.index, self.source, self.parts = index, source, parts
        self.n = source.shape[0]
        (self.r0, self.r1, self.r2, self.r3, self.fin) = bufs
        self.final = final
        self.send, self.recv, self.local = sems
        self.place = place

    def remote(self, src, dst, k, device):
        return pltpu.make_async_remote_copy(
            src_ref=src,
            dst_ref=dst,
            send_sem=self.send.at[self.index, k],
            recv_sem=self.recv.at[self.index, k],
            device_id=device,
            device_id_type=MESH,
        )

    def mine(self, first, count):
        return pl.ds(pl.multiple_of(self.place[2][0] * (self.n // 2) + first, 16), count)

    def core_copy(self):
        n, (dp, me, bits) = self.n, self.place
        other = pl.ds(pl.multiple_of((1 - bits[0]) * (n // 2), 16), n // 2)
        return self.remote(self.source.at[other, :], self.r0, 0, (dp + 1 - 2 * bits[0], me))

    def partner(self, axis):
        dp, me, bits = self.place
        return (dp + 2 * axis * (1 - 2 * bits[axis]), me)

    def axes(self, p):
        return (1, 2) if self.parts[p][2] == 0 else (2, 1)

    def lanes(self, p):
        return slice(self.parts[p][0], self.parts[p][1])

    def offset(self, p, depth):
        if depth == 0:
            return 0
        n, (_, me, bits) = self.n, self.place
        one, two = self.axes(p)
        result = bits[one] * (n // 4)
        if depth > 1:
            result = result + bits[two] * (n // 8)
        if depth > 2:
            result = result + me * (n // 32)
        return result

    def halving(self, p, depth):
        n, (_, _, bits) = self.n, self.place
        axis = self.axes(p)[depth - 1]
        size = n // (4 if depth == 1 else 8)
        other = self.offset(p, depth - 1) + (1 - bits[axis]) * size
        buf = self.r1 if depth == 1 else self.r2
        return self.remote(
            self.source.at[self.mine(other, size), self.lanes(p)],
            buf.at[:, self.lanes(p)],
            2 * depth - 1 + p,
            self.partner(axis),
        )

    def quarter(self, p, t):
        n, (dp, me, _) = self.n, self.place
        peer = lax.rem(me + t, 4)
        return self.remote(
            self.source.at[self.mine(self.offset(p, 2) + peer * (n // 32), n // 32), self.lanes(p)],
            self.r3.at[t - 1, :, self.lanes(p)],
            5 + 3 * p + t - 1,
            (dp, peer),
        )

    def final_rows(self, p, depth):
        size = self.n // (2, 4, 8, 32)[depth]
        lanes = slice(None) if p is None else self.lanes(p)
        return self.final.at[self.mine(self.offset(p, depth), size), lanes]

    def keep_copy(self, p):
        return pltpu.make_async_copy(
            self.fin.at[:, self.lanes(p)], self.final_rows(p, 3), self.local.at[2 * self.index + p]
        )

    def spread(self, p, t):
        dp, me, _ = self.place
        return self.remote(
            self.fin.at[:, self.lanes(p)],
            self.final_rows(p, 3),
            11 + 3 * p + t - 1,
            (dp, lax.rem(me + t, 4)),
        )

    def doubling(self, p, depth):
        ref = self.final_rows(p, depth)
        return self.remote(ref, ref, 15 + 2 * (3 - depth) + p, self.partner(self.axes(p)[depth - 1]))

    def core_back(self):
        dp, me, bits = self.place
        ref = self.final_rows(None, 0)
        return self.remote(ref, ref, 21, (dp + 1 - 2 * bits[0], me))

    def add(self, first, buf, count, lanes):
        step = 128 if count % 128 == 0 else count

        def body(i):
            rows = self.mine(first + i * step, step)
            self.source[rows, lanes] = self.source[rows, lanes] + buf[pl.ds(pl.multiple_of(i * step, 16), step), lanes]

        if count == step:
            body(0)
        else:
            loop(count // step, body)

    def stages(self):
        n = self.n
        both = range(len(self.parts))

        def s0():
            self.core_copy().start()

        def s1():
            self.core_copy().wait()
            self.add(0, self.r0, n // 2, slice(None))
            for p in both:
                self.halving(p, 1).start()

        def s2():
            for p in both:
                self.halving(p, 1).wait()
                self.add(self.offset(p, 1), self.r1, n // 4, self.lanes(p))
                self.halving(p, 2).start()

        def s3():
            for p in both:
                self.halving(p, 2).wait()
                self.add(self.offset(p, 2), self.r2, n // 8, self.lanes(p))
                for t in range(1, 4):
                    self.quarter(p, t).start()

        def s4():
            for p in both:
                for t in range(1, 4):
                    self.quarter(p, t).wait()
                lanes = self.lanes(p)
                mine = self.source[self.mine(self.offset(p, 3), n // 32), lanes].astype(f32)
                for t in range(3):
                    mine = mine + self.r3[t, :, lanes].astype(f32)
                self.fin[:, lanes] = mine.astype(bf)
                self.keep_copy(p).start()
                for t in range(1, 4):
                    self.spread(p, t).start()

        def s5():
            for p in both:
                self.keep_copy(p).wait()
                for t in range(1, 4):
                    self.spread(p, t).wait()
                self.doubling(p, 2).start()

        def s6():
            for p in both:
                self.doubling(p, 2).wait()
                self.doubling(p, 1).start()

        def s7():
            for p in both:
                self.doubling(p, 1).wait()
            self.core_back().start()

        def s8():
            self.core_back().wait()

        return [s0, s1, s2, s3, s4, s5, s6, s7, s8]


SEGMENTS = [(FF // 2, D)] * 2 + [(D, FF // 2)] * 2 + [(D, D), (3 * D, D), (D, D)] + [(D, 384)] * PAIRS


def seg_scratch(n, w):
    return [
        pltpu.VMEM((n // 2, w), bf),
        pltpu.VMEM((n // 4, w), bf),
        pltpu.VMEM((n // 8, w), bf),
        pltpu.VMEM((3, n // 32, w), bf),
        pltpu.VMEM((n // 32, w), bf),
    ]


SCHEDULE = {
    0: [("sums", 0), ("mid", 0), ("sums", 2), ("cross", 1), ("cross", 3), ("cross", 5), ("sums", 3), ("first", 0), ("self", 2)],
    1: [("sums", 0), ("sums", 1), ("cross", 0), ("cross", 2), ("cross", 5), ("cross", 7), ("sums", 4), ("self", 0), ("self", 4)],
    2: [("sums", 1), ("cross", 0), ("cross", 3), ("cross", 4), ("cross", 6), ("sums", 5), ("self", 5), ("self", 12), ("end", 3)],
    3: [("cross", 0), ("cross", 1), ("cross", 4), ("cross", 6), ("sums", 3), ("first", 1), ("self", 2), ("self", 8), ("self", 13)],
    4: [("sums", 2), ("first", 0), ("gso", 0), ("self", 4), ("input", 0), ("end", 5), ("end", 8), ("end", 13), ("end", 15)],
    5: [("sums", 5), ("self", 0), ("self", 6), ("self", 13), ("input", 1), ("end", 9), ("end", 17), ("end", 25), ("end", 31)],
    6: [("sums", 6), ("self", 5), ("self", 14), ("end", 2), ("end", 14), ("end", 22), ("end", 29), ("end", 36), ("end", 38)],
    7: [("self", 4), ("self", 5), ("self", 13), ("self", 15), ("end", 4), ("end", 16), ("end", 21), ("end", 27), ("end", 32)],
    8: [("self", 8), ("self", 9), ("self", 15), ("input", 1), ("end", 12), ("end", 20), ("end", 26), ("end", 33), ("end", 35)],
    9: [("self", 13), ("end", 1), ("end", 7), ("end", 11), ("end", 19), ("end", 24), ("end", 30), ("end", 37), ("end", 40)],
    10: [("end", 0), ("end", 6), ("end", 10), ("end", 18), ("end", 23), ("end", 28), ("end", 34), ("end", 39), ("end", 41)],
}


def layer_kernel(
    tgt_len, src_len, x_in, meml, cot_in, wqkv_in, wso_in, wcq_in, wckv_in, wco_in, win_in, wout_in, gain, bias, omega,
    out, igrad, mgrad, f_out, f_in, f_two, f_so, f_qkv, vout,
    x, cot, wqkv, wso, wcq, wckv, wco, win, wout,
    packed, sh, n1, marks, q8, mem, kv, ch, qfs, kfs, qfc, kfc, dfc, pre2, do,
    act, hg, br3, late, pre1, g3, vec, vbuf, vz,
    *rest,
):
    (load_sem, out_sem, send, recv, local, vsend, vrecv, xsend, xrecv, msend, mrecv) = rest[-11:]
    seg_bufs = rest[:-11]
    slow, br2 = late.at[:L], late.at[L:]
    two, gso = late.at[: 3 * D], late.at[3 * D :]
    me = lax.axis_index("mem")
    dp = lax.axis_index("dp")
    n = 4
    piece = L // n
    bits = (lax.rem(dp, 2), lax.rem(dp // 2, 2), lax.rem(dp // 4, 2))
    place = (dp, me, bits)
    near = [(dp + (1 << a) * (1 - 2 * bits[a]), me) for a in range(3)]
    peers = near + [(dp, lax.rem(me + t, n)) for t in range(1, n)]

    loads = {}
    for i, (name, src, dst) in enumerate(
        [
            ("x", x_in, x), ("wqkv", wqkv_in, wqkv), ("wso", wso_in, wso), ("wcq", wcq_in, wcq), ("wckv", wckv_in, wckv),
            ("wco", wco_in, wco), ("win", win_in, win), ("wout", wout_in, wout), ("cot", cot_in, cot),
        ]
    ):
        loads[name] = pltpu.make_async_copy(src, dst, load_sem.at[i])
        loads[name].start()

    barrier = pltpu.get_barrier_semaphore()
    for peer in peers:
        pl.semaphore_signal(barrier, inc=1, device_id=peer, device_id_type=MESH)
    pl.semaphore_wait(barrier, len(peers))

    def exchange(t):
        peer = lax.rem(me + t, n)
        return pltpu.make_async_remote_copy(
            src_ref=meml.at[peer],
            dst_ref=mem.at[span(me, piece), :],
            send_sem=xsend.at[t],
            recv_sem=xrecv.at[t],
            device_id=(dp, peer),
            device_id_type=MESH,
        )

    own = pltpu.make_async_copy(meml.at[me], mem.at[span(me, piece), :], xsend.at[0])
    for t in range(1, n):
        exchange(t).start()
    own.start()

    whole_parts = ((0, 256, 0), (256, 512, 1))
    wide_parts = ((0, 512, 0), (512, 1024, 1))
    pair_parts = (((0, 128, 0), (128, 384, 1)), ((0, 128, 1), (128, 384, 0)))

    def pieces(w_out, w_in, co, two, so, qkv):
        half = FF // 2
        return [
            w_out.at[:half], w_out.at[half:], w_in.at[:, :half], w_in.at[:, half:], co, two, so,
        ] + [qkv.at[j] for j in range(PAIRS)]

    sources = pieces(wout, win, wco, two, gso, g3)
    finals = pieces(f_out, f_in, f_two.at[:D], f_two.at[D:], f_so, f_qkv)
    ticks = {}
    for i, (rows, width) in enumerate(SEGMENTS):
        parts = {D: whole_parts, FF // 2: wide_parts, 384: pair_parts[i % 2]}[width]
        stages = Segment(i, sources[i], parts, seg_bufs[5 * i : 5 * i + 5], finals[i], (send, recv, local), place).stages()
        for (phase, step), fn in zip(SCHEDULE[i], stages):
            ticks.setdefault(phase, []).append((step, i, fn))

    def at(phase, step, fn):
        ticks.setdefault(phase, []).append((step, -1, fn))

    def run(phase, i, unit=1, part=0):
        todo = {}
        for step, order, fn in ticks.get(phase, []):
            if step % unit == part:
                todo.setdefault(step // unit, []).append((order, fn))
        for step, fns in sorted(todo.items()):

            def stage(fns=fns):
                for _, fn in sorted(fns, key=lambda item: item[0]):
                    fn()

            if not isinstance(i, int):
                pl.when(i == step)(stage)
            elif i == step:
                stage()

    lane = lane_of()
    lengths = [jnp.zeros((1, 128), jnp.int32)] * 2
    for s in range(16):
        lengths[0] = jnp.where(lane == s, tgt_len[0, s], lengths[0])
        lengths[1] = jnp.where(lane == s, src_len[me, s], lengths[1])
    is_doc = jnp.where(src_len[me, 0] > SHORT, 1, 0)

    def features(i):
        rows = span(i, TB)
        feats, one_hot, inside = key_features(lengths[0], is_doc, TB, i * TB)
        kfs[rows, :] = feats
        qfs[rows, :] = one_hot
        qfc[rows, :] = one_hot
        marks[rows, :] = jnp.broadcast_to(jnp.sum(inside, axis=1, keepdims=True), (TB, 128))
        feats, _, _ = key_features(lengths[1], is_doc, TB, i * TB)
        kfc[rows, :] = feats

    loop(L // TB, features)
    loads["x"].wait()
    loads["wqkv"].wait()

    packed[:, :D] = dot(x[...], wqkv[:, :D]).astype(bf) * bf(SCALE)
    packed[:, D:] = dot(x[...], wqkv[:, D:]).astype(bf)

    causal = lax.broadcasted_iota(jnp.int32, (SELF_BQ, SELF_BQ), 0) >= lax.broadcasted_iota(
        jnp.int32, (SELF_BQ, SELF_BQ), 1
    )

    def lanes_at(first, j):
        return pl.ds(pl.multiple_of(first + j * 128, 128), 128)

    for b in range(L // SELF_BQ):
        low, high = b * SELF_BQ, (b + 1) * SELF_BQ

        def self_pair(j, low=low, high=high):
            def section(first, last, mask):
                keys = jnp.concatenate([packed[first:last, lanes_at(D, j)], kfs[first:last, :]], axis=1)
                values = packed[first:last, lanes_at(2 * D, j)]
                return keys, jnp.concatenate([values, jnp.ones((last - first, 128), bf)], axis=1), mask

            sections = [section(low, high, causal)]
            if low:
                sections.append(section(0, low, None))
            sh[low:high, span(j, 128)] = softmax_pair(
                j, packed[low:high, span(j, 128)], sections, qfs, slice(low, high)
            )

        loop(PAIRS, self_pair)

    loads["wso"].wait()
    loads["wcq"].wait()

    def first_norm(i):
        rows = slice(i * TB, (i + 1) * TB)
        branch = dot(sh[rows, :], wso[...])
        yield
        normed, scaler = norm(omega[0:1, :] * x[rows, :].astype(f32) + branch)
        n1[rows, :] = normed
        marks[rows, :] = jnp.where(half_lanes(), marks[rows, :], scaler)
        first = (normed * gain[0:1, :] + bias[0:1, :]).astype(bf)
        yield
        q8[rows, :] = dot(first, wcq[...]).astype(bf) * bf(SCALE)

    weave(first_norm(i) for i in range(L // TB))

    own.wait()
    for t in range(1, n):
        exchange(t).wait()
    loads["wckv"].wait()

    kv[...] = dot(mem[...], wckv[...]).astype(bf)

    def cross_pair(i):
        j = i // (L // CROSS_BQ)
        rows = span(lax.rem(i, L // CROSS_BQ), CROSS_BQ)
        keys = jnp.concatenate([kv[:, span(j, 128)], kfc[...]], axis=1)
        values = jnp.concatenate([kv[:, lanes_at(D, j)], jnp.ones((L, 128), bf)], axis=1)
        ch[rows, span(j, 128)] = softmax_pair(j, q8[rows, span(j, 128)], [(keys, values, None)], qfc, rows)

    loop(PAIRS * (L // CROSS_BQ), cross_pair)

    vec[...] = jnp.zeros_like(vec)
    for name in ("wco", "win", "wout", "cot"):
        loads[name].wait()

    def tokens(i, part):
        rows = pl.ds(pl.multiple_of(i * TB + part * (TB // 2), TB // 2), TB // 2)
        branch = dot(ch[rows, :], wco[...])
        yield
        n2, r2 = norm(omega[1:2, :] * (n1[rows, :] * gain[0:1, :] + bias[0:1, :]) + branch)
        pre2[rows, :] = n2
        marks[rows, :] = jnp.where(lane < 96, marks[rows, :], r2)
        second_low = (n2 * gain[1:2, :] + bias[1:2, :]).astype(bf)
        slow[rows, :] = second_low
        yield
        for c in range(FF // WIDE):
            cols = slice(c * WIDE, (c + 1) * WIDE)
            h = dot(second_low, win[:, cols])
            yield
            square = h * h
            cdf = 0.5 + 0.5 * jnp.tanh(h * (GELU_C + (GELU_C * GELU_A) * square))
            value = h * cdf
            act[rows, cols] = value.astype(bf)
            slope = cdf + value * (1.0 - cdf) * (2.0 * GELU_C + (6.0 * GELU_C * GELU_A) * square)
            hg[rows, cols] = slope.astype(bf)
            yield
        branch = dot(act[rows, :], wout[...])
        yield
        second = pre2[rows, :] * gain[1:2, :] + bias[1:2, :]
        n3, r3 = norm(omega[2:3, :] * second + branch)
        third = n3 * gain[2:3, :] + bias[2:3, :]
        kept = marks[rows, :][:, 0:1]
        up = cot[rows, :].astype(f32) * kept
        cot[rows, :] = (third * kept).astype(bf)
        pre3 = norm_back(up, n3, r3, gain[2:3, :])
        vec[2:3, :] += total(up * n3)
        vec[5:6, :] += total(up)
        vec[8:9, :] += total(pre3 * second)
        low3 = pre3.astype(bf)
        br3[rows, :] = low3
        pre1[rows, :] = omega[2:3, :] * pre3
        yield
        for c in range(FF // WIDE):
            cols = slice(c * WIDE, (c + 1) * WIDE)
            back = dot(low3, wout[cols, :], NT)
            yield
            hg[rows, cols] = (back * hg[rows, cols].astype(f32)).astype(bf)
            yield

    loop(L // TB, lambda i: weave(tokens(i, part) for part in range(2)))
    out_copy = pltpu.make_async_copy(cot, out, out_sem.at[0])
    out_copy.start()

    def out_weight(i):
        wout[span(i, L), :] = dot(act[:, span(i, L)], br3[...], TN).astype(bf)

    loop(FF // L, out_weight)
    run("sums", 0)

    def second_back(i):
        rows = span(i, TB)
        branch = dot(hg[rows, :], win[...], NT)
        grad = pre1[rows, :] + branch
        n2 = pre2[rows, :]
        back2 = norm_back(grad, n2, marks[rows, :][:, 96:97], gain[1:2, :])
        vec[1:2, :] += total(grad * n2)
        vec[4:5, :] += total(grad)
        vec[7:8, :] += total(back2 * (n1[rows, :] * gain[0:1, :] + bias[0:1, :]))
        pre2[rows, :] = back2
        br2[rows, :] = back2.astype(bf)

    loop(L // TB, second_back)
    run("mid", 0)

    def in_weight(i):
        win[:, span(i, L)] = dot(slow[...], hg[:, span(i, L)], TN).astype(bf)

    loop(FF // L, in_weight)
    run("sums", 1)

    def heads_back(i):
        rows = span(i, TB)
        dlow = dot(br2[rows, :], wco[...], NT).astype(bf)
        do[rows, :] = dlow
        dfc[rows, :] = delta_features(dlow.astype(f32) * ch[rows, :].astype(f32))

    loop(L // TB, heads_back)
    wco[...] = dot(ch[...], br2[...], TN).astype(bf)
    run("sums", 2)

    kvg, qg, fl = hg.at[:, : 2 * D], hg.at[:, 2 * D : 3 * D], hg.at[:, 3 * D :]
    pg, mgs = act.at[:, : 3 * D], act.at[:, 3 * D :]
    br1 = br3
    blocks = L // CROSS_BK

    def cross_back(i):
        run("cross", i)
        j = i // blocks
        b = lax.rem(i, blocks)
        rows = span(b, CROSS_BK)
        lanes = span(j, 128)
        dk, dv, dq = back_tile(
            j, kv[rows, lanes], kv[rows, lanes_at(D, j)], kfc[rows, :], q8[:, lanes], qfc[...], do[:, lanes], dfc[...], None
        )
        kvg[rows, lanes] = dk.astype(bf)
        kvg[rows, lanes_at(D, j)] = dv.astype(bf)

        @pl.when(b == 0)
        def _():
            pre1[:, lanes] = dq

        @pl.when(b > 0)
        def _():
            pre1[:, lanes] += dq

    loop(PAIRS * blocks, cross_back)

    run("sums", 3)
    fl[...] = (n1[...] * gain[0:1, :] + bias[0:1, :]).astype(bf)
    qg[...] = (pre1[...] * SCALE).astype(bf)

    run("sums", 4)
    two[:D, :] = dot(fl[...], qg[...], TN).astype(bf)
    two[D : 2 * D, :] = dot(mem[...], kvg[:, :D], TN).astype(bf)
    two[2 * D :, :] = dot(mem[...], kvg[:, D:], TN).astype(bf)
    run("sums", 5)
    mgs[...] = dot(kvg[...], wckv[...], NT).astype(bf)

    def memory_back(t):
        peer = lax.rem(me + t, n)
        return pltpu.make_async_remote_copy(
            src_ref=mgs.at[span(peer, piece), :],
            dst_ref=mgrad.at[me],
            send_sem=msend.at[t],
            recv_sem=mrecv.at[t],
            device_id=(dp, peer),
            device_id_type=MESH,
        )

    memory_own = pltpu.make_async_copy(mgs.at[span(me, piece), :], mgrad.at[me], msend.at[0])
    memory_own.start()
    for t in range(1, n):
        memory_back(t).start()

    def first_back(i):
        run("first", i)
        rows = slice(i * TB, (i + 1) * TB)
        branch = dot(qg[rows, :], wcq[...], NT)
        yield
        normed = n1[rows, :]
        grad = omega[1:2, :] * pre2[rows, :] + branch
        back1 = norm_back(grad, normed, marks[rows, :][:, 64:65], gain[0:1, :])
        vec[0:1, :] += total(grad * normed)
        vec[3:4, :] += total(grad)
        vec[6:7, :] += total(back1 * x[rows, :].astype(f32))
        pre1[rows, :] = back1
        low1 = back1.astype(bf)
        br1[rows, :] = low1
        yield
        dlow = dot(low1, wso[...], NT).astype(bf)
        do[rows, :] = dlow
        yield
        dfc[rows, :] = delta_features(dlow.astype(f32) * sh[rows, :].astype(f32))

    weave(first_back(i) for i in range(L // TB))

    run("gso", 0)
    gso[...] = dot(sh[...], br1[...], TN).astype(bf)
    run("sums", 6)

    def vec_near(a):
        return pltpu.make_async_remote_copy(
            src_ref=vec.at[pl.ds(16 * a, 16), :],
            dst_ref=vbuf.at[a],
            send_sem=vsend.at[a],
            recv_sem=vrecv.at[a],
            device_id=near[a],
            device_id_type=MESH,
        )

    def vec_far(t):
        return pltpu.make_async_remote_copy(
            src_ref=vec.at[pl.ds(48, 16), :],
            dst_ref=vz.at[me],
            send_sem=vsend.at[2 + t],
            recv_sem=vrecv.at[2 + t],
            device_id=(dp, lax.rem(me + t, n)),
            device_id_type=MESH,
        )

    def vec_next(a):
        vec_near(a).wait()
        vec[16 * (a + 1) : 16 * (a + 2), :] = vec[16 * a : 16 * (a + 1), :] + vbuf[a]
        if a < 2:
            vec_near(a + 1).start()
        else:
            for t in range(1, n):
                vec_far(t).start()

    def vec_last():
        for t in range(1, n):
            vec_far(t).wait()
        vz[me] = vec[48:64, :]
        vout[...] = (vz[0] + vz[1]) + (vz[2] + vz[3])

    vec_near(0).start()
    at("self", 3, lambda: vec_next(0))
    at("self", 7, lambda: vec_next(1))
    at("self", 12, lambda: vec_next(2))
    at("end", 4, vec_last)

    below = lax.broadcasted_iota(jnp.int32, (SELF_BK, SELF_BK), 1) >= lax.broadcasted_iota(
        jnp.int32, (SELF_BK, SELF_BK), 0
    )
    parts = L // SELF_BK

    def self_back(j):
        dqs = []
        for b in range(parts):
            run("self", j, parts, b)
            low, high = b * SELF_BK, (b + 1) * SELF_BK
            dk, dv, dq = back_tile(
                j,
                packed[low:high, lanes_at(D, j)],
                packed[low:high, lanes_at(2 * D, j)],
                kfs[low:high, :],
                packed[low:, span(j, 128)],
                qfs[low:, :],
                do[low:, span(j, 128)],
                dfc[low:, :],
                below,
            )
            pg[low:high, lanes_at(D, j)] = dk.astype(bf)
            pg[low:high, lanes_at(2 * D, j)] = dv.astype(bf)
            for i in range(b, parts):
                share = dq[(i - b) * SELF_BK : (i - b + 1) * SELF_BK, :]
                if b == 0:
                    dqs.append(share)
                else:
                    dqs[i] = dqs[i] + share
        for i, share in enumerate(dqs):
            pg[i * SELF_BK : (i + 1) * SELF_BK, span(j, 128)] = (share * SCALE).astype(bf)
        both = jnp.concatenate([pg[:, lanes_at(c * D, j)] for c in range(3)], axis=1)
        g3[j] = dot(x[...], both, TN).astype(bf)

    loop(PAIRS, self_back)

    def igrad_copy(i):
        return pltpu.make_async_copy(pre1.at[span(i, TB), :], igrad.at[span(i, TB), :], out_sem.at[1 + i])

    def input_back(i):
        run("input", i)
        rows = span(i, TB)
        pre1[rows, :] = omega[0:1, :] * pre1[rows, :] + dot(pg[rows, :], wqkv[...], NT)
        igrad_copy(i).start()

    loop(L // TB, input_back)
    for _, _, fn in sorted(ticks["end"], key=lambda item: item[:2]):
        fn()
    out_copy.wait()
    memory_own.wait()
    for t in range(1, n):
        memory_back(t).wait()
    for i in range(L // TB):
        igrad_copy(i).wait()


CASTS = (
    [(0, (slice(i * D, (i + 1) * D), slice(0, D)), 0, (slice(i * D, (i + 1) * D), slice(0, D))) for i in range(4)]
    + [(1, (slice(0, D), slice(i * D, (i + 1) * D)), 1, (slice(0, D), slice(i * D, (i + 1) * D))) for i in range(4)]
    + [
        (2, (slice(0, D), slice(0, D)), 2, (slice(0, D), slice(0, D))),
        (2, (slice(D, 2 * D), slice(0, D)), 3, (slice(0, D), slice(0, D))),
        (2, (slice(2 * D, 3 * D), slice(0, D)), 4, (slice(0, D), slice(0, D))),
        (2, (slice(3 * D, 4 * D), slice(0, D)), 4, (slice(0, D), slice(D, 2 * D))),
        (3, (slice(0, D), slice(0, D)), 5, (slice(0, D), slice(0, D))),
    ]
)


def cast_kernel(
    out_in, igrad_in, mgrad_in, f_out, f_in, f_two, f_so, f_qkv,
    out, igrad, mgrad, g_out, g_in, g_co, g_cq, g_ckv, g_so, g_qkv,
    narrow, wide, qkv_narrow, qkv_wide, out_held, igrad_held, sems, out_sems,
):
    passed = [(out_in, out_held, out), (igrad_in, igrad_held, igrad)]
    whole_in = [pltpu.make_async_copy(src, held, sems.at[i]) for i, (src, held, _) in enumerate(passed)]
    froms = (f_out, f_in, f_two, f_so)
    tos = (g_out, g_in, g_co, g_cq, g_ckv, g_so)
    pieces = []
    for source, window, target, place in CASTS:
        pieces.append((froms[source].at[window], tos[target].at[place]))
    for i in range(2):
        pieces.append((mgrad_in.at[pl.ds(i * D, D), :], mgrad.at[pl.ds(i * D, D), :]))
    ins = [pltpu.make_async_copy(src, narrow.at[i], sems.at[2 + i]) for i, (src, _) in enumerate(pieces)]
    outs = [pltpu.make_async_copy(wide.at[i], dst, out_sems.at[i]) for i, (_, dst) in enumerate(pieces)]
    qkv_in = pltpu.make_async_copy(f_qkv, qkv_narrow, sems.at[2 + len(pieces)])
    qkv_out = pltpu.make_async_copy(qkv_wide, g_qkv, out_sems.at[len(pieces)])
    for copy in whole_in + ins:
        copy.start()
    qkv_in.start()
    whole_out = [
        pltpu.make_async_copy(held, dst, out_sems.at[len(pieces) + 1 + i]) for i, (_, held, dst) in enumerate(passed)
    ]
    for copy_in, copy_out in zip(whole_in, whole_out):
        copy_in.wait()
        copy_out.start()
    for i, copy in enumerate(ins):
        copy.wait()

        def body(r, i=i):
            wide[i, span(r, 64), :] = narrow[i, span(r, 64), :].astype(f32)

        loop(D // 64, body)
        outs[i].start()
    qkv_in.wait()

    def body(r):
        for j in range(PAIRS):
            for c in range(3):
                qkv_wide[span(r, 64), c * D + j * 128 : c * D + (j + 1) * 128] = qkv_narrow[
                    j, span(r, 64), c * 128 : (c + 1) * 128
                ].astype(f32)

    loop(D // 64, body)
    qkv_out.start()
    for copy in whole_out + outs:
        copy.wait()
    qkv_out.wait()


VM = pl.BlockSpec(memory_space=pltpu.VMEM)
SM = pl.BlockSpec(memory_space=pltpu.SMEM)
ANY = pl.BlockSpec(memory_space=pl.ANY)


def per_device(
    inputs, memory, cotangent, tgt_len, src_len,
    self_qkv, self_out, cross_query, cross_kv, cross_out, ffn_in, ffn_out, ln_gain, ln_bias, omega_scale, dp,
):
    shape = jax.ShapeDtypeStruct
    scratch = [
        pltpu.VMEM((L, D), bf),
        pltpu.VMEM((L, D), bf),
        pltpu.VMEM((D, 3 * D), bf),
        pltpu.VMEM((D, D), bf),
        pltpu.VMEM((D, D), bf),
        pltpu.VMEM((D, 2 * D), bf),
        pltpu.VMEM((D, D), bf),
        pltpu.VMEM((D, FF), bf),
        pltpu.VMEM((FF, D), bf),
        pltpu.VMEM((L, 3 * D), bf),
        pltpu.VMEM((L, D), bf),
        pltpu.VMEM((L, D), f32),
        pltpu.VMEM((L, 128), f32),
        pltpu.VMEM((L, D), bf),
        pltpu.VMEM((L, D), bf),
        pltpu.VMEM((L, 2 * D), bf),
        pltpu.VMEM((L, D), bf),
        pltpu.VMEM((L, 128), bf),
        pltpu.VMEM((L, 128), bf),
        pltpu.VMEM((L, 128), bf),
        pltpu.VMEM((L, 128), bf),
        pltpu.VMEM((L, 128), bf),
        pltpu.VMEM((L, D), f32),
        pltpu.VMEM((L, D), bf),
        pltpu.VMEM((L, FF), bf),
        pltpu.VMEM((L, FF), bf),
        pltpu.VMEM((L, D), bf),
        pltpu.VMEM((2 * L, D), bf),
        pltpu.VMEM((L, D), f32),
        pltpu.VMEM((PAIRS, D, 384), bf),
        pltpu.VMEM((64, D), f32),
        pltpu.VMEM((3, 16, D), f32),
        pltpu.VMEM((4, 16, D), f32),
    ]
    for n, w in SEGMENTS:
        scratch += seg_scratch(n, w)
    count = len(SEGMENTS)
    sem = pltpu.SemaphoreType.DMA
    scratch += [
        sem((9,)), sem((5,)), sem((count, 22)), sem((count, 22)), sem((2 * count,)), sem((6,)), sem((6,)),
        sem((4,)), sem((4,)), sem((4,)), sem((4,)),
    ]
    results = pl.pallas_call(
        layer_kernel,
        out_shape=[
            shape((L, D), bf),
            shape((L, D), f32),
            shape((4, L // 4, D), bf),
            shape((FF, D), bf),
            shape((D, FF), bf),
            shape((4 * D, D), bf),
            shape((D, D), bf),
            shape((PAIRS, D, 384), bf),
            shape((16, D), f32),
        ],
        in_specs=[SM] * 2 + [ANY] * 10 + [VM] * 3,
        out_specs=[ANY] * 8 + [VM],
        scratch_shapes=scratch,
        compiler_params=pltpu.CompilerParams(collective_id=0, has_side_effects=True, vmem_limit_bytes=(64 << 20) - (128 << 10)),
        name="layer",
    )(
        tgt_len, src_len, inputs.reshape(L, D), memory, cotangent.reshape(L, D), self_qkv, self_out, cross_query, cross_kv,
        cross_out, ffn_in, ffn_out, ln_gain, ln_bias, omega_scale,
    )
    output, igrad, mgrad, grads, small = results[0], results[1], results[2], results[3:8], results[8]

    blocks = dp // 8
    if blocks > 1:
        groups = [[i + 8 * b for b in range(blocks)] for i in range(8)]
        *grads, small = lax.psum((*grads, small), "dp", axis_index_groups=groups)

    pieces = len(CASTS) + 2
    output, igrad, mgrad, g_out, g_in, g_co, g_cq, g_ckv, g_so, g_qkv = pl.pallas_call(
        cast_kernel,
        out_shape=[
            shape((L, D), bf),
            shape((L, D), f32),
            shape((L, D), f32),
            shape((FF, D), f32),
            shape((D, FF), f32),
            shape((D, D), f32),
            shape((D, D), f32),
            shape((D, 2 * D), f32),
            shape((D, D), f32),
            shape((D, 3 * D), f32),
        ],
        in_specs=[ANY] * 8,
        out_specs=[ANY] * 10,
        scratch_shapes=[
            pltpu.VMEM((pieces, D, D), bf),
            pltpu.VMEM((pieces, D, D), f32),
            pltpu.VMEM((PAIRS, D, 384), bf),
            pltpu.VMEM((D, 3 * D), f32),
            pltpu.VMEM((L, D), bf),
            pltpu.VMEM((L, D), f32),
            sem((pieces + 3,)),
            sem((pieces + 3,)),
        ],
        compiler_params=pltpu.CompilerParams(vmem_limit_bytes=62 << 20),
        name="casts",
    )(output, igrad, mgrad.reshape(L, D), *grads)
    return (
        output.reshape(1, L, D),
        igrad.reshape(1, L, D),
        mgrad.reshape(4, L // 4, D),
        g_qkv,
        g_so,
        g_cq,
        g_ckv,
        g_co,
        g_in,
        g_out,
        small[0:3],
        small[3:6],
        small[6:9],
    )


def solution(mesh):
    rows = P(("dp", "mem"), None, None)
    return jax.shard_map(
        functools.partial(per_device, dp=mesh.shape["dp"]),
        mesh=mesh,
        in_specs=(rows, P("dp", "mem", None), rows, P(("dp", "mem"), None), P("dp", None)) + (P(),) * 10,
        out_specs=(rows, rows, P("dp", "mem", None)) + (P(),) * 10,
        check_vma=False,
    )
```
